32 devices in a mesh: dp: 8 (over z, x), ctx: 4 (over y, core).
Axes of the slice: x: 2, y: 2, z: 4, core: 2. Of those that a mesh axis runs over, the one named last changes fastest.
Arguments:
- tokens: bfloat16 [8, 2048, 768], P('dp', 'ctx'), may hold values from -6 to 6
- lengths: int32 [8], P('dp'), may hold values from 513 to 2048, as said below
- thought_pos: int32 [8, 6], P('dp'), may hold values from 1 to 2047, as said below
- cotangent: bfloat16 [8, 2048, 768], P('dp', 'ctx'), may hold values from -6 to 6
- qkv_weight: bfloat16 [768, 2304], P(('dp', 'ctx')), may hold values from -0.21875 to 0.21875
- out_weight: bfloat16 [768, 768], P(('dp', 'ctx')), may hold values from -2.5 to 2.5
- fc_weight: bfloat16 [768, 3072], P(('dp', 'ctx')), may hold values from -0.21875 to 0.21875
- proj_weight: bfloat16 [3072, 768], P(('dp', 'ctx')), may hold values from -0.109375 to 0.109375
- qv_bias: bfloat16 [1536], P(('dp', 'ctx')), may hold values from -1.5 to 1.5
- out_bias: bfloat16 [768], P(('dp', 'ctx')), may hold values from -1.5 to 1.5
- fc_bias: bfloat16 [3072], P(('dp', 'ctx')), may hold values from -1.5 to 1.5
- proj_bias: bfloat16 [768], P(('dp', 'ctx')), may hold values from -1.5 to 1.5
- first_gain: bfloat16 [768], P(('dp', 'ctx')), may hold values from 0.5 to 1.5
- first_shift: bfloat16 [768], P(('dp', 'ctx')), may hold values from -1 to 1
- second_gain: bfloat16 [768], P(('dp', 'ctx')), may hold values from 0.5 to 1.5
- second_shift: bfloat16 [768], P(('dp', 'ctx')), may hold values from -1 to 1
Outputs:
- mixed: bfloat16 [8, 2048, 768], P('dp', 'ctx')
- tokens_grad: float32 [8, 2048, 768], P('dp', 'ctx')
- qkv_weight_grad: float32 [768, 2304], P(('dp', 'ctx'))
- out_weight_grad: float32 [768, 768], P(('dp', 'ctx'))
- fc_weight_grad: float32 [768, 3072], P(('dp', 'ctx'))
- proj_weight_grad: float32 [3072, 768], P(('dp', 'ctx'))
- qv_bias_grad: float32 [1536], P(('dp', 'ctx'))
- out_bias_grad: float32 [768], P(('dp', 'ctx'))
- fc_bias_grad: float32 [3072], P(('dp', 'ctx'))
- proj_bias_grad: float32 [768], P(('dp', 'ctx'))
- first_gain_grad: float32 [768], P(('dp', 'ctx'))
- first_shift_grad: float32 [768], P(('dp', 'ctx'))
- second_gain_grad: float32 [768], P(('dp', 'ctx'))
- second_shift_grad: float32 [768], P(('dp', 'ctx'))
The draws below stay inside these ranges and needn't reach their ends.
Inputs may be any that keep to these rules, and one draw needn't show every extreme that they name: `lengths`: every draw holds a sequence of length 2048 and one of length 513. `thought_pos`: each entry lies from 1 to its sequence's length minus one; entries may repeat; the first entry of each sequence is a positive multiple of 512; every draw holds an entry 1 and an entry 2047.
All inputs are finite; a program needn't handle non-finite values.
Results may differ from the reference program's by a relative error of at most 0.011.
Values may be sent and summed in bfloat16 or wider, within the bound.
No kernel may reach another device: no remote copies, remote signals or barrier semaphores. Data moves between devices by JAX's collectives and lax.ppermute only.
A program may use at most 256 MiB of HBM per device.

```python
import jax
import jax.numpy as jnp
from jax import lax

D = 768
HEADS = 12
HEAD_DIM = 64
FF = 3072
QUARTER = 512
THOUGHTS = 6
LEN = 2048
SEQS = 8


def make_lengths(key):
    seeded = jax.random.fold_in(key, 11)
    values = jax.random.randint(jax.random.fold_in(seeded, 1), (SEQS,), QUARTER + 1, LEN + 1)
    shuffled = jax.random.permutation(jax.random.fold_in(seeded, 2), SEQS)
    values = values.at[shuffled[0]].set(LEN)
    values = values.at[shuffled[1]].set(QUARTER + 1)
    return (values.astype(jnp.int32), shuffled)


def draw_lengths(key, part):
    values, shuffled = make_lengths(key)
    return values


def draw_thought_pos(key, part):
    limits, shuffled = make_lengths(key)
    seeded = jax.random.fold_in(key, 23)
    random_bits = jax.random.randint(jax.random.fold_in(seeded, 1), (SEQS, THOUGHTS), 0, 1 << 20)
    placed = 1 + random_bits % (limits[:, None] - 1)
    quarter_count = (limits - 1) // QUARTER
    chosen = jax.random.randint(jax.random.fold_in(seeded, 2), (SEQS,), 0, 1 << 20)
    boundary = (1 + chosen % quarter_count) * QUARTER
    placed = placed.at[:, 0].set(boundary)
    placed = placed.at[shuffled[0], 1].set(LEN - 1)
    placed = placed.at[shuffled[1], 1].set(1)
    return placed.astype(jnp.int32)


def steps_of(key, shape, pieces, least, high):
    factor_of = 1.0
    for position, parts in pieces:
        steps = jax.random.uniform(jax.random.fold_in(jax.random.fold_in(key, 6), position), (parts,), jnp.float32, least / len(pieces), high / len(pieces))
        factor_of = factor_of * jnp.repeat(jnp.exp(steps), shape[position] // parts).reshape((-1,) + (1,) * (len(shape) - 1 - position))
    return factor_of


def bell_draw(rng, dims, scale, most, pieces=(), kind=jnp.bfloat16):
    level = steps_of(rng, dims, pieces, -0.22, 0.18) if pieces else 1.0
    values = jax.random.normal(rng, dims, jnp.float32) * scale * level
    return jnp.minimum(jnp.maximum(values, -most), most).astype(kind)


def setup_inputs(seed: int = 0) -> dict:
    key_list = jax.random.split(jax.random.key(seed), 17)
    tokens = bell_draw(key_list[0], (SEQS, LEN, D), 1.0, 6.0, ((0, 8), (1, 4)))
    lengths = draw_lengths(jax.random.fold_in(key_list[16], 71), 0)
    thought_pos = draw_thought_pos(jax.random.fold_in(key_list[16], 71), 0)
    cotangent = bell_draw(key_list[3], (SEQS, LEN, D), 1.0, 6.0, ((0, 8), (1, 4)))
    qkv_weight = bell_draw(key_list[4], (D, 3 * D), D ** -0.5, 0.21875, ((0, 32),))
    out_weight = bell_draw(key_list[5], (D, D), (D * 16 // LEN) ** -0.5, 2.5, ((0, 32),))
    fc_weight = bell_draw(key_list[6], (D, FF), D ** -0.5, 0.21875, ((0, 32),))
    proj_weight = bell_draw(key_list[7], (FF, D), FF ** -0.5, 0.109375, ((0, 32),))
    qv_bias = bell_draw(key_list[8], (2 * D,), 0.3, 1.5, ((0, 32),))
    out_bias = bell_draw(key_list[9], (D,), 0.3, 1.5, ((0, 32),))
    fc_bias = bell_draw(key_list[10], (FF,), 0.3, 1.5, ((0, 32),))
    proj_bias = bell_draw(key_list[11], (D,), 0.3, 1.5, ((0, 32),))
    first_gain = jnp.clip(1.0 + 0.1 * jax.random.normal(key_list[12], (D,), jnp.float32), 0.5, 1.5).astype(jnp.bfloat16)
    first_shift = bell_draw(key_list[13], (D,), 0.2, 1.0, ((0, 32),))
    second_gain = jnp.clip(1.0 + 0.1 * jax.random.normal(key_list[14], (D,), jnp.float32), 0.5, 1.5).astype(jnp.bfloat16)
    second_shift = bell_draw(key_list[15], (D,), 0.2, 1.0, ((0, 32),))
    return dict(tokens=tokens, lengths=lengths, thought_pos=thought_pos, cotangent=cotangent, qkv_weight=qkv_weight, out_weight=out_weight, fc_weight=fc_weight, proj_weight=proj_weight, qv_bias=qv_bias, out_bias=out_bias, fc_bias=fc_bias, proj_bias=proj_bias, first_gain=first_gain, first_shift=first_shift, second_gain=second_gain, second_shift=second_shift)


@jax.custom_vjp
def low(v):
    return lax.optimization_barrier(v.astype(jnp.bfloat16)).astype(jnp.float32)

@jax.custom_vjp
def low_back(v):
    return v

def low_keep(v):
    return (low(v), None)

def low_pass(kept, grad):
    return (grad,)

def back_keep(v):
    return (v, None)

def back_low(kept, grad):
    return (low(grad),)
low.defvjp(low_keep, low_pass)
low_back.defvjp(back_keep, back_low)

def matmul(left, right):
    return jnp.dot(left, right, precision=lax.Precision.HIGHEST)

def layer_norm(values, gain, shift):
    center = values - lax.optimization_barrier(jnp.mean(values, -1, keepdims=True))
    spread = lax.optimization_barrier(jnp.mean(center * center, -1, keepdims=True))
    return center * lax.rsqrt(spread + 1e-05) * gain + shift

def sequence_block(seq_tokens, params, seq_length, seq_thoughts):
    qkv_weight, out_weight, fc_weight, proj_weight, qv_bias, out_bias, fc_bias, proj_bias, first_gain, first_shift, second_gain, second_shift = params
    slots = jnp.arange(LEN, dtype=jnp.int32)
    thought = jnp.any(seq_thoughts[:, None] == slots[None, :], axis=0)
    valid = slots < seq_length
    earlier = jnp.concatenate([jnp.zeros_like(seq_tokens[:1]), seq_tokens[:-1]], axis=0)
    inputs = jnp.where(thought[:, None], earlier, seq_tokens)
    normed = low(layer_norm(inputs, first_gain, first_shift))
    bias_full = jnp.concatenate([qv_bias[:D], jnp.zeros((D,), jnp.float32), qv_bias[D:]])
    projected = low(low_back(matmul(normed, qkv_weight) + bias_full))
    queries = projected[:, :D].reshape(LEN, HEADS, HEAD_DIM)
    keys = projected[:, D:2 * D].reshape(LEN, HEADS, HEAD_DIM)
    values = projected[:, 2 * D:].reshape(LEN, HEADS, HEAD_DIM)
    scores = jnp.einsum('qhd,khd->hqk', queries, keys, precision=lax.Precision.HIGHEST) * HEAD_DIM ** (-0.5)
    scores = low_back(scores)
    allowed = (slots[None, :] <= slots[:, None]) & valid[None, :]
    scores = jnp.where(allowed[None], scores, -1000000000.0)
    probs = low(jax.nn.softmax(scores, axis=-1))
    attended = jnp.einsum('hqk,khd->qhd', probs, values, precision=lax.Precision.HIGHEST).reshape(LEN, D)
    attended = low(low_back(attended))
    branch = low_back(matmul(attended, out_weight) + out_bias)
    middle = inputs + branch
    normed_two = low(layer_norm(middle, second_gain, second_shift))
    hidden = low_back(matmul(normed_two, fc_weight) + fc_bias)
    active = low(jax.nn.gelu(hidden, approximate=True))
    mlp_out = low_back(matmul(active, proj_weight) + proj_bias)
    return jnp.where(valid[:, None], middle + mlp_out, 0.0)

def reference(tokens, lengths, thought_pos, cotangent, qkv_weight, out_weight, fc_weight, proj_weight, qv_bias, out_bias, fc_bias, proj_bias, first_gain, first_shift, second_gain, second_shift):
    params = tuple((weight.astype(jnp.float32) for weight in (qkv_weight, out_weight, fc_weight, proj_weight, qv_bias, out_bias, fc_bias, proj_bias, first_gain, first_shift, second_gain, second_shift)))

    def one_sequence(totals, packed):
        seq_tokens, seq_length, seq_thoughts, seq_cot = packed

        def forward(values, *weights):
            return sequence_block(values, weights, seq_length, seq_thoughts)
        result, backward = jax.vjp(forward, seq_tokens.astype(jnp.float32), *params)
        grads = backward(seq_cot.astype(jnp.float32))
        totals = tuple((total + grad for total, grad in zip(totals, grads[1:])))
        return (totals, (result.astype(jnp.bfloat16), grads[0]))
    zeros = tuple((jnp.zeros_like(weight) for weight in params))
    totals, outputs = lax.scan(one_sequence, zeros, (tokens, lengths, thought_pos, cotangent))
    mixed, tokens_grad = outputs
    return (mixed, tokens_grad, totals[0], totals[1], totals[2], totals[3], totals[4], totals[5], totals[6], totals[7], totals[8], totals[9], totals[10], totals[11])
```

```python
import jax
import jax.numpy as jnp
from jax import lax
from jax.experimental import pallas as pl
from jax.experimental.pallas import tpu as pltpu
from jax.sharding import PartitionSpec as P

ALL = ("dp", "ctx")
LOW = jnp.bfloat16
FULL = jnp.float32
HEAD = 64
LANES = 128
SCALE = 0.125
VMEM = 48 << 20


def flat_bits():
    return (lax.axis_size("dp") * lax.axis_size("ctx")).bit_length() - 1


def flat_index():
    return lax.axis_index("dp") * lax.axis_size("ctx") + lax.axis_index("ctx")


def bit_of(bit):
    return (flat_index() >> bit) & 1


def swap(value, bit):
    count = 1 << flat_bits()
    return lax.ppermute(value, ALL, [(i, i ^ (1 << bit)) for i in range(count)])


def pair(mine, other, place, axis):
    shape = mine.shape[:axis] + (2,) + mine.shape[axis:]
    mine, other = jnp.expand_dims(mine, axis), jnp.expand_dims(other, axis)
    whole = jnp.zeros(shape, mine.dtype)
    whole = lax.dynamic_update_slice_in_dim(whole, mine, place, axis)
    return lax.dynamic_update_slice_in_dim(whole, other, 1 - place, axis)


def orders():
    top = flat_bits()
    rest = list(range(4, top))
    return ([1, 2, 3] + rest, [2, 3, 1] + rest, [3, 1, 2] + rest)


def grow(block, done, bit):
    other = swap(block, bit)
    rows, cols = block.shape[1:]
    high = 1 << len([b for b in done if b > bit])
    low = 1 << len([b for b in done if b < bit])
    whole = pair(
        block.reshape(high, low, rows, cols), other.reshape(high, low, rows, cols), bit_of(bit), 1
    )
    return whole.reshape(high * 2 * low, rows, cols)


def gather_links(block, cuts):
    plans = [list(reversed(order)) for order in orders()]
    block = block[None]
    done = []
    common = flat_bits() - 4
    for bit in plans[0][:common]:
        block = grow(block, done, bit)
        done = done + [bit]
    parts, at = [], 0
    for cut in cuts:
        parts.append(block[:, :, at : at + cut])
        at += cut
    known = [list(done) for _ in cuts]
    for step in range(common, flat_bits() - 1):
        for which in range(len(cuts)):
            bit = plans[which][step]
            parts[which] = grow(parts[which], known[which], bit)
            known[which].append(bit)
    return parts


class Sum:
    def __init__(self, addends, left):
        self.addends = addends
        self.left = left

    def half(self, bit, place):
        low = 1 << len([b for b in self.left if b < bit])
        high = 1 << len([b for b in self.left if b > bit])
        out = []
        for value in self.addends:
            rows, cols = value.shape[1:]
            view = value.reshape(high, 2, low, rows, cols)
            out.append(
                lax.dynamic_index_in_dim(view, place, 1, keepdims=False).reshape(
                    high * low, rows, cols
                )
            )
        return out

    def total(self):
        result = self.addends[0].astype(FULL)
        for value in self.addends[1:]:
            result = result + value.astype(FULL)
        return result

    def step(self, bit):
        place = bit_of(bit)
        left = [b for b in self.left if b != bit]
        send = Sum(self.half(bit, 1 - place), left).total().astype(LOW)
        return Sum(self.half(bit, place) + [swap(send, bit)], left)


def scatter_links(parts, plans):
    links = list(range(1, flat_bits()))
    sums = [Sum(addends, links) for addends in parts]
    for step in range(len(links)):
        sums = [value.step(plan[step]) for value, plan in zip(sums, plans)]
    return [value.total()[0] for value in sums]


def finish(total, rows, cols):
    core = bit_of(0)
    mine = lax.dynamic_slice_in_dim(total, core * rows, rows, 0)
    other = swap(lax.dynamic_slice_in_dim(total, (1 - core) * rows, rows, 0), 0)
    first = jnp.where(core == 0, mine, other)
    second = jnp.where(core == 0, other, mine)
    return first, second


def weight_grad(left, right, plan):
    core = bit_of(0)
    height, cols = left.shape[1], right.shape[1]
    half = cols // 2
    rows = height >> flat_bits()
    kept = dot_tn(left, lax.dynamic_slice_in_dim(right, core * half, half, 1))
    send = dot_tn(left, lax.dynamic_slice_in_dim(right, (1 - core) * half, half, 1)).astype(LOW)
    shape = (height // (2 * rows), 2 * rows, half)
    (total,) = scatter_links([[kept.reshape(shape), swap(send, 0).reshape(shape)]], [plan])
    return jnp.concatenate(finish(total, rows, cols), 1)


def dot(a, b):
    return lax.dot_general(a, b, (((1,), (0,)), ((), ())), preferred_element_type=FULL)


def dot_nt(a, b):
    return lax.dot_general(a, b, (((1,), (1,)), ((), ())), preferred_element_type=FULL)


def dot_tn(a, b):
    return lax.dot_general(a, b, (((0,), (0,)), ((), ())), preferred_element_type=FULL)


def head_lanes(value, head):
    lane = lax.broadcasted_iota(jnp.int32, (1, LANES), 1)
    return jnp.where(lane // HEAD == head, value, jnp.zeros_like(value))


def causal(size):
    shape = (size, size)
    return lax.broadcasted_iota(jnp.int32, shape, 0) <= lax.broadcasted_iota(jnp.int32, shape, 1)


def attend_kernel(far_ref, q_ref, k_ref, v_ref, out_ref, lse_ref, top_ref, acc_ref):
    size = q_ref.shape[0]
    mine = pl.program_id(1)
    query = q_ref[...] * jnp.asarray(SCALE, LOW)

    def step(block, first):
        at = pl.ds(pl.multiple_of(block * size, size), size)
        key = k_ref[at, :]
        value = jnp.transpose(v_ref[at, :])
        for head in range(2):
            ones = jnp.ones((16, size), LOW)
            wide = jnp.concatenate([value[head * HEAD : (head + 1) * HEAD], ones], 0)
            scores = dot_nt(key, head_lanes(query, head))
            row = slice(head, head + 1)
            if first:
                scores = jnp.where(causal(size), scores, -1e9)
                top = jnp.max(scores, 0, keepdims=True)
                acc_ref[head] = dot(wide, jnp.exp(scores - top).astype(LOW))
            else:
                old = top_ref[row, :]
                top = jnp.maximum(old, jnp.max(scores, 0, keepdims=True))
                acc_ref[head] = acc_ref[head] * jnp.exp(old - top) + dot(
                    wide, jnp.exp(scores - top).astype(LOW)
                )
            top_ref[row, :] = top

    step(mine, True)

    @pl.loop(0, mine + far_ref[0])
    def _(i):
        step(jnp.where(i < mine, 0, 2 + i - mine), False)

    outs = []
    for head in range(2):
        total = acc_ref[head, HEAD : HEAD + 1, :]
        outs.append(acc_ref[head, :HEAD, :] / total)
        lse_ref[0, head : head + 1, :] = top_ref[head : head + 1, :] + jnp.log(total)
    out_ref[...] = jnp.transpose(jnp.concatenate(outs, 0)).astype(LOW)


def attend(far, query, key, value, quarter):
    near, width = query.shape
    pairs = width // LANES
    total = key.shape[0]
    rows = pl.BlockSpec((quarter, LANES), lambda p, i, s: (i, p))
    every = pl.BlockSpec((total, LANES), lambda p, i, s: (0, p))
    return pl.pallas_call(
        attend_kernel,
        out_shape=(
            jax.ShapeDtypeStruct((near, width), LOW),
            jax.ShapeDtypeStruct((pairs, 8, near), FULL),
        ),
        grid_spec=pltpu.PrefetchScalarGridSpec(
            num_scalar_prefetch=1,
            grid=(pairs, near // quarter),
            in_specs=[rows, every, every],
            out_specs=(rows, pl.BlockSpec((1, 8, quarter), lambda p, i, s: (p, 0, i))),
            scratch_shapes=[
                pltpu.VMEM((8, quarter), FULL),
                pltpu.VMEM((2, HEAD + 16, quarter), FULL),
            ],
        ),
        compiler_params=pltpu.CompilerParams(vmem_limit_bytes=VMEM),
        cost_estimate=pl.CostEstimate(
            flops=6 * 4 * quarter * quarter * LANES * 2 * pairs,
            bytes_accessed=8 << 20,
            transcendentals=6 * quarter * quarter * 2 * pairs,
        ),
        name="attend",
    )(far, query, key, value)


def attend_back_kernel(
    far_ref, q_ref, k_ref, v_ref, grad_ref, out_ref, lse_ref, dq_ref, dk_ref, dv_ref, acc_ref
):
    near = q_ref.shape[0]
    size = near // 2
    spans = (slice(0, size), slice(size, near))
    query = q_ref[...] * jnp.asarray(SCALE, LOW)
    grad = grad_ref[...]
    product = jnp.transpose(grad.astype(FULL) * out_ref[...].astype(FULL))
    delta = [
        jnp.sum(product[head * HEAD : (head + 1) * HEAD], 0, keepdims=True) for head in range(2)
    ]

    def block(at, work):
        key, value = k_ref[at, :], v_ref[at, :]
        turned = jnp.transpose(key)
        dk = dv = None
        for which, masked, first in work:
            span = spans[which]
            for head in range(2):
                part = slice(head * HEAD, (head + 1) * HEAD)
                q_head = head_lanes(query[span], head)
                g_head = head_lanes(grad[span], head)
                probs = jnp.exp(dot_nt(key, q_head) - lse_ref[0, head : head + 1, span])
                if masked:
                    probs = jnp.where(causal(size), probs, 0.0)
                moved = probs * (dot_nt(value, g_head) - delta[head][:, span])
                moved, probs = moved.astype(LOW), probs.astype(LOW)
                new_k, new_v = dot(moved, q_head), dot(probs, g_head)
                dk = new_k if dk is None else dk + new_k
                dv = new_v if dv is None else dv + new_v
                new_q = dot(turned[part], moved)
                if first:
                    acc_ref[which, part, :] = new_q
                else:
                    acc_ref[which, part, :] += new_q
        dk_ref[at, :] = dk.astype(LOW)
        dv_ref[at, :] = dv.astype(LOW)

    block(spans[0], [(0, True, True), (1, False, True)])
    block(spans[1], [(1, True, False)])

    @pl.loop(0, far_ref[0])
    def _(i):
        at = pl.ds(pl.multiple_of(near + i * size, size), size)
        block(at, [(0, False, False), (1, False, False)])

    @pl.loop(far_ref[0], 2)
    def _(i):
        at = pl.ds(pl.multiple_of(near + i * size, size), size)
        dk_ref[at, :] = jnp.zeros((size, LANES), LOW)
        dv_ref[at, :] = jnp.zeros((size, LANES), LOW)

    for which in range(2):
        dq_ref[spans[which], :] = (jnp.transpose(acc_ref[which]) * SCALE).astype(LOW)


def attend_back(far, query, key, value, grad, out, lse):
    near, width = query.shape
    pairs = width // LANES
    total = key.shape[0]
    rows = pl.BlockSpec((near, LANES), lambda p, s: (0, p))
    every = pl.BlockSpec((total, LANES), lambda p, s: (0, p))
    return pl.pallas_call(
        attend_back_kernel,
        out_shape=(
            jax.ShapeDtypeStruct((near, width), LOW),
            jax.ShapeDtypeStruct((total, width), LOW),
            jax.ShapeDtypeStruct((total, width), LOW),
        ),
        grid_spec=pltpu.PrefetchScalarGridSpec(
            num_scalar_prefetch=1,
            grid=(pairs,),
            in_specs=[rows, every, every, rows, rows, pl.BlockSpec((1, 8, near), lambda p, s: (p, 0, 0))],
            out_specs=(rows, every, every),
            scratch_shapes=[pltpu.VMEM((2, LANES, near // 2), FULL)],
        ),
        compiler_params=pltpu.CompilerParams(vmem_limit_bytes=VMEM),
        cost_estimate=pl.CostEstimate(
            flops=6 * 10 * near * near // 4 * LANES * 2 * pairs,
            bytes_accessed=16 << 20,
            transcendentals=6 * near * near // 4 * 2 * pairs,
        ),
        name="attend_back",
    )(far, query, key, value, grad, out, lse)


def normalize(values):
    center = values - jnp.mean(values, -1, keepdims=True)
    spread = jnp.mean(center * center, -1, keepdims=True)
    root = lax.rsqrt(spread + 1e-05)
    return center * root, root


def normalize_back(grad, gain, hat, root):
    scaled = grad * gain
    return root * (
        scaled
        - jnp.mean(scaled, -1, keepdims=True)
        - hat * jnp.mean(scaled * hat, -1, keepdims=True)
    )


def gelu_tanh(values):
    return jax.nn.gelu(values, approximate=True)


def shards(
    tokens,
    lengths,
    thought_pos,
    cotangent,
    qkv_weight,
    out_weight,
    fc_weight,
    proj_weight,
    qv_bias,
    out_bias,
    fc_bias,
    proj_bias,
    first_gain,
    first_shift,
    second_gain,
    second_shift,
):
    _, quarter, width = tokens.shape
    half = width // 2
    near = 2 * quarter
    slice_rows = qkv_weight.shape[0]
    count = 1 << flat_bits()
    plans = orders()
    core, second = bit_of(0), bit_of(1)
    far = (2 * second).astype(jnp.int32).reshape(1)

    late = lax.all_gather(
        jnp.concatenate([fc_weight, out_weight], 1), ALL, axis=0, tiled=True
    )
    hidden_width = fc_weight.shape[1]
    fc_full, out_full = late[:, :hidden_width], late[:, hidden_width:]

    mine = tokens[0]
    flips = [(i, i ^ 2) for i in range(count) if not i & 2]
    before = lax.ppermute(mine, ALL, flips)
    partner = swap(mine, 0)
    near_tokens = pair(mine, partner, core, 0).reshape(near, width)
    before_partner = swap(before, 0)
    far_tokens = pair(before, before_partner, core, 0).reshape(near, width)

    third = slice_rows * 4
    small = jnp.zeros((slice_rows, LANES), LOW)
    rows_of = (
        jnp.concatenate([qv_bias, out_bias, first_gain]),
        fc_bias,
        jnp.concatenate([proj_bias, first_shift, second_gain, second_shift]),
    )
    small = small.at[:3, :third].set(jnp.stack(rows_of))
    split = qkv_weight.reshape(slice_rows, 3, 2, half)
    keep = lax.dynamic_index_in_dim(split, core, 2, keepdims=False).reshape(slice_rows, 3 * half)
    send = lax.dynamic_index_in_dim(split, 1 - core, 2, keepdims=False).reshape(
        slice_rows, 3 * half
    )
    keep, send = jnp.concatenate([keep, small], 1), jnp.concatenate([send, small], 1)
    chip = pair(keep, swap(send, 0), core, 0).reshape(2 * slice_rows, 3 * half + LANES)
    q_weight, k_weight, v_small = gather_links(chip, (half, half, half + LANES))
    q_weight = q_weight.reshape(width, half)
    k_weight = k_weight.reshape(width, half)
    v_weight = v_small[:, :, :half].reshape(width, half)
    small = v_small.reshape(count, slice_rows, half + LANES)[:, :3, half : half + third]
    small = small.astype(FULL)
    at = slice_rows

    def vector(row, first, size):
        return small[:, row, first : first + size].reshape(1, count * size)

    qv_full = vector(0, 0, 2 * at)
    out_bias_full, gain_one = vector(0, 2 * at, at), vector(0, 3 * at, at)
    fc_bias_full = vector(1, 0, 4 * at)
    proj_bias_full, shift_one = vector(2, 0, at), vector(2, at, at)
    gain_two, shift_two = vector(2, 2 * at, at), vector(2, 3 * at, at)

    high = proj_weight.shape[0]
    split = proj_weight.reshape(high, 2, half)
    keep = lax.dynamic_index_in_dim(split, core, 1, keepdims=False)
    send = lax.dynamic_index_in_dim(split, 1 - core, 1, keepdims=False)
    chip = pair(keep, swap(send, 0), core, 0).reshape(2 * high, half)
    proj_parts = gather_links(chip, (half // 3,) * 3)
    proj_half = jnp.concatenate(proj_parts, 2).reshape(count * high, half)
    proj_full = pair(proj_half, swap(proj_half, 0), core, 1).reshape(count * high, width)

    slots = jnp.arange(near, dtype=jnp.int32)
    thoughts = thought_pos[0]

    def is_thought(at_slots):
        return jnp.any(thoughts[None, :] == at_slots[:, None], 1, keepdims=True)

    thought_near = is_thought(second * near + slots)
    thought_far = is_thought(slots)
    shifted_near = jnp.concatenate([far_tokens[-1:], near_tokens[:-1]], 0)
    shifted_far = jnp.concatenate([far_tokens[:1], far_tokens[:-1]], 0)
    inputs_near = jnp.where(thought_near, shifted_near, near_tokens)
    inputs_far = jnp.where(thought_far, shifted_far, far_tokens)
    inputs_all = jnp.concatenate([inputs_near, inputs_far], 0)
    hat_all, root_all = normalize(inputs_all.astype(FULL))
    normed = (hat_all * gain_one + shift_one).astype(LOW)
    own = core * quarter
    inputs = lax.dynamic_slice_in_dim(inputs_near, own, quarter, 0).astype(FULL)

    own_half = core * half
    q_bias = lax.dynamic_slice_in_dim(qv_full[:, :width], own_half, half, 1)
    v_bias = lax.dynamic_slice_in_dim(qv_full[:, width:], own_half, half, 1)
    query = (dot(normed[:near], q_weight) + q_bias).astype(LOW)
    key = dot(normed, k_weight).astype(LOW)
    value = (dot(normed, v_weight) + v_bias).astype(LOW)

    attended_heads, logsum = attend(far, query, key, value, quarter)

    def rows_to_core(array):
        return (
            lax.dynamic_slice_in_dim(array, own, quarter, 0),
            lax.dynamic_slice_in_dim(array, quarter - own, quarter, 0),
        )

    keep, send = rows_to_core(attended_heads)
    attended = pair(keep, swap(send, 0), core, 1).reshape(quarter, width)

    middle = inputs + dot(attended, out_full) + out_bias_full
    hat_two, root_two = normalize(middle)
    normed_two = (hat_two * gain_two + shift_two).astype(LOW)
    hidden = dot(normed_two, fc_full) + fc_bias_full
    active = gelu_tanh(hidden).astype(LOW)
    my_slots = (2 * second + core) * quarter + jnp.arange(quarter, dtype=jnp.int32)
    valid = (my_slots < lengths[0])[:, None]
    grad_valid = jnp.where(valid, cotangent[0], jnp.zeros_like(cotangent[0]))
    proj_weight_grad = weight_grad(active, grad_valid, plans[1])
    output = middle + dot(active, proj_full) + proj_bias_full
    mixed = jnp.where(valid, output, 0.0).astype(LOW)[None]

    proj_bias_grad = jnp.sum(grad_valid.astype(FULL), 0)
    grad_active = dot_nt(grad_valid, proj_full)
    _, gelu_back = jax.vjp(gelu_tanh, hidden)
    grad_hidden = gelu_back(grad_active)[0].astype(LOW)
    fc_weight_grad = weight_grad(normed_two, grad_hidden, plans[0])
    fc_bias_grad = jnp.sum(grad_hidden.astype(FULL), 0)
    grad_normed_two = dot_nt(grad_hidden, fc_full)
    second_gain_grad = jnp.sum(grad_normed_two * hat_two, 0)
    second_shift_grad = jnp.sum(grad_normed_two, 0)
    grad_middle = grad_valid.astype(FULL) + normalize_back(
        grad_normed_two, gain_two, hat_two, root_two
    )
    grad_attn = grad_middle.astype(LOW)
    out_weight_grad = weight_grad(attended, grad_attn, plans[2])
    out_bias_grad = jnp.sum(grad_attn.astype(FULL), 0)
    grad_attended = dot_nt(grad_attn, out_full).astype(LOW)

    keep = lax.dynamic_slice_in_dim(grad_attended, own_half, half, 1)
    send = lax.dynamic_slice_in_dim(grad_attended, half - own_half, half, 1)
    grad_heads = pair(keep, swap(send, 0), core, 0).reshape(near, half)

    grad_query, grad_key, grad_value = attend_back(
        far, query, key, value, grad_heads, attended_heads, logsum
    )

    shape = (count // 2, 2 * slice_rows, half)
    q_grad = dot_tn(normed[:near], grad_query).reshape(shape)
    k_grad = dot_tn(normed, grad_key).reshape(shape)
    v_grad = dot_tn(normed, grad_value).reshape(shape)
    totals = scatter_links([[q_grad], [k_grad], [v_grad]], plans)
    first, last = finish(jnp.concatenate(totals, 1), slice_rows, 3 * width)
    qkv_weight_grad = jnp.stack(
        [first.reshape(slice_rows, 3, half), last.reshape(slice_rows, 3, half)], 2
    ).reshape(slice_rows, 3 * width)
    zero = jnp.zeros((half,), FULL)
    q_sum = jnp.sum(grad_query.astype(FULL), 0)
    v_sum = jnp.sum(grad_value.astype(FULL), 0)
    low_core = core == 0
    qv_bias_grad = jnp.concatenate(
        [
            jnp.where(low_core, q_sum, zero),
            jnp.where(low_core, zero, q_sum),
            jnp.where(low_core, v_sum, zero),
            jnp.where(low_core, zero, v_sum),
        ]
    )

    part = dot_nt(grad_key, k_weight) + dot_nt(grad_value, v_weight)
    part_near = part[:near] + dot_nt(grad_query, q_weight)
    part_far = part[near:]
    first_gain_grad = jnp.sum(part_near * hat_all[:near], 0) + jnp.sum(
        part_far * hat_all[near:], 0
    )
    first_shift_grad = jnp.sum(part_near, 0) + jnp.sum(part_far, 0)
    keep_near, send_near = rows_to_core(part_near)
    keep_far, send_far = rows_to_core(part_far)
    got = swap(jnp.stack([send_near, send_far]).astype(LOW), 0).astype(FULL)
    back = lax.ppermute(
        (keep_far + got[1]).astype(LOW), ALL, [(b, a) for a, b in flips]
    ).astype(FULL)
    grad_normed = keep_near + got[0] + back
    hat = lax.dynamic_slice_in_dim(hat_all, own, quarter, 0)
    root = lax.dynamic_slice_in_dim(root_all, own, quarter, 0)
    grad_inputs = grad_middle + normalize_back(grad_normed, gain_one, hat, root)
    thought = lax.dynamic_slice_in_dim(thought_near, own, quarter, 0)
    kept = jnp.where(thought, 0.0, grad_inputs)
    moved = jnp.where(thought, grad_inputs, 0.0)
    parts = lax.axis_size("ctx")
    following = lax.ppermute(moved[:1], "ctx", [(i, i - 1) for i in range(1, parts)])
    tokens_grad = (kept + jnp.concatenate([moved[1:], following], 0))[None]

    grads = (
        qv_bias_grad,
        out_bias_grad,
        fc_bias_grad,
        proj_bias_grad,
        first_gain_grad,
        first_shift_grad,
        second_gain_grad,
        second_shift_grad,
    )
    sizes = [grad.shape[0] // count for grad in grads]
    packed = jnp.concatenate([g.reshape(count, s) for g, s in zip(grads, sizes)], 1)
    left = packed
    for bit in reversed(range(flat_bits())):
        place = bit_of(bit)
        size = left.shape[0] // 2
        there = lax.dynamic_slice_in_dim(left, (1 - place) * size, size, 0)
        left = lax.dynamic_slice_in_dim(left, place * size, size, 0) + swap(there, bit)
    shares, at = [], 0
    for size in sizes:
        shares.append(left[0, at : at + size])
        at += size
    return (
        mixed,
        tokens_grad,
        qkv_weight_grad,
        out_weight_grad,
        fc_weight_grad,
        proj_weight_grad,
        *shares,
    )


def solution(mesh):
    rows, matrix, vector = P("dp", "ctx", None), P(ALL, None), P(ALL)
    return jax.shard_map(
        shards,
        mesh=mesh,
        in_specs=(rows, P("dp"), P("dp", None), rows) + (matrix,) * 4 + (vector,) * 8,
        out_specs=(rows, rows) + (matrix,) * 4 + (vector,) * 8,
        check_vma=False,
    )
```

```python
import jax
import jax.numpy as jnp
from jax import lax
from jax.experimental import pallas as pl
from jax.experimental.pallas import tpu as pltpu
from jax.sharding import PartitionSpec as P

ALL = ("dp", "ctx")
LOW = jnp.bfloat16
FULL = jnp.float32
HEAD = 64
LANES = 128
SCALE = 0.125
VMEM = 48 << 20
SHORT = pl.CostEstimate(flops=1 << 29, bytes_accessed=1 << 19, transcendentals=0)


def flat_bits():
    return (lax.axis_size("dp") * lax.axis_size("ctx")).bit_length() - 1


def flat_index():
    return lax.axis_index("dp") * lax.axis_size("ctx") + lax.axis_index("ctx")


def bit_of(bit):
    return (flat_index() >> bit) & 1


def swap(value, bit):
    count = 1 << flat_bits()
    return lax.ppermute(value, ALL, [(i, i ^ (1 << bit)) for i in range(count)])


def after(value, *others):
    return lax.optimization_barrier((value, others))[0]


def pair(mine, other, place, axis):
    shape = mine.shape[:axis] + (2,) + mine.shape[axis:]
    whole = jnp.broadcast_to(jnp.expand_dims(mine, axis), shape)
    return lax.dynamic_update_slice_in_dim(whole, jnp.expand_dims(other, axis), 1 - place, axis)


def beside(mine, other, place):
    low = place == 0
    return jnp.concatenate([jnp.where(low, mine, other), jnp.where(low, other, mine)], -1)


def orders():
    rest = list(range(3, flat_bits()))
    return [1, 2] + rest, [2, 1] + rest


def grow(block, done, bit, wait=()):
    other = after(swap(block, bit), *wait)
    rows, cols = block.shape[1:]
    high = 1 << len([b for b in done if b > bit])
    low = 1 << len([b for b in done if b < bit])
    whole = pair(
        block.reshape(high, low, rows, cols), other.reshape(high, low, rows, cols), bit_of(bit), 1
    )
    return whole.reshape(high * 2 * low, rows, cols)


def gather_common(block):
    block, done = block[None], []
    for bit in reversed(range(3, flat_bits())):
        block = grow(block, done, bit)
        done.append(bit)
    return block


def gather_step(parts, plans, step, wait=()):
    out = []
    for part, order in zip(parts, plans):
        plan = list(reversed(order))
        at = flat_bits() - 3 + step
        out.append(grow(part, plan[:at], plan[at], wait))
    return out


class Sum:
    def __init__(self, addends, left, kind=LOW):
        self.addends = addends
        self.left = left
        self.kind = kind

    def total(self, bit=None, place=None):
        result = None
        for value, bits, (start, size) in self.addends:
            rows = value.shape[1]
            dims, begin, width = [], [], []
            for b in sorted(bits, reverse=True):
                dims.append(2)
                if b == bit:
                    begin.append(place)
                    width.append(1)
                elif b in self.left:
                    begin.append(0)
                    width.append(2)
                else:
                    begin.append(bit_of(b))
                    width.append(1)
            view = value.reshape(*dims, rows, value.shape[2])
            piece = lax.dynamic_slice(view, (*begin, 0, start), (*width, rows, size))
            piece = piece.reshape(-1, rows, size).astype(FULL)
            result = piece if result is None else result + piece
        return result

    def prepare(self, bit):
        send = self.total(bit, 1 - bit_of(bit)).astype(self.kind)
        return send, Sum(self.addends, [b for b in self.left if b != bit], self.kind), bit


def prepare(sums, plans, step):
    return [value.prepare(plan[step]) for value, plan in zip(sums, plans)]


def sends(prepared):
    return [send for send, _, _ in prepared]


def exchange(prepared, wait=()):
    out = []
    for send, keep, bit in prepared:
        got = after(swap(send, bit), *wait)
        out.append(Sum(keep.addends + [(got, keep.left, (0, got.shape[2]))], keep.left, keep.kind))
    return out


def start_sum(arrays, start, size, kind=LOW):
    links = list(range(1, flat_bits()))
    return Sum([(value, links, (start, size)) for value in arrays], links, kind)


def finish(total, rows):
    core = bit_of(0)
    mine = lax.dynamic_slice_in_dim(total, core * rows, rows, 0)
    other = swap(lax.dynamic_slice_in_dim(total, (1 - core) * rows, rows, 0), 0)
    return jnp.where(core == 0, mine, other), jnp.where(core == 0, other, mine)


def dot(a, b):
    return lax.dot_general(a, b, (((1,), (0,)), ((), ())), preferred_element_type=FULL)


def dot_nt(a, b):
    return lax.dot_general(a, b, (((1,), (1,)), ((), ())), preferred_element_type=FULL)


def dot_tn(a, b):
    return lax.dot_general(a, b, (((0,), (0,)), ((), ())), preferred_element_type=FULL)


def head_lanes(value, head):
    lane = lax.broadcasted_iota(jnp.int32, (1, LANES), 1)
    return jnp.where(lane // HEAD == head, value, jnp.zeros_like(value))


def causal(size):
    shape = (size, size)
    return lax.broadcasted_iota(jnp.int32, shape, 0) <= lax.broadcasted_iota(jnp.int32, shape, 1)


def attend_kernel(far_ref, q_ref, k_ref, v_ref, *refs):
    out_ref, lse_ref, top_ref, acc_ref = refs[-4:]
    size = q_ref.shape[0]
    mine = pl.program_id(0)
    query = q_ref[...] * jnp.asarray(SCALE, LOW)

    def step(block, first):
        at = pl.ds(pl.multiple_of(block * size, size), size)
        key = k_ref[at, :]
        value = jnp.transpose(v_ref[at, :])
        for head in range(2):
            ones = jnp.ones((16, size), LOW)
            wide = jnp.concatenate([value[head * HEAD : (head + 1) * HEAD], ones], 0)
            scores = dot_nt(key, head_lanes(query, head))
            row = slice(head, head + 1)
            if first:
                scores = jnp.where(causal(size), scores, -1e9)
                top = jnp.max(scores, 0, keepdims=True)
                acc_ref[head] = dot(wide, jnp.exp(scores - top).astype(LOW))
            else:
                old = top_ref[row, :]
                top = jnp.maximum(old, jnp.max(scores, 0, keepdims=True))
                acc_ref[head] = acc_ref[head] * jnp.exp(old - top) + dot(
                    wide, jnp.exp(scores - top).astype(LOW)
                )
            top_ref[row, :] = top

    step(mine, True)

    @pl.loop(0, mine + far_ref[0])
    def _(i):
        step(jnp.where(i < mine, 0, 2 + i - mine), False)

    outs = []
    for head in range(2):
        total = acc_ref[head, HEAD : HEAD + 1, :]
        outs.append(acc_ref[head, :HEAD, :] / total)
        lse_ref[0, head : head + 1, :] = top_ref[head : head + 1, :] + jnp.log(total)
    out_ref[...] = jnp.transpose(jnp.concatenate(outs, 0)).astype(LOW)


def attend(far, query, keyval, quarter, which, earlier):
    near, width = query.shape
    total = keyval.shape[0]
    pairs = width // LANES
    rows = pl.BlockSpec((quarter, LANES), lambda i, s: (i, which))
    return pl.pallas_call(
        attend_kernel,
        out_shape=(
            jax.ShapeDtypeStruct((near, width), LOW),
            jax.ShapeDtypeStruct((pairs, 8, near), FULL),
        ),
        grid_spec=pltpu.PrefetchScalarGridSpec(
            num_scalar_prefetch=1,
            grid=(near // quarter,),
            in_specs=[
                rows,
                pl.BlockSpec((total, LANES), lambda i, s: (0, which)),
                pl.BlockSpec((total, LANES), lambda i, s: (0, which + pairs)),
            ]
            + [pl.BlockSpec(memory_space=pl.ANY)] * len(earlier),
            out_specs=(rows, pl.BlockSpec((1, 8, quarter), lambda i, s: (which, 0, i))),
            scratch_shapes=[
                pltpu.VMEM((8, quarter), FULL),
                pltpu.VMEM((2, HEAD + 16, quarter), FULL),
            ],
        ),
        input_output_aliases={4 + i: i for i in range(len(earlier))},
        compiler_params=pltpu.CompilerParams(vmem_limit_bytes=VMEM),
        cost_estimate=SHORT,
        name="attend",
    )(far, query, keyval, keyval, *earlier)


def attend_back_kernel(
    far_ref, q_ref, k_ref, v_ref, grad_ref, out_ref, lse_ref, *refs
):
    dq_ref, dk_ref, dv_ref, acc_ref = refs[-4:]
    near = q_ref.shape[0]
    size = near // 2
    spans = (slice(0, size), slice(size, near))
    query = q_ref[...] * jnp.asarray(SCALE, LOW)
    grad = grad_ref[...]
    product = jnp.transpose(grad.astype(FULL) * out_ref[...].astype(FULL))
    delta = [
        jnp.sum(product[head * HEAD : (head + 1) * HEAD], 0, keepdims=True) for head in range(2)
    ]

    def block(at, work):
        key, value = k_ref[at, :], v_ref[at, :]
        turned = jnp.transpose(key)
        dk = dv = None
        for which, masked, first in work:
            span = spans[which]
            for head in range(2):
                part = slice(head * HEAD, (head + 1) * HEAD)
                q_head = head_lanes(query[span], head)
                g_head = head_lanes(grad[span], head)
                probs = jnp.exp(dot_nt(key, q_head) - lse_ref[0, head : head + 1, span])
                if masked:
                    probs = jnp.where(causal(size), probs, 0.0)
                moved = probs * (dot_nt(value, g_head) - delta[head][:, span])
                moved, probs = moved.astype(LOW), probs.astype(LOW)
                new_k, new_v = dot(moved, q_head), dot(probs, g_head)
                dk = new_k if dk is None else dk + new_k
                dv = new_v if dv is None else dv + new_v
                new_q = dot(turned[part], moved)
                if first:
                    acc_ref[which, part, :] = new_q
                else:
                    acc_ref[which, part, :] += new_q
        dk_ref[at, :] = dk.astype(LOW)
        dv_ref[at, :] = dv.astype(LOW)

    block(spans[0], [(0, True, True), (1, False, True)])
    block(spans[1], [(1, True, False)])

    @pl.loop(0, far_ref[0])
    def _(i):
        at = pl.ds(pl.multiple_of(near + i * size, size), size)
        block(at, [(0, False, False), (1, False, False)])

    @pl.loop(far_ref[0], 2)
    def _(i):
        at = pl.ds(pl.multiple_of(near + i * size, size), size)
        dk_ref[at, :] = jnp.zeros((size, LANES), LOW)
        dv_ref[at, :] = jnp.zeros((size, LANES), LOW)

    for which in range(2):
        dq_ref[spans[which], :] = (jnp.transpose(acc_ref[which]) * SCALE).astype(LOW)


def attend_back(far, query, keyval, grad, out, lse, which, earlier):
    near, width = query.shape
    total = keyval.shape[0]
    pairs = width // LANES
    rows = pl.BlockSpec((near, LANES), lambda p, s: (0, which))
    every = pl.BlockSpec((total, LANES), lambda p, s: (0, which))
    return pl.pallas_call(
        attend_back_kernel,
        out_shape=(
            jax.ShapeDtypeStruct((near, width), LOW),
            jax.ShapeDtypeStruct((total, width), LOW),
            jax.ShapeDtypeStruct((total, width), LOW),
        ),
        grid_spec=pltpu.PrefetchScalarGridSpec(
            num_scalar_prefetch=1,
            grid=(1,),
            in_specs=[
                rows,
                every,
                pl.BlockSpec((total, LANES), lambda p, s: (0, which + pairs)),
                rows,
                rows,
                pl.BlockSpec((1, 8, near), lambda p, s: (which, 0, 0)),
            ]
            + [pl.BlockSpec(memory_space=pl.ANY)] * len(earlier),
            out_specs=(rows, every, every),
            scratch_shapes=[pltpu.VMEM((2, LANES, near // 2), FULL)],
        ),
        input_output_aliases={7 + i: i for i in range(len(earlier))},
        compiler_params=pltpu.CompilerParams(vmem_limit_bytes=VMEM),
        cost_estimate=SHORT,
        name="attend_back",
    )(far, query, keyval, keyval, grad, out, lse, *earlier)


def grads_kernel(n_ref, dq_ref, dk_ref, dv_ref, a_ref, b_ref):
    near, width = dq_ref.shape
    turned = jnp.transpose(n_ref[...])
    low = jnp.concatenate(
        [
            dot(turned[:, :near], dq_ref[...]).astype(LOW),
            dot(turned, dk_ref[...]).astype(LOW),
            dot(turned, dv_ref[...]).astype(LOW),
        ],
        1,
    )
    cut = a_ref.shape[1]
    a_ref[...] = low[:, :cut]
    b_ref[...] = low[:, cut:]


def qkv_grads(normed, dq, dk, dv):
    width = normed.shape[1]
    cols = 3 * dq.shape[1]
    cut = (cols // LANES + 1) // 2 * LANES
    return pl.pallas_call(
        grads_kernel,
        out_shape=(
            jax.ShapeDtypeStruct((width, cut), LOW),
            jax.ShapeDtypeStruct((width, cols - cut), LOW),
        ),
        compiler_params=pltpu.CompilerParams(vmem_limit_bytes=VMEM),
        cost_estimate=SHORT,
        name="qkv_grads",
    )(normed, dq, dk, dv)


CURVE = 0.7978845608028654
CUBIC = 0.044715


def feed_kernel(
    core_ref, n_ref, g_ref, fc_ref, fb_ref, pr_ref,
    out_ref, back_ref, fc_grad_ref, pr_grad_ref, fb_grad_ref, turned_ref,
):
    step = pl.program_id(0)
    half = g_ref.shape[1] // 2

    @pl.when(step == 0)
    def _():
        turned_ref[...] = jnp.transpose(n_ref[...])

    proj = pr_ref[...].reshape(fc_ref.shape[1], n_ref.shape[1])
    grad = g_ref[...]
    hidden = dot(n_ref[...], fc_ref[...]) + fb_ref[...]
    square = hidden * hidden
    bend = jnp.tanh(hidden * (CURVE + (CURVE * CUBIC) * square))
    gate = 0.5 * (1.0 + bend)
    active = (hidden * gate).astype(LOW)
    slope = gate + hidden * (0.5 * (1.0 - bend * bend)) * (
        CURVE + (3 * CURVE * CUBIC) * square
    )
    grad_hidden = (dot_nt(grad, proj) * slope).astype(LOW)
    out, back = dot(active, proj), dot_nt(grad_hidden, fc_ref[...])

    @pl.when(step == 0)
    def _():
        out_ref[...] = out
        back_ref[...] = back

    @pl.when(step > 0)
    def _():
        out_ref[...] += out
        back_ref[...] += back

    fb_grad_ref[...] = jnp.sum(grad_hidden.astype(FULL), 0, keepdims=True)
    fc_grad_ref[0] = dot(turned_ref[...], grad_hidden).astype(LOW)
    pr_grad = dot_tn(active, grad)
    low, high = pr_grad[:, :half].astype(LOW), pr_grad[:, half:].astype(LOW)
    first = core_ref[0] == 0
    pr_grad_ref[0] = jnp.where(first, high, low)
    pr_grad_ref[1] = jnp.where(first, low, high)


def feed(core, normed, grad, fc, fc_bias, proj, proj_rows):
    rows, width = normed.shape
    hidden = fc.shape[1]
    chunk = hidden // 4
    group = chunk // proj_rows
    steps = hidden // (2 * chunk)

    def block(i, s):
        return jnp.where(i < steps, (1 - s[0]) * steps + i, s[0] * steps + i - steps)

    whole = pl.BlockSpec((rows, width), lambda i, s: (0, 0))
    return pl.pallas_call(
        feed_kernel,
        out_shape=(
            jax.ShapeDtypeStruct((rows, width), FULL),
            jax.ShapeDtypeStruct((rows, width), FULL),
            jax.ShapeDtypeStruct((2, width, hidden // 2), LOW),
            jax.ShapeDtypeStruct((2, hidden, width // 2), LOW),
            jax.ShapeDtypeStruct((1, hidden), FULL),
        ),
        grid_spec=pltpu.PrefetchScalarGridSpec(
            num_scalar_prefetch=1,
            grid=(2 * steps,),
            in_specs=[
                whole,
                whole,
                pl.BlockSpec((width, chunk), lambda i, s: (0, block(i, s))),
                pl.BlockSpec((1, chunk), lambda i, s: (0, block(i, s))),
                pl.BlockSpec((group, proj_rows, width), lambda i, s: (block(i, s), 0, 0)),
            ],
            out_specs=(
                whole,
                whole,
                pl.BlockSpec(
                    (1, width, chunk), lambda i, s: (jnp.where(i < steps, 0, 1), 0, lax.rem(i, steps))
                ),
                pl.BlockSpec((2, chunk, width // 2), lambda i, s: (0, block(i, s), 0)),
                pl.BlockSpec((1, chunk), lambda i, s: (0, block(i, s))),
            ),
            scratch_shapes=[pltpu.VMEM((width, rows), LOW)],
        ),
        compiler_params=pltpu.CompilerParams(vmem_limit_bytes=VMEM),
        cost_estimate=SHORT,
        name="feed",
    )(core, normed, grad, fc, fc_bias, proj)


def turn_kernel(
    core_ref, n_ref, hat_ref, root_ref, gain_ref, g_ref, att_ref, w_ref,
    middle_ref, keep_ref, send_ref, w_keep_ref, w_send_ref, gain_grad_ref, shift_ref, bias_ref,
):
    half = keep_ref.shape[1]
    grad, hat = n_ref[...], hat_ref[...]
    gain_grad_ref[...] = jnp.sum(grad * hat, 0, keepdims=True)
    shift_ref[...] = jnp.sum(grad, 0, keepdims=True)
    middle = g_ref[...].astype(FULL) + normalize_back(grad, gain_ref[...], hat, root_ref[...])
    middle_ref[...] = middle
    low = middle.astype(LOW)
    bias_ref[...] = jnp.sum(low.astype(FULL), 0, keepdims=True)
    first = core_ref[0] == 0
    for whole, kept, sent in (
        (dot_nt(low, w_ref[...]), keep_ref, send_ref),
        (dot(jnp.transpose(att_ref[...]), low), w_keep_ref, w_send_ref),
    ):
        whole = whole.astype(LOW)
        one, two = whole[:, :half], whole[:, half:]
        kept[...] = jnp.where(first, one, two)
        sent[...] = jnp.where(first, two, one)


def turn(core, grad, hat, root, gain, grad_valid, attended, weight):
    rows, width = grad.shape
    vmem = pl.BlockSpec(memory_space=pltpu.VMEM)
    shape = jax.ShapeDtypeStruct
    return pl.pallas_call(
        turn_kernel,
        in_specs=[pl.BlockSpec(memory_space=pltpu.SMEM)] + [vmem] * 7,
        out_shape=(
            shape((rows, width), FULL),
            shape((rows, width // 2), LOW),
            shape((rows, width // 2), LOW),
            shape((width, width // 2), LOW),
            shape((width, width // 2), LOW),
            shape((1, width), FULL),
            shape((1, width), FULL),
            shape((1, width), FULL),
        ),
        compiler_params=pltpu.CompilerParams(vmem_limit_bytes=VMEM),
        cost_estimate=SHORT,
        name="turn",
    )(core, grad, hat, root, gain, grad_valid, attended, weight)


def norm_back_kernel(
    core_ref, dq_ref, dk_ref, dv_ref, wq_ref, wkv_ref, hat_ref,
    keep_ref, send_ref, gain_ref, shift_ref, q_sum_ref, v_sum_ref, part_ref,
):
    step = pl.program_id(0)
    half = dk_ref.shape[1]
    part_ref[...] = dot_nt(dk_ref[...], wkv_ref[:, :half]) + dot_nt(
        dv_ref[...], wkv_ref[:, half:]
    )

    @pl.when(step == 0)
    def _():
        for ref in (gain_ref, shift_ref, q_sum_ref, v_sum_ref):
            ref[...] = jnp.zeros_like(ref)

    @pl.when(lax.rem(step, 2) == 1)
    def _():
        part_ref[...] += dot_nt(dq_ref[...], wq_ref[...])
        q_sum_ref[...] += jnp.sum(dq_ref[...].astype(FULL), 0, keepdims=True)

    part = part_ref[...]
    v_sum_ref[...] += jnp.sum(dv_ref[...].astype(FULL), 0, keepdims=True)
    gain_ref[...] += jnp.sum(part * hat_ref[...], 0, keepdims=True)
    shift_ref[...] += jnp.sum(part, 0, keepdims=True)

    @pl.when(step < 2)
    def _():
        send_ref[0] = part.astype(LOW)

    @pl.when(step >= 2)
    def _():
        keep_ref[0] = part


def norm_back(core, dq, dk, dv, q_weight, keyval_weight, hat):
    quarter, half, width = dq.shape[0] // 2, dq.shape[1], hat.shape[1]

    def at(i, s):
        return jnp.where(i < 2, 1 - s[0], s[0])

    def block(i, s):
        return (jnp.where(lax.rem(i, 2) == 0, 2, 0) + at(i, s), 0)

    whole = lambda i, s: (0, 0)
    line, short = pl.BlockSpec((1, width), whole), pl.BlockSpec((1, half), whole)
    shape = jax.ShapeDtypeStruct
    return pl.pallas_call(
        norm_back_kernel,
        out_shape=(
            shape((2, quarter, width), FULL),
            shape((2, quarter, width), LOW),
            shape((1, width), FULL),
            shape((1, width), FULL),
            shape((1, half), FULL),
            shape((1, half), FULL),
        ),
        grid_spec=pltpu.PrefetchScalarGridSpec(
            num_scalar_prefetch=1,
            grid=(4,),
            in_specs=[
                pl.BlockSpec((quarter, half), lambda i, s: (at(i, s), 0)),
                pl.BlockSpec((quarter, half), block),
                pl.BlockSpec((quarter, half), block),
                pl.BlockSpec((width, half), whole),
                pl.BlockSpec((width, 2 * half), whole),
                pl.BlockSpec((quarter, width), block),
            ],
            out_specs=(
                pl.BlockSpec((1, quarter, width), lambda i, s: (jnp.maximum(i - 2, 0), 0, 0)),
                pl.BlockSpec((1, quarter, width), lambda i, s: (jnp.minimum(i, 1), 0, 0)),
                line,
                line,
                short,
                short,
            ),
            scratch_shapes=[pltpu.VMEM((quarter, width), FULL)],
        ),
        compiler_params=pltpu.CompilerParams(vmem_limit_bytes=VMEM),
        cost_estimate=SHORT,
        name="norm_back",
    )(core, dq, dk, dv, q_weight, keyval_weight, hat)


def normalize(values):
    center = values - jnp.mean(values, -1, keepdims=True)
    spread = jnp.mean(center * center, -1, keepdims=True)
    root = lax.rsqrt(spread + 1e-05)
    return center * root, root


def normalize_back(grad, gain, hat, root):
    scaled = grad * gain
    return root * (
        scaled
        - jnp.mean(scaled, -1, keepdims=True)
        - hat * jnp.mean(scaled * hat, -1, keepdims=True)
    )


def shards(
    tokens,
    lengths,
    thought_pos,
    cotangent,
    qkv_weight,
    out_weight,
    fc_weight,
    proj_weight,
    qv_bias,
    out_bias,
    fc_bias,
    proj_bias,
    first_gain,
    first_shift,
    second_gain,
    second_shift,
):
    _, quarter, width = tokens.shape
    half = width // 2
    near = 2 * quarter
    slice_rows = qkv_weight.shape[0]
    count = 1 << flat_bits()
    plans = orders()
    core, second = bit_of(0), bit_of(1)
    far = (2 * second).astype(jnp.int32).reshape(1)

    high, hidden_width = proj_weight.shape[0], fc_weight.shape[1]
    blocks = hidden_width // width
    fc_rows = [fc_weight[:, i * width : (i + 1) * width] for i in range(blocks)]
    late = lax.all_gather(
        jnp.concatenate([proj_weight, *fc_rows, out_weight], 0), ALL, axis=0, tiled=True
    ).reshape(count, high + (blocks + 1) * slice_rows, width)

    mine = tokens[0]
    flips = [(i, i ^ 2) for i in range(count) if not i & 2]
    before = lax.ppermute(mine, ALL, flips)
    near_tokens = pair(mine, swap(mine, 0), core, 0).reshape(near, width)

    third = slice_rows * 4
    small = jnp.zeros((slice_rows, LANES), LOW)
    rows_of = (
        jnp.concatenate([qv_bias, out_bias, first_gain]),
        fc_bias,
        jnp.concatenate([proj_bias, first_shift, second_gain, second_shift]),
    )
    small = small.at[:3, :third].set(jnp.stack(rows_of))
    split = qkv_weight.reshape(slice_rows, 3, 2, half)
    keep = lax.dynamic_index_in_dim(split, core, 2, keepdims=False).reshape(slice_rows, 3 * half)
    send = lax.dynamic_index_in_dim(split, 1 - core, 2, keepdims=False).reshape(
        slice_rows, 3 * half
    )
    keep, send = jnp.concatenate([keep, small], 1), jnp.concatenate([send, small], 1)
    chip = pair(keep, swap(send, 0), core, 0).reshape(2 * slice_rows, 3 * half + LANES)
    block = gather_common(chip)
    parts = [
        jnp.concatenate([block[:, :, :half], block[:, :, 3 * half :]], 2),
        block[:, :, half : 3 * half],
    ]
    first_parts = gather_step(parts, plans, 0)

    before = after(before, block)
    far_tokens = pair(before, swap(before, 0), core, 0).reshape(near, width)
    slots = jnp.arange(near, dtype=jnp.int32)
    thoughts = thought_pos[0]

    def is_thought(at_slots):
        return jnp.any(thoughts[None, :] == at_slots[:, None], 1, keepdims=True)

    thought_near = is_thought(second * near + slots)
    thought_far = is_thought(slots)
    shifted_near = jnp.concatenate([far_tokens[-1:], near_tokens[:-1]], 0)
    shifted_far = jnp.concatenate([far_tokens[:1], far_tokens[:-1]], 0)
    inputs_near = jnp.where(thought_near, shifted_near, near_tokens)
    inputs_far = jnp.where(thought_far, shifted_far, far_tokens)
    inputs_all = jnp.concatenate([inputs_near, inputs_far], 0)
    hat_all, root_all = normalize(inputs_all.astype(FULL))
    own = core * quarter
    inputs = lax.dynamic_slice_in_dim(inputs_near, own, quarter, 0).astype(FULL)

    parts = gather_step(first_parts, plans, 1, (hat_all, root_all))
    q_weight = parts[0][:, :, :half].reshape(width, half)
    keyval_weight = parts[1].reshape(width, 2 * half)
    small = parts[0].reshape(count, slice_rows, half + LANES)[:, :3, half : half + third]
    small = small.astype(FULL)
    at = slice_rows

    def vector(row, first, size):
        return small[:, row, first : first + size].reshape(1, count * size)

    qv_full = vector(0, 0, 2 * at)
    out_bias_full, gain_one = vector(0, 2 * at, at), vector(0, 3 * at, at)
    fc_bias_full = vector(1, 0, 4 * at)
    proj_bias_full, shift_one = vector(2, 0, at), vector(2, at, at)
    gain_two, shift_two = vector(2, 2 * at, at), vector(2, 3 * at, at)

    normed = (hat_all * gain_one + shift_one).astype(LOW)
    own_half = core * half
    q_bias = lax.dynamic_slice_in_dim(qv_full[:, :width], own_half, half, 1)
    v_bias = lax.dynamic_slice_in_dim(qv_full[:, width:], own_half, half, 1)
    query = (dot(normed[:near], q_weight) + q_bias).astype(LOW)
    keyval_bias = jnp.concatenate([jnp.zeros((1, half), FULL), v_bias], 1)
    keyval = (dot(normed, keyval_weight) + keyval_bias).astype(LOW)

    def rows_to_core(array):
        return (
            lax.dynamic_slice_in_dim(array, own, quarter, 0),
            lax.dynamic_slice_in_dim(array, quarter - own, quarter, 0),
        )

    pairs = half // LANES
    heads = ()
    for which in range(pairs):
        heads = attend(far, query, keyval, quarter, which, heads)
    heads, logsums = heads
    keep, send = rows_to_core(heads)
    attended = beside(keep, swap(send, 0), core)
    late = after(late, attended)
    fc_full = late[:, high : high + blocks * slice_rows]
    fc_full = fc_full.reshape(count, blocks, slice_rows, width).transpose(0, 2, 1, 3)
    fc_full = fc_full.reshape(width, hidden_width)
    out_full = late[:, high + blocks * slice_rows :].reshape(width, width)

    middle = inputs + dot(attended, out_full) + out_bias_full
    hat_two, root_two = normalize(middle)
    normed_two = (hat_two * gain_two + shift_two).astype(LOW)
    my_slots = (2 * second + core) * quarter + jnp.arange(quarter, dtype=jnp.int32)
    valid = (my_slots < lengths[0])[:, None]
    grad_valid = jnp.where(valid, cotangent[0], jnp.zeros_like(cotangent[0]))
    proj_full, proj_rows = late, high
    if high % 16:
        proj_full, proj_rows = late[:, :high].reshape(1, hidden_width, width), hidden_width // 4
        proj_full = proj_full.reshape(4, proj_rows, width)
    core_at = core.astype(jnp.int32).reshape(1)
    fed, grad_normed_two, fc_grads, proj_grads, fc_bias_grad = feed(
        core_at, normed_two, grad_valid, fc_full, fc_bias_full, proj_full, proj_rows
    )
    fc_bias_grad = fc_bias_grad[0]
    output = middle + fed + proj_bias_full
    mixed = jnp.where(valid, output, 0.0).astype(LOW)[None]
    proj_bias_grad = jnp.sum(grad_valid.astype(FULL), 0)

    chips = count // 2
    fc_shape = (chips, 2 * slice_rows, hidden_width // 2)
    fc_pair = [fc_grads[1].reshape(fc_shape), swap(fc_grads[0], 0).reshape(fc_shape)]

    turned = turn(
        core_at, grad_normed_two, hat_two, root_two, gain_two, grad_valid, attended, out_full
    )
    grad_middle, keep, send, out_kept, out_send = turned[:5]
    second_gain_grad, second_shift_grad, out_bias_grad = (value[0] for value in turned[5:])
    grad_heads = pair(keep, swap(send, 0), core, 0).reshape(near, half)
    out_shape = (chips, 2 * slice_rows, half)
    proj_shape = (chips, 2 * high, half)
    proj_kept, proj_send = (
        jnp.concatenate(
            [grad.reshape(proj_shape), other.reshape(out_shape)], 1
        )
        for grad, other in ((proj_grads[1], out_kept), (proj_grads[0], out_send))
    )
    proj_pair = [proj_kept, swap(proj_send, 0)]
    early = [start_sum(fc_pair, 0, hidden_width // 2), start_sum(proj_pair, 0, half)]
    early_plans = plans
    ready = prepare(early, early_plans, 0)

    grads = ()
    now = after(grad_heads, *sends(ready))
    for which in range(pairs):
        if which == 2:
            ready = prepare(exchange(ready, grads), early_plans, 1)
            now = after(grad_heads, *sends(ready))
        grads = attend_back(
            far, query, keyval, now, heads, logsums, which, grads
        )
    ready = prepare(exchange(ready, grads), early_plans, 2)
    grad_query, grad_key, grad_value = after(grads, *sends(ready))

    last = [
        start_sum([value.reshape(chips, 2 * slice_rows, -1)], 0, value.shape[1])
        for value in qkv_grads(normed, grad_query, grad_key, grad_value)
    ]
    last_ready = prepare(last, plans, 0)

    part, part_send, first_gain_grad, first_shift_grad, q_sum, v_sum = norm_back(
        core_at,
        after(grad_query, *sends(last_ready)),
        grad_key,
        grad_value,
        q_weight,
        keyval_weight,
        hat_all,
    )
    got = swap(part_send, 0)
    ready = prepare(exchange(ready, (part_send,)), early_plans, 3)
    last = exchange(last_ready, (part_send,))
    last_ready = prepare(last, plans, 1)
    got = after(got, *sends(last_ready), *sends(ready))
    far_sum = (part[0] + got[0].astype(FULL)).astype(LOW)
    back = lax.ppermute(far_sum, ALL, [(b, a) for a, b in flips])
    first_gain_grad, first_shift_grad, q_sum, v_sum = (
        value[0] for value in (first_gain_grad, first_shift_grad, q_sum, v_sum)
    )
    zero = jnp.zeros((half,), FULL)
    low_core = core == 0
    qv_bias_grad = jnp.concatenate(
        [
            jnp.where(low_core, q_sum, zero),
            jnp.where(low_core, zero, q_sum),
            jnp.where(low_core, v_sum, zero),
            jnp.where(low_core, zero, v_sum),
        ]
    )
    grads = (
        qv_bias_grad,
        out_bias_grad,
        fc_bias_grad,
        proj_bias_grad,
        first_gain_grad,
        first_shift_grad,
        second_gain_grad,
        second_shift_grad,
    )
    sizes = [grad.shape[0] // count for grad in grads]
    packed = jnp.concatenate([g.reshape(count, s) for g, s in zip(grads, sizes)], 1)
    share = jnp.sum(lax.all_to_all(packed, ALL, 0, 0, tiled=True), 0, keepdims=True)
    for step in range(2, flat_bits() - 1):
        last = exchange(last_ready, (far_sum,))
        last_ready = prepare(last, plans, step)
    last = exchange(last_ready)
    for step in range(4, flat_bits() - 1):
        ready = prepare(exchange(ready), early_plans, step)
    early = exchange(ready, (far_sum,))
    fc_total, proj_total = (value.total()[0] for value in early)
    fc_weight_grad = jnp.concatenate(finish(fc_total, slice_rows), 1)

    def by_core(total):
        mine = lax.dynamic_slice_in_dim(total, core * (total.shape[0] // 2), total.shape[0] // 2, 0)
        return mine

    def by_other(total):
        size = total.shape[0] // 2
        return lax.dynamic_slice_in_dim(total, (1 - core) * size, size, 0)

    proj_part, out_part = proj_total[: 2 * high], proj_total[2 * high :]
    mine = jnp.concatenate([by_core(proj_part), by_core(out_part)], 0)
    other = swap(jnp.concatenate([by_other(proj_part), by_other(out_part)], 0), 0)
    both = beside(mine, other, core)
    proj_weight_grad, out_weight_grad = both[:high], both[high:]
    sides = finish(jnp.concatenate([value.total()[0] for value in last], 1), slice_rows)
    qkv_weight_grad = jnp.concatenate(
        [
            side[:, kind * half : (kind + 1) * half]
            for kind in range(3)
            for side in sides
        ],
        1,
    )

    grad_normed = part[1] + got[1].astype(FULL) + back.astype(FULL)
    hat = lax.dynamic_slice_in_dim(hat_all, own, quarter, 0)
    root = lax.dynamic_slice_in_dim(root_all, own, quarter, 0)
    grad_inputs = grad_middle + normalize_back(grad_normed, gain_one, hat, root)
    thought = lax.dynamic_slice_in_dim(thought_near, own, quarter, 0)
    kept = jnp.where(thought, 0.0, grad_inputs)
    moved = jnp.where(thought, grad_inputs, 0.0)
    ctx = lax.axis_size("ctx")
    following = lax.ppermute(moved[:1], "ctx", [(i, i - 1) for i in range(1, ctx)])
    tokens_grad = (kept + jnp.concatenate([moved[1:], following], 0))[None]

    shares, at = [], 0
    for size in sizes:
        shares.append(share[0, at : at + size])
        at += size
    return (
        mixed,
        tokens_grad,
        qkv_weight_grad,
        out_weight_grad,
        fc_weight_grad,
        proj_weight_grad,
        *shares,
    )


def solution(mesh):
    rows, matrix, vector = P("dp", "ctx", None), P(ALL, None), P(ALL)
    return jax.shard_map(
        shards,
        mesh=mesh,
        in_specs=(rows, P("dp"), P("dp", None), rows) + (matrix,) * 4 + (vector,) * 8,
        out_specs=(rows, rows) + (matrix,) * 4 + (vector,) * 8,
        check_vma=False,
    )
```

```python
import functools

import jax
import jax.numpy as jnp
from jax import lax
from jax.experimental import pallas as pl
from jax.experimental.pallas import tpu as pltpu
from jax.sharding import PartitionSpec as P

ALL = ("dp", "ctx")
LOW = jnp.bfloat16
FULL = jnp.float32
HEAD = 64
LANES = 128
SCALE = 0.125
VMEM = 48 << 20
SHORT = pl.CostEstimate(flops=1 << 29, bytes_accessed=1 << 19, transcendentals=0)


def flat_bits():
    return (lax.axis_size("dp") * lax.axis_size("ctx")).bit_length() - 1


def flat_index():
    return lax.axis_index("dp") * lax.axis_size("ctx") + lax.axis_index("ctx")


def bit_of(bit):
    return (flat_index() >> bit) & 1


def swap(value, bit):
    count = 1 << flat_bits()
    return lax.ppermute(value, ALL, [(i, i ^ (1 << bit)) for i in range(count)])


def after(value, *others):
    return lax.optimization_barrier((value, others))[0]


def pair(mine, other, place, axis):
    shape = mine.shape[:axis] + (2,) + mine.shape[axis:]
    whole = jnp.broadcast_to(jnp.expand_dims(mine, axis), shape)
    return lax.dynamic_update_slice_in_dim(whole, jnp.expand_dims(other, axis), 1 - place, axis)


def beside(mine, other, place):
    low = place == 0
    return jnp.concatenate([jnp.where(low, mine, other), jnp.where(low, other, mine)], -1)


def orders():
    rest = list(range(3, flat_bits()))
    return [1, 2] + rest, [2, 1] + rest


def grow(block, done, bit, wait=()):
    other = after(swap(block, bit), *wait)
    rows, cols = block.shape[1:]
    high = 1 << len([b for b in done if b > bit])
    low = 1 << len([b for b in done if b < bit])
    whole = pair(
        block.reshape(high, low, rows, cols), other.reshape(high, low, rows, cols), bit_of(bit), 1
    )
    return whole.reshape(high * 2 * low, rows, cols)


def gather_common(block, wait):
    block, done = block[None], []
    for bit in reversed(range(3, flat_bits())):
        block = grow(block, done, bit, wait if bit == 3 else ())
        done.append(bit)
    return block


def gather_step(parts, plans, step, wait=()):
    out = []
    for part, order in zip(parts, plans):
        plan = list(reversed(order))
        at = flat_bits() - 3 + step
        out.append(grow(part, plan[:at], plan[at], wait))
    return out


class Sum:
    def __init__(self, addends, left, kind=LOW):
        self.addends = addends
        self.left = left
        self.kind = kind

    def total(self, bit=None, place=None):
        result = None
        for value, bits, (start, size) in self.addends:
            rows = value.shape[1]
            dims, begin, width = [], [], []
            for b in sorted(bits, reverse=True):
                dims.append(2)
                if b == bit:
                    begin.append(place)
                    width.append(1)
                elif b in self.left:
                    begin.append(0)
                    width.append(2)
                else:
                    begin.append(bit_of(b))
                    width.append(1)
            view = value.reshape(*dims, rows, value.shape[2])
            piece = lax.dynamic_slice(view, (*begin, 0, start), (*width, rows, size))
            piece = piece.reshape(-1, rows, size).astype(FULL)
            result = piece if result is None else result + piece
        return result

    def prepare(self, bit):
        send = self.total(bit, 1 - bit_of(bit)).astype(self.kind)
        return send, Sum(self.addends, [b for b in self.left if b != bit], self.kind), bit


def prepare(sums, plans, step):
    return [value.prepare(plan[step]) for value, plan in zip(sums, plans)]


def sends(prepared):
    return [send for send, _, _ in prepared]


def exchange(prepared, wait=()):
    out = []
    for send, keep, bit in prepared:
        got = after(swap(send, bit), *wait)
        out.append(Sum(keep.addends + [(got, keep.left, (0, got.shape[2]))], keep.left, keep.kind))
    return out


def start_sum(arrays, start, size, kind=LOW):
    links = list(range(1, flat_bits()))
    return Sum([(value, links, (start, size)) for value in arrays], links, kind)


def finish(total, rows):
    core = bit_of(0)
    mine = lax.dynamic_slice_in_dim(total, core * rows, rows, 0)
    other = swap(lax.dynamic_slice_in_dim(total, (1 - core) * rows, rows, 0), 0)
    return jnp.where(core == 0, mine, other), jnp.where(core == 0, other, mine)


def dot(a, b):
    return lax.dot_general(a, b, (((1,), (0,)), ((), ())), preferred_element_type=FULL)


def dot_nt(a, b):
    return lax.dot_general(a, b, (((1,), (1,)), ((), ())), preferred_element_type=FULL)


def dot_tn(a, b):
    return lax.dot_general(a, b, (((0,), (0,)), ((), ())), preferred_element_type=FULL)


def head_lanes(value, head):
    lane = lax.broadcasted_iota(jnp.int32, (1, LANES), 1)
    return jnp.where(lane // HEAD == head, value, jnp.zeros_like(value))


def causal(size):
    shape = (size, size)
    return lax.broadcasted_iota(jnp.int32, shape, 0) <= lax.broadcasted_iota(jnp.int32, shape, 1)


def attend_kernel(far_ref, q_ref, k_ref, v_ref, *refs):
    out_ref, lse_ref, top_ref, acc_ref = refs[-4:]
    size = q_ref.shape[0]
    mine = pl.program_id(0)
    query = q_ref[...] * jnp.asarray(SCALE, LOW)

    def step(block, first):
        at = pl.ds(pl.multiple_of(block * size, size), size)
        key = k_ref[at, :]
        value = jnp.transpose(v_ref[at, :])
        for head in range(2):
            ones = jnp.ones((16, size), LOW)
            wide = jnp.concatenate([value[head * HEAD : (head + 1) * HEAD], ones], 0)
            scores = dot_nt(key, head_lanes(query, head))
            row = slice(head, head + 1)
            if first:
                scores = jnp.where(causal(size), scores, -1e9)
                top = jnp.max(scores, 0, keepdims=True)
                acc_ref[head] = dot(wide, jnp.exp(scores - top).astype(LOW))
            else:
                old = top_ref[row, :]
                top = jnp.maximum(old, jnp.max(scores, 0, keepdims=True))
                acc_ref[head] = acc_ref[head] * jnp.exp(old - top) + dot(
                    wide, jnp.exp(scores - top).astype(LOW)
                )
            top_ref[row, :] = top

    step(mine, True)

    @pl.loop(0, mine + far_ref[0])
    def _(i):
        step(jnp.where(i < mine, 0, 2 + i - mine), False)

    outs = []
    for head in range(2):
        total = acc_ref[head, HEAD : HEAD + 1, :]
        outs.append(acc_ref[head, :HEAD, :] / total)
        lse_ref[0, head : head + 1, :] = top_ref[head : head + 1, :] + jnp.log(total)
    out_ref[...] = jnp.transpose(jnp.concatenate(outs, 0)).astype(LOW)


def attend(far, query, keyval, quarter, which, earlier):
    near, width = query.shape
    total = keyval.shape[0]
    pairs = width // LANES
    rows = pl.BlockSpec((quarter, LANES), lambda i, s: (i, which))
    return pl.pallas_call(
        attend_kernel,
        out_shape=(
            jax.ShapeDtypeStruct((near, width), LOW),
            jax.ShapeDtypeStruct((pairs, 8, near), FULL),
        ),
        grid_spec=pltpu.PrefetchScalarGridSpec(
            num_scalar_prefetch=1,
            grid=(near // quarter,),
            in_specs=[
                rows,
                pl.BlockSpec((total, LANES), lambda i, s: (0, which)),
                pl.BlockSpec((total, LANES), lambda i, s: (0, which + pairs)),
            ]
            + [pl.BlockSpec(memory_space=pl.ANY)] * len(earlier),
            out_specs=(rows, pl.BlockSpec((1, 8, quarter), lambda i, s: (which, 0, i))),
            scratch_shapes=[
                pltpu.VMEM((8, quarter), FULL),
                pltpu.VMEM((2, HEAD + 16, quarter), FULL),
            ],
        ),
        input_output_aliases={4 + i: i for i in range(len(earlier))},
        compiler_params=pltpu.CompilerParams(vmem_limit_bytes=VMEM),
        cost_estimate=SHORT,
        name="attend",
    )(far, query, keyval, keyval, *earlier)


def attend_back_kernel(
    far_ref, q_ref, k_ref, v_ref, grad_ref, out_ref, lse_ref, *refs
):
    dq_ref, dk_ref, dv_ref, acc_ref = refs[-4:]
    near = q_ref.shape[0]
    size = near // 2
    spans = (slice(0, size), slice(size, near))
    query = q_ref[...] * jnp.asarray(SCALE, LOW)
    grad = grad_ref[...]
    product = jnp.transpose(grad.astype(FULL) * out_ref[...].astype(FULL))
    delta = [
        jnp.sum(product[head * HEAD : (head + 1) * HEAD], 0, keepdims=True) for head in range(2)
    ]

    def block(at, work):
        key, value = k_ref[at, :], v_ref[at, :]
        turned = jnp.transpose(key)
        dk = dv = None
        for which, masked, first in work:
            span = spans[which]
            for head in range(2):
                part = slice(head * HEAD, (head + 1) * HEAD)
                q_head = head_lanes(query[span], head)
                g_head = head_lanes(grad[span], head)
                probs = jnp.exp(dot_nt(key, q_head) - lse_ref[0, head : head + 1, span])
                if masked:
                    probs = jnp.where(causal(size), probs, 0.0)
                moved = probs * (dot_nt(value, g_head) - delta[head][:, span])
                moved, probs = moved.astype(LOW), probs.astype(LOW)
                new_k, new_v = dot(moved, q_head), dot(probs, g_head)
                dk = new_k if dk is None else dk + new_k
                dv = new_v if dv is None else dv + new_v
                new_q = dot(turned[part], moved)
                if first:
                    acc_ref[which, part, :] = new_q
                else:
                    acc_ref[which, part, :] += new_q
        dk_ref[at, :] = dk.astype(LOW)
        dv_ref[at, :] = dv.astype(LOW)

    block(spans[0], [(0, True, True), (1, False, True)])
    block(spans[1], [(1, True, False)])

    @pl.loop(0, far_ref[0])
    def _(i):
        at = pl.ds(pl.multiple_of(near + i * size, size), size)
        block(at, [(0, False, False), (1, False, False)])

    @pl.loop(far_ref[0], 2)
    def _(i):
        at = pl.ds(pl.multiple_of(near + i * size, size), size)
        dk_ref[at, :] = jnp.zeros((size, LANES), LOW)
        dv_ref[at, :] = jnp.zeros((size, LANES), LOW)

    for which in range(2):
        dq_ref[spans[which], :] = (jnp.transpose(acc_ref[which]) * SCALE).astype(LOW)


def attend_back(far, query, keyval, grad, out, lse, which, earlier):
    near, width = query.shape
    total = keyval.shape[0]
    pairs = width // LANES
    rows = pl.BlockSpec((near, LANES), lambda p, s: (0, which))
    every = pl.BlockSpec((total, LANES), lambda p, s: (0, which))
    return pl.pallas_call(
        attend_back_kernel,
        out_shape=(
            jax.ShapeDtypeStruct((near, width), LOW),
            jax.ShapeDtypeStruct((total, width), LOW),
            jax.ShapeDtypeStruct((total, width), LOW),
        ),
        grid_spec=pltpu.PrefetchScalarGridSpec(
            num_scalar_prefetch=1,
            grid=(1,),
            in_specs=[
                rows,
                every,
                pl.BlockSpec((total, LANES), lambda p, s: (0, which + pairs)),
                rows,
                rows,
                pl.BlockSpec((1, 8, near), lambda p, s: (which, 0, 0)),
            ]
            + [pl.BlockSpec(memory_space=pl.ANY)] * len(earlier),
            out_specs=(rows, every, every),
            scratch_shapes=[pltpu.VMEM((2, LANES, near // 2), FULL)],
        ),
        input_output_aliases={7 + i: i for i in range(len(earlier))},
        compiler_params=pltpu.CompilerParams(vmem_limit_bytes=VMEM),
        cost_estimate=SHORT,
        name="attend_back",
    )(far, query, keyval, keyval, grad, out, lse, *earlier)


def grads_kernel(n_ref, dq_ref, dk_ref, dv_ref, mine_ref, other_ref, a_ref, b_ref):
    near, width = dq_ref.shape
    turned = jnp.transpose(n_ref[...])
    low = jnp.concatenate(
        [
            dot(turned[:, :near], dq_ref[...]).astype(LOW),
            dot(turned, dk_ref[...]).astype(LOW),
            dot(turned, dv_ref[...]).astype(LOW),
            (mine_ref[...].astype(FULL) + other_ref[...].astype(FULL)).astype(LOW),
        ],
        1,
    )
    cut = a_ref.shape[1]
    a_ref[...] = low[:, :cut]
    b_ref[...] = low[:, cut:]


def qkv_grads(normed, dq, dk, dv, mine, other):
    width = normed.shape[1]
    cut = 2 * dq.shape[1]
    return pl.pallas_call(
        grads_kernel,
        out_shape=(
            jax.ShapeDtypeStruct((width, cut), LOW),
            jax.ShapeDtypeStruct((width, cut), LOW),
        ),
        compiler_params=pltpu.CompilerParams(vmem_limit_bytes=VMEM),
        cost_estimate=SHORT,
        name="qkv_grads",
    )(normed, dq, dk, dv, mine, other)


CURVE = 0.7978845608028654
CUBIC = 0.044715


def feed_kernel(
    shard_rows, core_ref, n_ref, g_ref, fc_ref, fb_ref, *refs
):
    pieces, refs = refs[:-8], refs[-8:]
    out_ref, back_ref, fc_send_ref, fc_keep_ref, pr_send_ref, pr_keep_ref = refs[:6]
    fb_grad_ref, turned_ref = refs[6:]

    step = pl.program_id(0)
    half = g_ref.shape[1] // 2

    @pl.when(step == 0)
    def _():
        turned_ref[...] = jnp.transpose(n_ref[...])

    if len(pieces) == 1:
        proj = pieces[0][...]
    else:
        size = shard_rows
        wide = [piece[...].astype(FULL) for piece in pieces]
        proj = jnp.concatenate(
            [
                piece[at : at + size]
                for at in range(0, wide[0].shape[0], size)
                for piece in wide
            ],
            0,
        ).astype(LOW)
    grad = g_ref[...]
    hidden = dot(n_ref[...], fc_ref[...]) + fb_ref[...]
    square = hidden * hidden
    bend = jnp.tanh(hidden * (CURVE + (CURVE * CUBIC) * square))
    gate = 0.5 * (1.0 + bend)
    active = (hidden * gate).astype(LOW)
    slope = gate + hidden * (0.5 * (1.0 - bend * bend)) * (
        CURVE + (3 * CURVE * CUBIC) * square
    )
    grad_hidden = (dot_nt(grad, proj) * slope).astype(LOW)
    out, back = dot(active, proj), dot_nt(grad_hidden, fc_ref[...])

    @pl.when(step == 0)
    def _():
        out_ref[...] = out
        back_ref[...] = back

    @pl.when(step > 0)
    def _():
        out_ref[...] += out
        back_ref[...] += back

    fb_grad_ref[...] = jnp.sum(grad_hidden.astype(FULL), 0, keepdims=True)
    fc_grad = dot(turned_ref[...], grad_hidden).astype(LOW)
    others = pl.num_programs(0) // 2

    @pl.when(step < others)
    def _():
        fc_send_ref[...] = fc_grad

    @pl.when(step >= others)
    def _():
        fc_keep_ref[...] = fc_grad

    pr_grad = dot_tn(active, grad)
    low, high = pr_grad[:, :half].astype(LOW), pr_grad[:, half:].astype(LOW)
    first = core_ref[0] == 0
    pr_send_ref[...] = jnp.where(first, high, low)
    pr_keep_ref[...] = jnp.where(first, low, high)


def feed(core, normed, grad, late, fc_bias, proj, shard_rows):
    rows, width = normed.shape
    hidden = fc_bias.shape[1]
    chunk = width
    blocks = hidden // chunk
    steps = blocks // 2

    def block(i, s):
        return jnp.where(i < steps, (1 - s[0]) * steps + i, s[0] * steps + i - steps)

    whole = pl.BlockSpec((rows, width), lambda i, s: (0, 0))
    if proj is None:
        pieces = [late] * blocks
        piece_specs = [
            pl.BlockSpec((width // blocks, width), lambda i, s, at=at: (block(i, s), at))
            for at in range(blocks + 1, 2 * blocks + 1)
        ]
    else:
        pieces = [proj]
        piece_specs = [pl.BlockSpec((chunk, width), lambda i, s: (block(i, s), 0))]
    half = pl.BlockSpec((chunk, width // 2), lambda i, s: (block(i, s), 0))
    return pl.pallas_call(
        functools.partial(feed_kernel, shard_rows),
        out_shape=(
            jax.ShapeDtypeStruct((rows, width), FULL),
            jax.ShapeDtypeStruct((rows, width), FULL),
            jax.ShapeDtypeStruct((width, hidden // 2), LOW),
            jax.ShapeDtypeStruct((width, hidden // 2), LOW),
            jax.ShapeDtypeStruct((hidden, width // 2), LOW),
            jax.ShapeDtypeStruct((hidden, width // 2), LOW),
            jax.ShapeDtypeStruct((1, hidden), FULL),
        ),
        grid_spec=pltpu.PrefetchScalarGridSpec(
            num_scalar_prefetch=1,
            grid=(blocks,),
            in_specs=[
                whole,
                whole,
                pl.BlockSpec((width, chunk), lambda i, s: (0, block(i, s))),
                pl.BlockSpec((1, chunk), lambda i, s: (0, block(i, s))),
                *piece_specs,
            ],
            out_specs=(
                whole,
                whole,
                pl.BlockSpec((width, chunk), lambda i, s: (0, jnp.minimum(i, steps - 1))),
                pl.BlockSpec((width, chunk), lambda i, s: (0, jnp.maximum(i - steps, 0))),
                half,
                half,
                pl.BlockSpec((1, chunk), lambda i, s: (0, block(i, s))),
            ),
            scratch_shapes=[pltpu.VMEM((width, rows), LOW)],
        ),
        compiler_params=pltpu.CompilerParams(vmem_limit_bytes=VMEM),
        cost_estimate=SHORT,
        name="feed",
    )(core, normed, grad, late, fc_bias, *pieces)


def turn_kernel(
    core_ref, n_ref, hat_ref, root_ref, gain_ref, g_ref, att_ref, w_ref,
    middle_ref, keep_ref, send_ref, w_keep_ref, w_send_ref, gain_grad_ref, shift_ref, bias_ref,
):
    half = keep_ref.shape[1]
    grad, hat = n_ref[...], hat_ref[...]
    gain_grad_ref[...] = jnp.sum(grad * hat, 0, keepdims=True)
    shift_ref[...] = jnp.sum(grad, 0, keepdims=True)
    middle = g_ref[...].astype(FULL) + normalize_back(grad, gain_ref[...], hat, root_ref[...])
    middle_ref[...] = middle
    low = middle.astype(LOW)
    bias_ref[...] = jnp.sum(low.astype(FULL), 0, keepdims=True)
    first = core_ref[0] == 0
    for whole, kept, sent in (
        (dot_nt(low, w_ref[...]), keep_ref, send_ref),
        (dot(jnp.transpose(att_ref[...]), low), w_keep_ref, w_send_ref),
    ):
        whole = whole.astype(LOW)
        one, two = whole[:, :half], whole[:, half:]
        kept[...] = jnp.where(first, one, two)
        sent[...] = jnp.where(first, two, one)


def turn(core, grad, hat, root, gain, grad_valid, attended, late, at):
    rows, width = grad.shape
    shape = jax.ShapeDtypeStruct

    def spec(*dims):
        return pl.BlockSpec(dims, lambda i, s: (0, 0))

    whole = spec(rows, width)
    return pl.pallas_call(
        turn_kernel,
        grid_spec=pltpu.PrefetchScalarGridSpec(
            num_scalar_prefetch=1,
            grid=(1,),
            in_specs=[
                whole,
                whole,
                spec(rows, 1),
                spec(1, width),
                whole,
                whole,
                pl.BlockSpec((width, width), lambda i, s: (0, at)),
            ],
            out_specs=(
                whole,
                spec(rows, width // 2),
                spec(rows, width // 2),
                spec(width, width // 2),
                spec(width, width // 2),
                spec(1, width),
                spec(1, width),
                spec(1, width),
            ),
        ),
        out_shape=(
            shape((rows, width), FULL),
            shape((rows, width // 2), LOW),
            shape((rows, width // 2), LOW),
            shape((width, width // 2), LOW),
            shape((width, width // 2), LOW),
            shape((1, width), FULL),
            shape((1, width), FULL),
            shape((1, width), FULL),
        ),
        compiler_params=pltpu.CompilerParams(vmem_limit_bytes=VMEM),
        cost_estimate=SHORT,
        name="turn",
    )(core, grad, hat, root, gain, grad_valid, attended, late)


def norm_back_kernel(
    core_ref, dq_ref, dk_ref, dv_ref, wq_ref, wkv_ref, hat_ref,
    keep_ref, send_ref, gain_ref, shift_ref, q_sum_ref, v_sum_ref, part_ref,
):
    step = pl.program_id(0)
    half = dk_ref.shape[1]
    part_ref[...] = dot_nt(dk_ref[...], wkv_ref[:, :half]) + dot_nt(
        dv_ref[...], wkv_ref[:, half:]
    )

    @pl.when(step == 0)
    def _():
        for ref in (gain_ref, shift_ref, q_sum_ref, v_sum_ref):
            ref[...] = jnp.zeros_like(ref)

    @pl.when(lax.rem(step, 2) == 1)
    def _():
        part_ref[...] += dot_nt(dq_ref[...], wq_ref[...])
        q_sum_ref[...] += jnp.sum(dq_ref[...].astype(FULL), 0, keepdims=True)

    part = part_ref[...]
    v_sum_ref[...] += jnp.sum(dv_ref[...].astype(FULL), 0, keepdims=True)
    gain_ref[...] += jnp.sum(part * hat_ref[...], 0, keepdims=True)
    shift_ref[...] += jnp.sum(part, 0, keepdims=True)

    @pl.when(step < 2)
    def _():
        send_ref[0] = part.astype(LOW)

    @pl.when(step >= 2)
    def _():
        keep_ref[0] = part


def norm_back(core, dq, dk, dv, q_weight, keyval_weight, hat):
    quarter, half, width = dq.shape[0] // 2, dq.shape[1], hat.shape[1]

    def at(i, s):
        return jnp.where(i < 2, 1 - s[0], s[0])

    def block(i, s):
        return (jnp.where(lax.rem(i, 2) == 0, 2, 0) + at(i, s), 0)

    whole = lambda i, s: (0, 0)
    line, short = pl.BlockSpec((1, width), whole), pl.BlockSpec((1, half), whole)
    shape = jax.ShapeDtypeStruct
    return pl.pallas_call(
        norm_back_kernel,
        out_shape=(
            shape((2, quarter, width), FULL),
            shape((2, quarter, width), LOW),
            shape((1, width), FULL),
            shape((1, width), FULL),
            shape((1, half), FULL),
            shape((1, half), FULL),
        ),
        grid_spec=pltpu.PrefetchScalarGridSpec(
            num_scalar_prefetch=1,
            grid=(4,),
            in_specs=[
                pl.BlockSpec((quarter, half), lambda i, s: (at(i, s), 0)),
                pl.BlockSpec((quarter, half), block),
                pl.BlockSpec((quarter, half), block),
                pl.BlockSpec((width, half), whole),
                pl.BlockSpec((width, 2 * half), whole),
                pl.BlockSpec((quarter, width), block),
            ],
            out_specs=(
                pl.BlockSpec((1, quarter, width), lambda i, s: (jnp.maximum(i - 2, 0), 0, 0)),
                pl.BlockSpec((1, quarter, width), lambda i, s: (jnp.minimum(i, 1), 0, 0)),
                line,
                line,
                short,
                short,
            ),
            scratch_shapes=[pltpu.VMEM((quarter, width), FULL)],
        ),
        compiler_params=pltpu.CompilerParams(vmem_limit_bytes=VMEM),
        cost_estimate=SHORT,
        name="norm_back",
    )(core, dq, dk, dv, q_weight, keyval_weight, hat)


def normalize(values):
    center = values - jnp.mean(values, -1, keepdims=True)
    spread = jnp.mean(center * center, -1, keepdims=True)
    root = lax.rsqrt(spread + 1e-05)
    return center * root, root


def normalize_back(grad, gain, hat, root):
    scaled = grad * gain
    return root * (
        scaled
        - jnp.mean(scaled, -1, keepdims=True)
        - hat * jnp.mean(scaled * hat, -1, keepdims=True)
    )


def shards(
    tokens,
    lengths,
    thought_pos,
    cotangent,
    qkv_weight,
    out_weight,
    fc_weight,
    proj_weight,
    qv_bias,
    out_bias,
    fc_bias,
    proj_bias,
    first_gain,
    first_shift,
    second_gain,
    second_shift,
):
    _, quarter, width = tokens.shape
    half = width // 2
    near = 2 * quarter
    slice_rows = qkv_weight.shape[0]
    count = 1 << flat_bits()
    plans = orders()
    core, second = bit_of(0), bit_of(1)
    far = (2 * second).astype(jnp.int32).reshape(1)

    high, hidden_width = proj_weight.shape[0], fc_weight.shape[1]
    blocks = hidden_width // width
    proj_rows = [proj_weight[i * slice_rows : (i + 1) * slice_rows] for i in range(blocks)]
    late = lax.all_gather(
        jnp.concatenate([fc_weight, out_weight, *proj_rows], 1), ALL, axis=0, tiled=True
    )

    mine = tokens[0]
    flips = [(i, i ^ 2) for i in range(count) if not i & 2]
    before = lax.ppermute(mine, ALL, flips)
    near_tokens = pair(mine, swap(mine, 0), core, 0).reshape(near, width)

    third = slice_rows * 4
    small = jnp.zeros((slice_rows, LANES), LOW)
    rows_of = (
        jnp.concatenate([qv_bias, out_bias, first_gain]),
        fc_bias,
        jnp.concatenate([proj_bias, first_shift, second_gain, second_shift]),
    )
    small = small.at[:3, :third].set(jnp.stack(rows_of))
    split = qkv_weight.reshape(slice_rows, 3, 2, half)
    keep = lax.dynamic_index_in_dim(split, core, 2, keepdims=False).reshape(slice_rows, 3 * half)
    send = lax.dynamic_index_in_dim(split, 1 - core, 2, keepdims=False).reshape(
        slice_rows, 3 * half
    )
    keep, send = jnp.concatenate([keep, small], 1), jnp.concatenate([send, small], 1)
    chip = pair(keep, swap(send, 0), core, 0).reshape(2 * slice_rows, 3 * half + LANES)
    block = gather_common(chip, (before,))
    far_tokens = pair(before, swap(before, 0), core, 0).reshape(near, width)
    slots = jnp.arange(near, dtype=jnp.int32)
    thoughts = thought_pos[0]

    def is_thought(at_slots):
        return jnp.any(thoughts[None, :] == at_slots[:, None], 1, keepdims=True)

    thought_near = is_thought(second * near + slots)
    thought_far = is_thought(slots)
    shifted_near = jnp.concatenate([far_tokens[-1:], near_tokens[:-1]], 0)
    shifted_far = jnp.concatenate([far_tokens[:1], far_tokens[:-1]], 0)
    inputs_near = jnp.where(thought_near, shifted_near, near_tokens)
    inputs_far = jnp.where(thought_far, shifted_far, far_tokens)
    inputs_all = jnp.concatenate([inputs_near, inputs_far], 0)
    hat_all, root_all = normalize(inputs_all.astype(FULL))
    own = core * quarter
    inputs = lax.dynamic_slice_in_dim(inputs_near, own, quarter, 0).astype(FULL)

    parts = [
        jnp.concatenate([block[:, :, :half], block[:, :, 3 * half :]], 2),
        block[:, :, half : 3 * half],
    ]
    first_parts = gather_step(parts, plans, 0)

    parts = gather_step(first_parts, plans, 1, (hat_all, root_all))
    q_weight = parts[0][:, :, :half].reshape(width, half)
    keyval_weight = parts[1].reshape(width, 2 * half)
    small = parts[0].reshape(count, slice_rows, half + LANES)[:, :3, half : half + third]
    small = small.astype(FULL)
    at = slice_rows

    def vector(row, first, size):
        return small[:, row, first : first + size].reshape(1, count * size)

    qv_full = vector(0, 0, 2 * at)
    out_bias_full, gain_one = vector(0, 2 * at, at), vector(0, 3 * at, at)
    fc_bias_full = vector(1, 0, 4 * at)
    proj_bias_full, shift_one = vector(2, 0, at), vector(2, at, at)
    gain_two, shift_two = vector(2, 2 * at, at), vector(2, 3 * at, at)

    normed = (hat_all * gain_one + shift_one).astype(LOW)
    own_half = core * half
    q_bias = lax.dynamic_slice_in_dim(qv_full[:, :width], own_half, half, 1)
    v_bias = lax.dynamic_slice_in_dim(qv_full[:, width:], own_half, half, 1)
    query = (dot(normed[:near], q_weight) + q_bias).astype(LOW)
    keyval_bias = jnp.concatenate([jnp.zeros((1, half), FULL), v_bias], 1)
    keyval = (dot(normed, keyval_weight) + keyval_bias).astype(LOW)

    def rows_to_core(array):
        return (
            lax.dynamic_slice_in_dim(array, own, quarter, 0),
            lax.dynamic_slice_in_dim(array, quarter - own, quarter, 0),
        )

    pairs = half // LANES
    heads = ()
    for which in range(pairs):
        heads = attend(far, query, keyval, quarter, which, heads)
    heads, logsums = heads
    keep, send = rows_to_core(heads)
    attended = beside(keep, swap(send, 0), core)
    late = after(late, attended)
    out_full = late[:, hidden_width : hidden_width + width]

    middle = inputs + dot(attended, out_full) + out_bias_full
    hat_two, root_two = normalize(middle)
    normed_two = (hat_two * gain_two + shift_two).astype(LOW)
    my_slots = (2 * second + core) * quarter + jnp.arange(quarter, dtype=jnp.int32)
    valid = (my_slots < lengths[0])[:, None]
    grad_valid = jnp.where(valid, cotangent[0], jnp.zeros_like(cotangent[0]))
    core_at = core.astype(jnp.int32).reshape(1)
    proj_full = None
    if slice_rows % 8:
        proj_full = late[:, hidden_width + width :].reshape(count, slice_rows, blocks, width)
        proj_full = proj_full.transpose(0, 2, 1, 3).reshape(hidden_width, width)
    fed, grad_normed_two, fc_send, fc_keep, proj_send, proj_keep, fc_bias_grad = feed(
        core_at, normed_two, grad_valid, late, fc_bias_full, proj_full, slice_rows
    )
    fc_bias_grad = fc_bias_grad[0]
    output = middle + fed + proj_bias_full
    mixed = jnp.where(valid, output, 0.0).astype(LOW)[None]
    proj_bias_grad = jnp.sum(grad_valid.astype(FULL), 0)

    chips = count // 2
    fc_shape = (chips, 2 * slice_rows, hidden_width // 2)
    proj_shape = (chips, 2 * high, half)
    fc_pair = [fc_keep.reshape(fc_shape), swap(fc_send, 0).reshape(fc_shape)]
    proj_pair = [proj_keep.reshape(proj_shape), swap(proj_send, 0).reshape(proj_shape)]

    turned = turn(
        core_at, grad_normed_two, hat_two, root_two, gain_two, grad_valid, attended, late, blocks
    )
    grad_middle, keep, send, out_kept, out_send = turned[:5]
    second_gain_grad, second_shift_grad, out_bias_grad = (value[0] for value in turned[5:])
    grad_heads = pair(keep, swap(send, 0), core, 0).reshape(near, half)
    early = [start_sum(fc_pair, 0, hidden_width // 2), start_sum(proj_pair, 0, half)]
    ready = prepare(early, plans, 0)
    out_got = swap(after(out_send, *sends(ready)), 0)

    grads = ()
    now = after(grad_heads, *sends(ready))
    for which in range(pairs):
        if which == 2:
            ready = prepare(exchange(ready, grads), plans, 1)
            now = after(grad_heads, *sends(ready))
        grads = attend_back(
            far, query, keyval, now, heads, logsums, which, grads
        )
    out_got = after(out_got, *grads)
    ready = prepare(exchange(ready, grads), plans, 2)
    grad_query, grad_key, grad_value = after(grads, *sends(ready))

    last = [
        start_sum([value.reshape(chips, 2 * slice_rows, -1)], 0, value.shape[1])
        for value in qkv_grads(normed, grad_query, grad_key, grad_value, out_kept, out_got)
    ]
    last_ready = prepare(last, plans, 0)

    part, part_send, first_gain_grad, first_shift_grad, q_sum, v_sum = norm_back(
        core_at,
        after(grad_query, *sends(last_ready)),
        grad_key,
        grad_value,
        q_weight,
        keyval_weight,
        hat_all,
    )
    got = swap(part_send, 0)
    last = exchange(last_ready, (part_send,))
    last_ready = prepare(last, plans, 1)
    ready = prepare(exchange(ready, sends(last_ready)), plans, 3)
    got = after(got, *sends(last_ready), *sends(ready))
    far_sum = (part[0] + got[0].astype(FULL)).astype(LOW)
    back = lax.ppermute(far_sum, ALL, [(b, a) for a, b in flips])
    first_gain_grad, first_shift_grad, q_sum, v_sum = (
        value[0] for value in (first_gain_grad, first_shift_grad, q_sum, v_sum)
    )
    zero = jnp.zeros((half,), FULL)
    low_core = core == 0
    qv_bias_grad = jnp.concatenate(
        [
            jnp.where(low_core, q_sum, zero),
            jnp.where(low_core, zero, q_sum),
            jnp.where(low_core, v_sum, zero),
            jnp.where(low_core, zero, v_sum),
        ]
    )
    grads = (
        qv_bias_grad,
        out_bias_grad,
        fc_bias_grad,
        proj_bias_grad,
        first_gain_grad,
        first_shift_grad,
        second_gain_grad,
        second_shift_grad,
    )
    sizes = [grad.shape[0] // count for grad in grads]
    packed = jnp.concatenate([g.reshape(count, s) for g, s in zip(grads, sizes)], 1)
    share = jnp.sum(lax.all_to_all(packed, ALL, 0, 0, tiled=True), 0, keepdims=True)
    for step in range(2, flat_bits() - 1):
        last = exchange(last_ready, (far_sum,))
        last_ready = prepare(last, plans, step)
    last = exchange(last_ready)
    for step in range(4, flat_bits() - 1):
        ready = prepare(exchange(ready), plans, step)
    fc_total, proj_total = (value.total()[0] for value in exchange(ready, (far_sum,)))
    fc_weight_grad = jnp.concatenate(finish(fc_total, slice_rows), 1)

    proj_weight_grad = jnp.concatenate(finish(proj_total, high), 1)
    sides = finish(jnp.concatenate([value.total()[0] for value in last], 1), slice_rows)
    kinds = [
        jnp.concatenate([side[:, i * half : (i + 1) * half] for side in sides], 1)
        for i in range(4)
    ]
    qkv_weight_grad, out_weight_grad = jnp.concatenate(kinds[:3], 1), kinds[3]

    grad_normed = part[1] + got[1].astype(FULL) + back.astype(FULL)
    hat = lax.dynamic_slice_in_dim(hat_all, own, quarter, 0)
    root = lax.dynamic_slice_in_dim(root_all, own, quarter, 0)
    grad_inputs = grad_middle + normalize_back(grad_normed, gain_one, hat, root)
    thought = lax.dynamic_slice_in_dim(thought_near, own, quarter, 0)
    kept = jnp.where(thought, 0.0, grad_inputs)
    moved = jnp.where(thought, grad_inputs, 0.0)
    ctx = lax.axis_size("ctx")
    following = lax.ppermute(moved[:1], "ctx", [(i, i - 1) for i in range(1, ctx)])
    tokens_grad = (kept + jnp.concatenate([moved[1:], following], 0))[None]

    shares, at = [], 0
    for size in sizes:
        shares.append(share[0, at : at + size])
        at += size
    return (
        mixed,
        tokens_grad,
        qkv_weight_grad,
        out_weight_grad,
        fc_weight_grad,
        proj_weight_grad,
        *shares,
    )


def solution(mesh):
    rows, matrix, vector = P("dp", "ctx", None), P(ALL, None), P(ALL)
    return jax.shard_map(
        shards,
        mesh=mesh,
        in_specs=(rows, P("dp"), P("dp", None), rows) + (matrix,) * 4 + (vector,) * 8,
        out_specs=(rows, rows) + (matrix,) * 4 + (vector,) * 8,
        check_vma=False,
    )
```

```python
import functools

import jax
import jax.numpy as jnp
from jax import lax
from jax.experimental import pallas as pl
from jax.experimental.pallas import tpu as pltpu
from jax.sharding import PartitionSpec as P

ALL = ("dp", "ctx")
LOW = jnp.bfloat16
FULL = jnp.float32
HEAD = 64
LANES = 128
SCALE = 0.125
VMEM = 48 << 20
SHORT = pl.CostEstimate(flops=1 << 29, bytes_accessed=1 << 19, transcendentals=0)


def flat_bits():
    return (lax.axis_size("dp") * lax.axis_size("ctx")).bit_length() - 1


def flat_index():
    return lax.axis_index("dp") * lax.axis_size("ctx") + lax.axis_index("ctx")


def bit_of(bit):
    return (flat_index() >> bit) & 1


def swap(value, bit):
    count = 1 << flat_bits()
    return lax.ppermute(value, ALL, [(i, i ^ (1 << bit)) for i in range(count)])


def after(value, *others):
    return lax.optimization_barrier((value, others))[0]


def pair(mine, other, place, axis):
    shape = mine.shape[:axis] + (2,) + mine.shape[axis:]
    whole = jnp.broadcast_to(jnp.expand_dims(mine, axis), shape)
    return lax.dynamic_update_slice_in_dim(whole, jnp.expand_dims(other, axis), 1 - place, axis)


def beside(mine, other, place):
    low = place == 0
    return jnp.concatenate([jnp.where(low, mine, other), jnp.where(low, other, mine)], -1)


def orders():
    rest = list(range(3, flat_bits()))
    return [1, 2] + rest, [2, 1] + rest


def grow(block, done, bit, wait=()):
    other = after(swap(block, bit), *wait)
    rows, cols = block.shape[1:]
    high = 1 << len([b for b in done if b > bit])
    low = 1 << len([b for b in done if b < bit])
    whole = pair(
        block.reshape(high, low, rows, cols), other.reshape(high, low, rows, cols), bit_of(bit), 1
    )
    return whole.reshape(high * 2 * low, rows, cols)


def gather_common(block):
    block, done = block[None], []
    for bit in reversed(range(3, flat_bits())):
        block = grow(block, done, bit)
        done.append(bit)
    return block


def gather_step(parts, plans, step, wait=()):
    out = []
    for part, order in zip(parts, plans):
        plan = list(reversed(order))
        at = flat_bits() - 3 + step
        out.append(grow(part, plan[:at], plan[at], wait))
    return out


class Sum:
    def __init__(self, addends, left, kind=LOW):
        self.addends = addends
        self.left = left
        self.kind = kind

    def total(self, bit=None, place=None):
        result = None
        for value, bits, (start, size) in self.addends:
            rows = value.shape[1]
            dims, begin, width = [], [], []
            for b in sorted(bits, reverse=True):
                dims.append(2)
                if b == bit:
                    begin.append(place)
                    width.append(1)
                elif b in self.left:
                    begin.append(0)
                    width.append(2)
                else:
                    begin.append(bit_of(b))
                    width.append(1)
            view = value.reshape(*dims, rows, value.shape[2])
            piece = lax.dynamic_slice(view, (*begin, 0, start), (*width, rows, size))
            piece = piece.reshape(-1, rows, size).astype(FULL)
            result = piece if result is None else result + piece
        return result

    def prepare(self, bit):
        send = self.total(bit, 1 - bit_of(bit)).astype(self.kind)
        return send, Sum(self.addends, [b for b in self.left if b != bit], self.kind), bit


def prepare(sums, plans, step):
    return [value.prepare(plan[step]) for value, plan in zip(sums, plans)]


def sends(prepared):
    return [send for send, _, _ in prepared]


def exchange(prepared, wait=()):
    gots = [swap(send, bit) for send, _, bit in prepared]
    gots = after(gots, *wait) if wait else gots
    return [
        Sum(keep.addends + [(got, keep.left, (0, got.shape[2]))], keep.left, keep.kind)
        for got, (_, keep, _) in zip(gots, prepared)
    ]


def start_sum(arrays, start, size, kind=LOW):
    links = list(range(1, flat_bits()))
    return Sum([(value, links, (start, size)) for value in arrays], links, kind)


def finish(total, rows):
    core = bit_of(0)
    mine = lax.dynamic_slice_in_dim(total, core * rows, rows, 0)
    other = swap(lax.dynamic_slice_in_dim(total, (1 - core) * rows, rows, 0), 0)
    return jnp.where(core == 0, mine, other), jnp.where(core == 0, other, mine)


def dot(a, b):
    return lax.dot_general(a, b, (((1,), (0,)), ((), ())), preferred_element_type=FULL)


def dot_nt(a, b):
    return lax.dot_general(a, b, (((1,), (1,)), ((), ())), preferred_element_type=FULL)


def dot_tn(a, b):
    return lax.dot_general(a, b, (((0,), (0,)), ((), ())), preferred_element_type=FULL)


def head_lanes(value, head):
    lane = lax.broadcasted_iota(jnp.int32, (1, LANES), 1)
    return jnp.where(lane // HEAD == head, value, jnp.zeros_like(value))


def causal(rows, cols):
    shape = (rows, cols)
    return lax.broadcasted_iota(jnp.int32, shape, 0) <= lax.broadcasted_iota(jnp.int32, shape, 1)


def attend_kernel(far_ref, q_ref, k_ref, v_ref, out_ref, lse_ref, top_ref, acc_ref):
    near = q_ref.shape[0]
    size = near // 2
    query = q_ref[...] * jnp.asarray(SCALE, LOW)

    def step(keys, queries, masked, first):
        key = k_ref[keys, :]
        value = jnp.transpose(v_ref[keys, :])
        for head in range(2):
            ones = jnp.ones((16, key.shape[0]), LOW)
            wide = jnp.concatenate([value[head * HEAD : (head + 1) * HEAD], ones], 0)
            scores = dot_nt(key, head_lanes(query[queries], head))
            if masked:
                scores = jnp.where(causal(*scores.shape), scores, -1e9)
            row = slice(head, head + 1)
            top = jnp.max(scores, 0, keepdims=True)
            if first:
                acc_ref[head, :, queries] = dot(wide, jnp.exp(scores - top).astype(LOW))
            else:
                old = top_ref[row, queries]
                top = jnp.maximum(old, top)
                acc_ref[head, :, queries] = acc_ref[head, :, queries] * jnp.exp(old - top) + dot(
                    wide, jnp.exp(scores - top).astype(LOW)
                )
            top_ref[row, queries] = top

    step(slice(0, size), slice(0, near), True, True)
    step(slice(size, near), slice(size, near), True, False)

    @pl.when(far_ref[0] > 0)
    def _():
        step(slice(near, 2 * near), slice(0, near), False, False)

    outs = []
    for head in range(2):
        total = acc_ref[head, HEAD : HEAD + 1, :]
        outs.append(acc_ref[head, :HEAD, :] / total)
        lse_ref[0, head : head + 1, :] = top_ref[head : head + 1, :] + jnp.log(total)
    out_ref[...] = jnp.transpose(jnp.concatenate(outs, 0)).astype(LOW)


def attend(far, query, keyval):
    near, width = query.shape
    total = keyval.shape[0]
    pairs = width // LANES
    rows = pl.BlockSpec((near, LANES), lambda p, s: (0, p))
    return pl.pallas_call(
        attend_kernel,
        out_shape=(
            jax.ShapeDtypeStruct((near, width), LOW),
            jax.ShapeDtypeStruct((pairs, 8, near), FULL),
        ),
        grid_spec=pltpu.PrefetchScalarGridSpec(
            num_scalar_prefetch=1,
            grid=(pairs,),
            in_specs=[
                rows,
                pl.BlockSpec((total, LANES), lambda p, s: (0, p)),
                pl.BlockSpec((total, LANES), lambda p, s: (0, p + pairs)),
            ],
            out_specs=(rows, pl.BlockSpec((1, 8, near), lambda p, s: (p, 0, 0))),
            scratch_shapes=[
                pltpu.VMEM((8, near), FULL),
                pltpu.VMEM((2, HEAD + 16, near), FULL),
            ],
        ),
        compiler_params=pltpu.CompilerParams(vmem_limit_bytes=VMEM),
        cost_estimate=SHORT,
        name="attend",
    )(far, query, keyval, keyval)


def attend_back_kernel(
    far_ref, q_ref, k_ref, v_ref, grad_ref, out_ref, lse_ref, *refs
):
    dq_ref, dk_ref, dv_ref, acc_ref = refs[-4:]
    near = q_ref.shape[0]
    size = near // 2
    spans = (slice(0, size), slice(size, near))
    query = q_ref[...] * jnp.asarray(SCALE, LOW)
    grad = grad_ref[...]
    product = jnp.transpose(grad.astype(FULL) * out_ref[...].astype(FULL))
    delta = [
        jnp.sum(product[head * HEAD : (head + 1) * HEAD], 0, keepdims=True) for head in range(2)
    ]

    def block(at, work):
        key, value = k_ref[at, :], v_ref[at, :]
        turned = jnp.transpose(key)
        dk = dv = None
        for which, masked, first in work:
            span = spans[which]
            for head in range(2):
                part = slice(head * HEAD, (head + 1) * HEAD)
                q_head = head_lanes(query[span], head)
                g_head = head_lanes(grad[span], head)
                probs = jnp.exp(dot_nt(key, q_head) - lse_ref[0, head : head + 1, span])
                if masked:
                    probs = jnp.where(causal(size, size), probs, 0.0)
                moved = probs * (dot_nt(value, g_head) - delta[head][:, span])
                moved, probs = moved.astype(LOW), probs.astype(LOW)
                new_k, new_v = dot(moved, q_head), dot(probs, g_head)
                dk = new_k if dk is None else dk + new_k
                dv = new_v if dv is None else dv + new_v
                new_q = dot(turned[part], moved)
                if first:
                    acc_ref[which, part, :] = new_q
                else:
                    acc_ref[which, part, :] += new_q
        dk_ref[at, :] = dk.astype(LOW)
        dv_ref[at, :] = dv.astype(LOW)

    block(spans[0], [(0, True, True), (1, False, True)])
    block(spans[1], [(1, True, False)])

    @pl.loop(0, far_ref[0])
    def _(i):
        at = pl.ds(pl.multiple_of(near + i * size, size), size)
        block(at, [(0, False, False), (1, False, False)])

    @pl.loop(far_ref[0], 2)
    def _(i):
        at = pl.ds(pl.multiple_of(near + i * size, size), size)
        dk_ref[at, :] = jnp.zeros((size, LANES), LOW)
        dv_ref[at, :] = jnp.zeros((size, LANES), LOW)

    for which in range(2):
        dq_ref[spans[which], :] = (jnp.transpose(acc_ref[which]) * SCALE).astype(LOW)


def attend_back(far, query, keyval, grad, out, lse, which, earlier):
    near, width = query.shape
    total = keyval.shape[0]
    pairs = width // LANES
    rows = pl.BlockSpec((near, LANES), lambda p, s: (0, which))
    every = pl.BlockSpec((total, LANES), lambda p, s: (0, which))
    return pl.pallas_call(
        attend_back_kernel,
        out_shape=(
            jax.ShapeDtypeStruct((near, width), LOW),
            jax.ShapeDtypeStruct((total, width), LOW),
            jax.ShapeDtypeStruct((total, width), LOW),
        ),
        grid_spec=pltpu.PrefetchScalarGridSpec(
            num_scalar_prefetch=1,
            grid=(1,),
            in_specs=[
                rows,
                every,
                pl.BlockSpec((total, LANES), lambda p, s: (0, which + pairs)),
                rows,
                rows,
                pl.BlockSpec((1, 8, near), lambda p, s: (which, 0, 0)),
            ]
            + [pl.BlockSpec(memory_space=pl.ANY)] * len(earlier),
            out_specs=(rows, every, every),
            scratch_shapes=[pltpu.VMEM((2, LANES, near // 2), FULL)],
        ),
        input_output_aliases={7 + i: i for i in range(len(earlier))},
        compiler_params=pltpu.CompilerParams(vmem_limit_bytes=VMEM),
        cost_estimate=SHORT,
        name="attend_back",
    )(far, query, keyval, keyval, grad, out, lse, *earlier)


def grads_kernel(n_ref, dq_ref, dk_ref, dv_ref, mine_ref, other_ref, a_ref, b_ref):
    near, width = dq_ref.shape
    turned = jnp.transpose(n_ref[...])
    low = jnp.concatenate(
        [
            dot(turned[:, :near], dq_ref[...]).astype(LOW),
            dot(turned, dk_ref[...]).astype(LOW),
            dot(turned, dv_ref[...]).astype(LOW),
            (mine_ref[...].astype(FULL) + other_ref[...].astype(FULL)).astype(LOW),
        ],
        1,
    )
    cut = a_ref.shape[1]
    a_ref[...] = low[:, :cut]
    b_ref[...] = low[:, cut:]


def qkv_grads(normed, dq, dk, dv, mine, other):
    width = normed.shape[1]
    cut = 2 * dq.shape[1]
    return pl.pallas_call(
        grads_kernel,
        out_shape=(
            jax.ShapeDtypeStruct((width, cut), LOW),
            jax.ShapeDtypeStruct((width, cut), LOW),
        ),
        compiler_params=pltpu.CompilerParams(vmem_limit_bytes=VMEM),
        cost_estimate=SHORT,
        name="qkv_grads",
    )(normed, dq, dk, dv, mine, other)


CURVE = 0.7978845608028654
CUBIC = 0.044715


def feed_kernel(
    shard_rows, core_ref, n_ref, g_ref, fc_ref, fb_ref, *refs
):
    pieces, refs = refs[:-8], refs[-8:]
    out_ref, back_ref, fc_send_ref, fc_keep_ref, pr_send_ref, pr_keep_ref = refs[:6]
    fb_grad_ref, turned_ref = refs[6:]

    step = pl.program_id(0)
    half = g_ref.shape[1] // 2

    @pl.when(step == 0)
    def _():
        turned_ref[...] = jnp.transpose(n_ref[...])

    if len(pieces) == 1:
        proj = pieces[0][...]
    else:
        size = shard_rows
        wide = [piece[...].astype(FULL) for piece in pieces]
        proj = jnp.concatenate(
            [
                piece[at : at + size]
                for at in range(0, wide[0].shape[0], size)
                for piece in wide
            ],
            0,
        ).astype(LOW)
    grad = g_ref[...]
    hidden = dot(n_ref[...], fc_ref[...]) + fb_ref[...]
    square = hidden * hidden
    bend = jnp.tanh(hidden * (CURVE + (CURVE * CUBIC) * square))
    gate = 0.5 * (1.0 + bend)
    active = (hidden * gate).astype(LOW)
    slope = gate + hidden * (0.5 * (1.0 - bend * bend)) * (
        CURVE + (3 * CURVE * CUBIC) * square
    )
    grad_hidden = (dot_nt(grad, proj) * slope).astype(LOW)
    out, back = dot(active, proj), dot_nt(grad_hidden, fc_ref[...])

    @pl.when(step == 0)
    def _():
        out_ref[...] = out
        back_ref[...] = back

    @pl.when(step > 0)
    def _():
        out_ref[...] += out
        back_ref[...] += back

    fb_grad_ref[...] = jnp.sum(grad_hidden.astype(FULL), 0, keepdims=True)
    fc_grad = dot(turned_ref[...], grad_hidden).astype(LOW)
    others = pl.num_programs(0) // 2

    @pl.when(step < others)
    def _():
        fc_send_ref[...] = fc_grad

    @pl.when(step >= others)
    def _():
        fc_keep_ref[...] = fc_grad

    pr_grad = dot_tn(active, grad)
    low, high = pr_grad[:, :half].astype(LOW), pr_grad[:, half:].astype(LOW)
    first = core_ref[0] == 0
    pr_send_ref[...] = jnp.where(first, high, low)
    pr_keep_ref[...] = jnp.where(first, low, high)


def beside_kernel(fc_ref, proj_ref, last_ref, out_ref):
    rows, at = fc_ref.shape
    width = proj_ref.shape[1]
    out_ref[:, :at] = fc_ref[...]
    out_ref[:, 2 * at :] = last_ref[...]
    wide = proj_ref[...].astype(FULL)
    for i in range(wide.shape[0] // rows):
        out_ref[:, at + i * width : at + (i + 1) * width] = wide[i * rows : (i + 1) * rows].astype(
            LOW
        )


def beside_rows(fc, proj, last):
    rows = fc.shape[0]
    if rows % 8:
        return jnp.concatenate(
            [fc] + [proj[i : i + rows] for i in range(0, proj.shape[0], rows)] + [last], 1
        )
    vmem = pl.BlockSpec(memory_space=pltpu.VMEM)
    return pl.pallas_call(
        beside_kernel,
        in_specs=[vmem, vmem, vmem],
        out_shape=jax.ShapeDtypeStruct((rows, 2 * fc.shape[1] + last.shape[1]), LOW),
        cost_estimate=SHORT,
        name="beside",
    )(fc, proj, last)


def feed(core, normed, grad, late, fc_bias, proj, shard_rows):
    rows, width = normed.shape
    hidden = fc_bias.shape[1]
    chunk = width
    blocks = hidden // chunk
    steps = blocks // 2

    def block(i, s):
        return jnp.where(i < steps, (1 - s[0]) * steps + i, s[0] * steps + i - steps)

    whole = pl.BlockSpec((rows, width), lambda i, s: (0, 0))
    if proj is None:
        pieces = [late] * blocks
        piece_specs = [
            pl.BlockSpec((width // blocks, width), lambda i, s, at=at: (block(i, s), at))
            for at in range(blocks, 2 * blocks)
        ]
    else:
        pieces = [proj]
        piece_specs = [pl.BlockSpec((chunk, width), lambda i, s: (block(i, s), 0))]
    half = pl.BlockSpec((chunk, width // 2), lambda i, s: (block(i, s), 0))
    return pl.pallas_call(
        functools.partial(feed_kernel, shard_rows),
        out_shape=(
            jax.ShapeDtypeStruct((rows, width), FULL),
            jax.ShapeDtypeStruct((rows, width), FULL),
            jax.ShapeDtypeStruct((width, hidden // 2), LOW),
            jax.ShapeDtypeStruct((width, hidden // 2), LOW),
            jax.ShapeDtypeStruct((hidden, width // 2), LOW),
            jax.ShapeDtypeStruct((hidden, width // 2), LOW),
            jax.ShapeDtypeStruct((1, hidden), FULL),
        ),
        grid_spec=pltpu.PrefetchScalarGridSpec(
            num_scalar_prefetch=1,
            grid=(blocks,),
            in_specs=[
                whole,
                whole,
                pl.BlockSpec((width, chunk), lambda i, s: (0, block(i, s))),
                pl.BlockSpec((1, chunk), lambda i, s: (0, block(i, s))),
                *piece_specs,
            ],
            out_specs=(
                whole,
                whole,
                pl.BlockSpec((width, chunk), lambda i, s: (0, jnp.minimum(i, steps - 1))),
                pl.BlockSpec((width, chunk), lambda i, s: (0, jnp.maximum(i - steps, 0))),
                half,
                half,
                pl.BlockSpec((1, chunk), lambda i, s: (0, block(i, s))),
            ),
            scratch_shapes=[pltpu.VMEM((width, rows), LOW)],
        ),
        compiler_params=pltpu.CompilerParams(vmem_limit_bytes=VMEM),
        cost_estimate=SHORT,
        name="feed",
    )(core, normed, grad, late, fc_bias, *pieces)


def turn_kernel(
    core_ref, n_ref, hat_ref, root_ref, gain_ref, g_ref, att_ref, w_ref,
    middle_ref, keep_ref, send_ref, w_keep_ref, w_send_ref, gain_grad_ref, shift_ref, bias_ref, last_ref,
):
    half = keep_ref.shape[1]
    grad, hat = n_ref[...], hat_ref[...]
    gain_grad_ref[...] = jnp.sum(grad * hat, 0, keepdims=True)
    shift_ref[...] = jnp.sum(grad, 0, keepdims=True)
    middle = g_ref[...].astype(FULL) + normalize_back(grad, gain_ref[...], hat, root_ref[...])
    middle_ref[...] = middle
    last_ref[...] = jnp.sum(g_ref[...].astype(FULL), 0, keepdims=True)
    low = middle.astype(LOW)
    bias_ref[...] = jnp.sum(low.astype(FULL), 0, keepdims=True)
    first = core_ref[0] == 0
    for whole, kept, sent in (
        (dot_nt(low, w_ref[...]), keep_ref, send_ref),
        (dot(jnp.transpose(att_ref[...]), low), w_keep_ref, w_send_ref),
    ):
        whole = whole.astype(LOW)
        one, two = whole[:, :half], whole[:, half:]
        kept[...] = jnp.where(first, one, two)
        sent[...] = jnp.where(first, two, one)


def turn(core, grad, hat, root, gain, grad_valid, attended, late, at):
    rows, width = grad.shape
    shape = jax.ShapeDtypeStruct

    def spec(*dims):
        return pl.BlockSpec(dims, lambda i, s: (0, 0))

    whole = spec(rows, width)
    return pl.pallas_call(
        turn_kernel,
        grid_spec=pltpu.PrefetchScalarGridSpec(
            num_scalar_prefetch=1,
            grid=(1,),
            in_specs=[
                whole,
                whole,
                spec(rows, 1),
                spec(1, width),
                whole,
                whole,
                pl.BlockSpec((width, width), lambda i, s: (0, at)),
            ],
            out_specs=(
                whole,
                spec(rows, width // 2),
                spec(rows, width // 2),
                spec(width, width // 2),
                spec(width, width // 2),
                spec(1, width),
                spec(1, width),
                spec(1, width),
                spec(1, width),
            ),
        ),
        out_shape=(
            shape((rows, width), FULL),
            shape((rows, width // 2), LOW),
            shape((rows, width // 2), LOW),
            shape((width, width // 2), LOW),
            shape((width, width // 2), LOW),
            shape((1, width), FULL),
            shape((1, width), FULL),
            shape((1, width), FULL),
            shape((1, width), FULL),
        ),
        compiler_params=pltpu.CompilerParams(vmem_limit_bytes=VMEM),
        cost_estimate=SHORT,
        name="turn",
    )(core, grad, hat, root, gain, grad_valid, attended, late)


def norm_back_kernel(
    core_ref, dq_ref, dk_ref, dv_ref, wq_ref, wkv_ref, hat_ref,
    keep_ref, send_ref, gain_ref, shift_ref, q_sum_ref, v_sum_ref, part_ref,
):
    step = pl.program_id(0)
    half = dk_ref.shape[1]
    part_ref[...] = dot_nt(dk_ref[...], wkv_ref[:, :half]) + dot_nt(
        dv_ref[...], wkv_ref[:, half:]
    )

    @pl.when(step == 0)
    def _():
        for ref in (gain_ref, shift_ref, q_sum_ref, v_sum_ref):
            ref[...] = jnp.zeros_like(ref)

    @pl.when(lax.rem(step, 2) == 1)
    def _():
        part_ref[...] += dot_nt(dq_ref[...], wq_ref[...])
        q_sum_ref[...] += jnp.sum(dq_ref[...].astype(FULL), 0, keepdims=True)

    part = part_ref[...]
    v_sum_ref[...] += jnp.sum(dv_ref[...].astype(FULL), 0, keepdims=True)
    gain_ref[...] += jnp.sum(part * hat_ref[...], 0, keepdims=True)
    shift_ref[...] += jnp.sum(part, 0, keepdims=True)

    @pl.when(step < 2)
    def _():
        send_ref[0] = part.astype(LOW)

    @pl.when(step >= 2)
    def _():
        keep_ref[0] = part


def norm_back(core, dq, dk, dv, q_weight, keyval_weight, hat):
    quarter, half, width = dq.shape[0] // 2, dq.shape[1], hat.shape[1]

    def at(i, s):
        return jnp.where(i < 2, 1 - s[0], s[0])

    def block(i, s):
        return (jnp.where(lax.rem(i, 2) == 0, 2, 0) + at(i, s), 0)

    whole = lambda i, s: (0, 0)
    line, short = pl.BlockSpec((1, width), whole), pl.BlockSpec((1, half), whole)
    shape = jax.ShapeDtypeStruct
    return pl.pallas_call(
        norm_back_kernel,
        out_shape=(
            shape((2, quarter, width), FULL),
            shape((2, quarter, width), LOW),
            shape((1, width), FULL),
            shape((1, width), FULL),
            shape((1, half), FULL),
            shape((1, half), FULL),
        ),
        grid_spec=pltpu.PrefetchScalarGridSpec(
            num_scalar_prefetch=1,
            grid=(4,),
            in_specs=[
                pl.BlockSpec((quarter, half), lambda i, s: (at(i, s), 0)),
                pl.BlockSpec((quarter, half), block),
                pl.BlockSpec((quarter, half), block),
                pl.BlockSpec((width, half), whole),
                pl.BlockSpec((width, 2 * half), whole),
                pl.BlockSpec((quarter, width), block),
            ],
            out_specs=(
                pl.BlockSpec((1, quarter, width), lambda i, s: (jnp.maximum(i - 2, 0), 0, 0)),
                pl.BlockSpec((1, quarter, width), lambda i, s: (jnp.minimum(i, 1), 0, 0)),
                line,
                line,
                short,
                short,
            ),
            scratch_shapes=[pltpu.VMEM((quarter, width), FULL)],
        ),
        compiler_params=pltpu.CompilerParams(vmem_limit_bytes=VMEM),
        cost_estimate=SHORT,
        name="norm_back",
    )(core, dq, dk, dv, q_weight, keyval_weight, hat)


def pack_kernel(slots, core_ref, *refs):
    out_ref = refs[-1]
    count = out_ref.shape[0]
    spreads = {}
    for slot, parts in enumerate(slots):
        total = None
        for ref_at, size, shift, by_core in parts:
            line = refs[ref_at][...]
            length = line.shape[1]
            shape = (count, length)
            device = lax.broadcasted_iota(jnp.int32, shape, 0) - (shift + by_core * core_ref[0])
            lane = lax.broadcasted_iota(jnp.int32, shape, 1) - device * size
            piece = jnp.where((lane >= 0) & (lane < size), line, 0.0)
            if (length, size) not in spreads:
                shape = (length, LANES)
                at = lax.broadcasted_iota(jnp.int32, shape, 0).astype(FULL)
                at = at - size * jnp.floor((at + 0.5) * (1.0 / size))
                lane = lax.broadcasted_iota(jnp.int32, shape, 1).astype(FULL)
                spreads[length, size] = jnp.where(at == lane, 1.0, 0.0)
            piece = lax.dot_general(
                piece,
                spreads[length, size],
                (((1,), (0,)), ((), ())),
                precision=lax.Precision.HIGHEST,
                preferred_element_type=FULL,
            )
            total = piece if total is None else total + piece
        out_ref[:, slot * LANES : (slot + 1) * LANES] = total


def pack(core, count, q_sum, v_sum, lines):
    size = 4 * q_sum.shape[1] // count
    slots = [[(0, size, 0, count // 4), (1, size, count // 2, count // 4)]]
    slots += [[(2 + i, line.shape[1] // count, 0, 0)] for i, line in enumerate(lines)]
    vmem = pl.BlockSpec(memory_space=pltpu.VMEM)
    packed = pl.pallas_call(
        functools.partial(pack_kernel, slots),
        in_specs=[pl.BlockSpec(memory_space=pltpu.SMEM)] + [vmem] * (2 + len(lines)),
        out_shape=jax.ShapeDtypeStruct((count, len(slots) * LANES), FULL),
        compiler_params=pltpu.CompilerParams(vmem_limit_bytes=VMEM),
        cost_estimate=SHORT,
        name="pack",
    )(core, q_sum, v_sum, *lines)
    return packed, [slot[0][1] for slot in slots]


def normalize(values):
    center = values - jnp.mean(values, -1, keepdims=True)
    spread = jnp.mean(center * center, -1, keepdims=True)
    root = lax.rsqrt(spread + 1e-05)
    return center * root, root


def normalize_back(grad, gain, hat, root):
    scaled = grad * gain
    return root * (
        scaled
        - jnp.mean(scaled, -1, keepdims=True)
        - hat * jnp.mean(scaled * hat, -1, keepdims=True)
    )


def shards(
    tokens,
    lengths,
    thought_pos,
    cotangent,
    qkv_weight,
    out_weight,
    fc_weight,
    proj_weight,
    qv_bias,
    out_bias,
    fc_bias,
    proj_bias,
    first_gain,
    first_shift,
    second_gain,
    second_shift,
):
    _, quarter, width = tokens.shape
    half = width // 2
    near = 2 * quarter
    slice_rows = qkv_weight.shape[0]
    count = 1 << flat_bits()
    plans = orders()
    core, second = bit_of(0), bit_of(1)
    far = (2 * second).astype(jnp.int32).reshape(1)

    high, hidden_width = proj_weight.shape[0], fc_weight.shape[1]
    blocks = hidden_width // width
    late = lax.all_gather(
        beside_rows(fc_weight, proj_weight, out_weight), ALL, axis=0, tiled=True
    )

    mine = tokens[0]
    flips = [(i, i ^ 2) for i in range(count) if not i & 2]
    before = lax.ppermute(mine, ALL, flips)
    near_tokens = pair(mine, swap(mine, 0), core, 0).reshape(near, width)

    third = slice_rows * 4
    small = jnp.zeros((slice_rows, LANES), LOW)
    rows_of = (
        jnp.concatenate([qv_bias, out_bias, first_gain]),
        fc_bias,
        jnp.concatenate([proj_bias, first_shift, second_gain, second_shift]),
    )
    small = small.at[:3, :third].set(jnp.stack(rows_of))
    split = qkv_weight.reshape(slice_rows, 3, 2, half)
    keep = lax.dynamic_index_in_dim(split, core, 2, keepdims=False).reshape(slice_rows, 3 * half)
    send = lax.dynamic_index_in_dim(split, 1 - core, 2, keepdims=False).reshape(
        slice_rows, 3 * half
    )
    keep, send = jnp.concatenate([keep, small], 1), jnp.concatenate([send, small], 1)
    chip = pair(keep, swap(send, 0), core, 0).reshape(2 * slice_rows, 3 * half + LANES)
    block = gather_common(chip)
    far_tokens = pair(before, swap(before, 0), core, 0).reshape(near, width)
    slots = jnp.arange(near, dtype=jnp.int32)
    thoughts = thought_pos[0]

    def is_thought(at_slots):
        return jnp.any(thoughts[None, :] == at_slots[:, None], 1, keepdims=True)

    thought_near = is_thought(second * near + slots)
    thought_far = is_thought(slots)
    shifted_near = jnp.concatenate([far_tokens[-1:], near_tokens[:-1]], 0)
    shifted_far = jnp.concatenate([far_tokens[:1], far_tokens[:-1]], 0)
    inputs_near = jnp.where(thought_near, shifted_near, near_tokens)
    inputs_far = jnp.where(thought_far, shifted_far, far_tokens)
    inputs_all = jnp.concatenate([inputs_near, inputs_far], 0)
    hat_all, root_all = normalize(inputs_all.astype(FULL))
    own = core * quarter
    inputs = lax.dynamic_slice_in_dim(inputs_near, own, quarter, 0).astype(FULL)

    parts = [
        jnp.concatenate([block[:, :, :half], block[:, :, 3 * half :]], 2),
        block[:, :, half : 3 * half],
    ]
    first_parts = gather_step(parts, plans, 0, (before,))

    parts = gather_step(first_parts, plans, 1, (hat_all, root_all))
    q_weight = parts[0][:, :, :half].reshape(width, half)
    keyval_weight = parts[1].reshape(width, 2 * half)
    small = parts[0].reshape(count, slice_rows, half + LANES)[:, :3, half : half + third]
    small = small.astype(FULL)
    at = slice_rows

    def vector(row, first, size):
        return small[:, row, first : first + size].reshape(1, count * size)

    qv_full = vector(0, 0, 2 * at)
    out_bias_full, gain_one = vector(0, 2 * at, at), vector(0, 3 * at, at)
    fc_bias_full = vector(1, 0, 4 * at)
    proj_bias_full, shift_one = vector(2, 0, at), vector(2, at, at)
    gain_two, shift_two = vector(2, 2 * at, at), vector(2, 3 * at, at)

    normed = (hat_all * gain_one + shift_one).astype(LOW)
    own_half = core * half
    q_bias = lax.dynamic_slice_in_dim(qv_full[:, :width], own_half, half, 1)
    v_bias = lax.dynamic_slice_in_dim(qv_full[:, width:], own_half, half, 1)
    query = (dot(normed[:near], q_weight) + q_bias).astype(LOW)
    keyval_bias = jnp.concatenate([jnp.zeros((1, half), FULL), v_bias], 1)
    keyval = (dot(normed, keyval_weight) + keyval_bias).astype(LOW)

    def rows_to_core(array):
        return (
            lax.dynamic_slice_in_dim(array, own, quarter, 0),
            lax.dynamic_slice_in_dim(array, quarter - own, quarter, 0),
        )

    pairs = half // LANES
    heads, logsums = attend(far, query, keyval)
    keep, send = rows_to_core(heads)
    attended = beside(keep, swap(send, 0), core)
    late = after(late, attended)
    out_full = late[:, 2 * hidden_width :]
    middle = inputs + dot(attended, out_full) + out_bias_full
    hat_two, root_two = normalize(middle)
    normed_two = (hat_two * gain_two + shift_two).astype(LOW)
    my_slots = (2 * second + core) * quarter + jnp.arange(quarter, dtype=jnp.int32)
    valid = (my_slots < lengths[0])[:, None]
    grad_valid = jnp.where(valid, cotangent[0], jnp.zeros_like(cotangent[0]))
    core_at = core.astype(jnp.int32).reshape(1)
    proj_full = None
    if slice_rows % 8:
        proj_full = late[:, hidden_width : 2 * hidden_width].reshape(count, slice_rows, blocks, width)
        proj_full = proj_full.transpose(0, 2, 1, 3).reshape(hidden_width, width)
    fed, grad_normed_two, fc_send, fc_keep, proj_send, proj_keep, fc_bias_grad = feed(
        core_at, normed_two, grad_valid, late, fc_bias_full, proj_full, slice_rows
    )
    output = middle + fed + proj_bias_full
    mixed = jnp.where(valid, output, 0.0).astype(LOW)[None]

    chips = count // 2
    fc_shape = (chips, 2 * slice_rows, hidden_width // 2)
    proj_shape = (chips, 2 * high, half)
    fc_got, proj_got = swap(fc_send, 0), swap(proj_send, 0)

    turned = turn(
        core_at, grad_normed_two, hat_two, root_two, gain_two, grad_valid, attended, late, 2 * blocks
    )
    grad_middle, keep, send, out_kept, out_send = turned[:5]
    second_gain_grad, second_shift_grad, out_bias_grad, proj_bias_grad = turned[5:]
    grad_heads = pair(keep, swap(send, 0), core, 0).reshape(near, half)
    fc_got, proj_got = after((fc_got, proj_got), grad_middle)
    fc_pair = [fc_keep.reshape(fc_shape), fc_got.reshape(fc_shape)]
    proj_pair = [proj_keep.reshape(proj_shape), proj_got.reshape(proj_shape)]
    early = [start_sum(fc_pair, 0, hidden_width // 2), start_sum(proj_pair, 0, half)]
    ready = prepare(early, plans, 0)
    out_got = swap(after(out_send, *sends(ready)), 0)

    grads = ()
    now = after(grad_heads, *sends(ready))
    for which in range(pairs):
        if which == 2:
            ready = prepare(exchange(ready, grads), plans, 1)
            now = after(grad_heads, *sends(ready))
        grads = attend_back(
            far, query, keyval, now, heads, logsums, which, grads
        )
    out_got = after(out_got, *grads)
    ready = prepare(exchange(ready, grads), plans, 2)
    grad_query, grad_key, grad_value = after(grads, *sends(ready))

    last = [
        start_sum([value.reshape(chips, 2 * slice_rows, -1)], 0, value.shape[1])
        for value in qkv_grads(normed, grad_query, grad_key, grad_value, out_kept, out_got)
    ]
    last_ready = prepare(last, plans, 0)

    part, part_send, first_gain_grad, first_shift_grad, q_sum, v_sum = norm_back(
        core_at,
        after(grad_query, *sends(last_ready)),
        grad_key,
        grad_value,
        q_weight,
        keyval_weight,
        hat_all,
    )
    got = swap(part_send, 0)
    both = exchange(last_ready + ready, (part_send,))
    last_ready = prepare(both[:2], plans, 1)
    ready = prepare(both[2:], plans, 3)
    got = after(got, *sends(last_ready), *sends(ready))
    far_sum = (part[0] + got[0].astype(FULL)).astype(LOW)
    back = lax.ppermute(far_sum, ALL, [(b, a) for a, b in flips])
    packed, sizes = pack(
        core_at,
        count,
        q_sum,
        v_sum,
        (
            out_bias_grad,
            fc_bias_grad,
            proj_bias_grad,
            first_gain_grad,
            first_shift_grad,
            second_gain_grad,
            second_shift_grad,
        ),
    )
    packed = after(packed, far_sum)
    share = jnp.sum(lax.all_to_all(packed, ALL, 0, 0, tiled=True), 0, keepdims=True)
    for step in range(2, flat_bits() - 1):
        last = exchange(last_ready, (far_sum,))
        last_ready = prepare(last, plans, step)
    last = exchange(last_ready)
    for step in range(4, flat_bits() - 1):
        ready = prepare(exchange(ready), plans, step)
    fc_total, proj_total = (value.total()[0] for value in exchange(ready, (far_sum,)))
    fc_weight_grad = jnp.concatenate(finish(fc_total, slice_rows), 1)

    proj_weight_grad = jnp.concatenate(finish(proj_total, high), 1)
    sides = finish(jnp.concatenate([value.total()[0] for value in last], 1), slice_rows)
    kinds = [
        jnp.concatenate([side[:, i * half : (i + 1) * half] for side in sides], 1)
        for i in range(4)
    ]
    qkv_weight_grad, out_weight_grad = jnp.concatenate(kinds[:3], 1), kinds[3]

    grad_normed = part[1] + got[1].astype(FULL) + back.astype(FULL)
    hat = lax.dynamic_slice_in_dim(hat_all, own, quarter, 0)
    root = lax.dynamic_slice_in_dim(root_all, own, quarter, 0)
    grad_inputs = grad_middle + normalize_back(grad_normed, gain_one, hat, root)
    thought = lax.dynamic_slice_in_dim(thought_near, own, quarter, 0)
    kept = jnp.where(thought, 0.0, grad_inputs)
    moved = jnp.where(thought, grad_inputs, 0.0)
    ctx = lax.axis_size("ctx")
    following = lax.ppermute(moved[:1], "ctx", [(i, i - 1) for i in range(1, ctx)])
    tokens_grad = (kept + jnp.concatenate([moved[1:], following], 0))[None]

    shares = [share[0, i * LANES : i * LANES + size] for i, size in enumerate(sizes)]
    return (
        mixed,
        tokens_grad,
        qkv_weight_grad,
        out_weight_grad,
        fc_weight_grad,
        proj_weight_grad,
        *shares,
    )


def solution(mesh):
    rows, matrix, vector = P("dp", "ctx", None), P(ALL, None), P(ALL)
    return jax.shard_map(
        shards,
        mesh=mesh,
        in_specs=(rows, P("dp"), P("dp", None), rows) + (matrix,) * 4 + (vector,) * 8,
        out_specs=(rows, rows) + (matrix,) * 4 + (vector,) * 8,
        check_vma=False,
    )
```

```python
import functools

import jax
import jax.numpy as jnp
from jax import lax
from jax.experimental import pallas as pl
from jax.experimental.pallas import tpu as pltpu
from jax.sharding import PartitionSpec as P

ALL = ("dp", "ctx")
LOW = jnp.bfloat16
FULL = jnp.float32
HEAD = 64
LANES = 128
SCALE = 0.125
VMEM = 48 << 20
SHORT = pl.CostEstimate(flops=1 << 20, bytes_accessed=1 << 12, transcendentals=0)
LONG = pl.CostEstimate(flops=12 << 30, bytes_accessed=1 << 12, transcendentals=0)


def flat_bits():
    return (lax.axis_size("dp") * lax.axis_size("ctx")).bit_length() - 1


def flat_index():
    return lax.axis_index("dp") * lax.axis_size("ctx") + lax.axis_index("ctx")


def bit_of(bit):
    return (flat_index() >> bit) & 1


def swap(value, bit):
    count = 1 << flat_bits()
    return lax.ppermute(value, ALL, [(i, i ^ (1 << bit)) for i in range(count)])


def after(value, *others):
    return lax.optimization_barrier((value, others))[0]


def pair(mine, other, place, axis):
    shape = mine.shape[:axis] + (2,) + mine.shape[axis:]
    whole = jnp.broadcast_to(jnp.expand_dims(mine, axis), shape)
    return lax.dynamic_update_slice_in_dim(whole, jnp.expand_dims(other, axis), 1 - place, axis)


def beside(mine, other, place):
    low = place == 0
    return jnp.concatenate([jnp.where(low, mine, other), jnp.where(low, other, mine)], -1)


def orders():
    rest = list(range(3, flat_bits()))
    return [1, 2] + rest, [2, 1] + rest


def grow(block, done, bit, wait=()):
    other = after(swap(block, bit), *wait)
    rows, cols = block.shape[1:]
    high = 1 << len([b for b in done if b > bit])
    low = 1 << len([b for b in done if b < bit])
    whole = pair(
        block.reshape(high, low, rows, cols), other.reshape(high, low, rows, cols), bit_of(bit), 1
    )
    return whole.reshape(high * 2 * low, rows, cols)


def gather_common(block, wait=()):
    block, done = block[None], []
    for bit in reversed(range(3, flat_bits())):
        block = grow(block, done, bit, () if done else wait)
        done.append(bit)
    return block


def gather_step(parts, plans, step, wait=()):
    out = []
    for part, order in zip(parts, plans):
        plan = list(reversed(order))
        at = flat_bits() - 3 + step
        out.append(grow(part, plan[:at], plan[at], wait))
    return out


class Sum:
    def __init__(self, addends, left):
        self.addends = addends
        self.left = left


def group_of(bits, left, bit):
    order, rest = sorted(bits, reverse=True), sorted(left, reverse=True)

    def index(i, s):
        group = 0
        for b in order:
            here = (s[0] >> b) & 1
            if b == bit:
                here = 1 - here
            elif b in rest:
                here = (i >> (len(rest) - 1 - rest.index(b))) & 1
            group = 2 * group + here
        return (group, 0, 0)

    return index


def total_of(refs):
    total = refs[0][0].astype(FULL)
    for ref in refs[1:]:
        total = total + ref[0].astype(FULL)
    return total


def send_kernel(counts, at_ref, *refs):
    outs = refs[len(refs) - len(counts) :]
    for count, out_ref in zip(counts, outs):
        out_ref[0] = total_of(refs[:count]).astype(LOW)
        refs = refs[count:]


def specs_of(sums, bits):
    arrays, specs = [], []
    for value, bit in zip(sums, bits):
        left = [b for b in value.left if b != bit]
        for array, own in value.addends:
            arrays.append(array)
            specs.append(pl.BlockSpec((1, *array.shape[1:]), group_of(own, left, bit)))
    return arrays, specs


def prepare(sums, plans, step):
    bits = [plan[step] for plan in plans]
    arrays, specs = specs_of(sums, bits)
    groups = 1 << (len(sums[0].left) - 1)
    shapes = [value.addends[0][0].shape[1:] for value in sums]
    sent = pl.pallas_call(
        functools.partial(send_kernel, [len(value.addends) for value in sums]),
        out_shape=tuple(jax.ShapeDtypeStruct((groups, *shape), LOW) for shape in shapes),
        grid_spec=pltpu.PrefetchScalarGridSpec(
            num_scalar_prefetch=1,
            grid=(groups,),
            in_specs=specs,
            out_specs=tuple(pl.BlockSpec((1, *shape), lambda i, s: (i, 0, 0)) for shape in shapes),
        ),
        compiler_params=pltpu.CompilerParams(vmem_limit_bytes=VMEM),
        cost_estimate=LONG,
        name="send",
    )(flat_index().astype(jnp.int32).reshape(1), *arrays)
    return [
        (send, Sum(value.addends, [b for b in value.left if b != bit]), bit)
        for send, value, bit in zip(sent, sums, bits)
    ]


def sends(prepared):
    return [send for send, _, _ in prepared]


def exchange(prepared, wait=()):
    gots = [swap(send, bit) for send, _, bit in prepared]
    gots = after(gots, *wait) if wait else gots
    return [
        Sum(keep.addends + [(got, keep.left)], keep.left)
        for got, (_, keep, _) in zip(gots, prepared)
    ]


def start_sum(arrays):
    links = list(range(1, flat_bits()))
    return Sum([(value, links) for value in arrays], links)


def finish_kernel(counts, at_ref, *refs):
    mine_ref, send_ref = refs[-2:]
    rows = mine_ref.shape[0]
    first = (at_ref[0] & 1) == 0
    column = 0
    for count in counts:
        total = total_of(refs[:count])
        refs = refs[count:]
        half, cols = total.shape[0] // 2, total.shape[1]
        one, two = total[:half], total[half:]
        mine, other = jnp.where(first, one, two), jnp.where(first, two, one)
        for at in range(0, half, rows):
            mine_ref[:, column : column + cols] = mine[at : at + rows]
            send_ref[:, column : column + cols] = other[at : at + rows]
            column += cols


def settle_kernel(at_ref, mine_ref, other_ref, fc_ref, proj_ref, qkv_ref, out_ref):
    first = (at_ref[0] & 1) == 0
    rows = mine_ref.shape[0]
    half = out_ref.shape[1] // 2
    start = 0

    def both(size):
        mine, other = mine_ref[:, start : start + size], other_ref[:, start : start + size]
        return jnp.where(first, mine, other), jnp.where(first, other, mine)

    size = fc_ref.shape[1] // 2
    fc_ref[:, :size], fc_ref[:, size:] = both(size)
    start += size
    for at in range(0, proj_ref.shape[0], rows):
        proj_ref[at : at + rows, :half], proj_ref[at : at + rows, half:] = both(half)
        start += half
    for kind in range(3):
        at = 2 * kind * half
        qkv_ref[:, at : at + half], qkv_ref[:, at + half : at + 2 * half] = both(half)
        start += half
    out_ref[:, :half], out_ref[:, half:] = both(half)


def finish(sums, rows, widths):
    at = flat_index().astype(jnp.int32).reshape(1)
    arrays, specs = specs_of(sums, [None] * len(sums))
    total = sum(
        value.addends[0][0].shape[1] // (2 * rows) * value.addends[0][0].shape[2]
        for value in sums
    )
    shape = jax.ShapeDtypeStruct
    whole = pl.BlockSpec((rows, total), lambda i, s: (0, 0))
    mine, send = pl.pallas_call(
        functools.partial(finish_kernel, [len(value.addends) for value in sums]),
        out_shape=(shape((rows, total), FULL),) * 2,
        grid_spec=pltpu.PrefetchScalarGridSpec(
            num_scalar_prefetch=1, grid=(1,), in_specs=specs, out_specs=(whole, whole)
        ),
        compiler_params=pltpu.CompilerParams(vmem_limit_bytes=VMEM),
        cost_estimate=SHORT,
        name="finish",
    )(at, *arrays)
    return pl.pallas_call(
        settle_kernel,
        out_shape=tuple(shape(size, FULL) for size in widths),
        grid_spec=pltpu.PrefetchScalarGridSpec(
            num_scalar_prefetch=1,
            grid=(1,),
            in_specs=[whole, whole],
            out_specs=tuple(pl.BlockSpec(size, lambda i, s: (0, 0)) for size in widths),
        ),
        compiler_params=pltpu.CompilerParams(vmem_limit_bytes=VMEM),
        cost_estimate=SHORT,
        name="settle",
    )(at, mine, swap(send, 0))


def dot(a, b):
    return lax.dot_general(a, b, (((1,), (0,)), ((), ())), preferred_element_type=FULL)


def dot_nt(a, b):
    return lax.dot_general(a, b, (((1,), (1,)), ((), ())), preferred_element_type=FULL)


def dot_tn(a, b):
    return lax.dot_general(a, b, (((0,), (0,)), ((), ())), preferred_element_type=FULL)


def head_lanes(value, head):
    lane = lax.broadcasted_iota(jnp.int32, (1, LANES), 1)
    return jnp.where(lane // HEAD == head, value, jnp.zeros_like(value))


def causal(rows, cols):
    shape = (rows, cols)
    return lax.broadcasted_iota(jnp.int32, shape, 0) <= lax.broadcasted_iota(jnp.int32, shape, 1)


def attend_kernel(far_ref, q_ref, k_ref, v_ref, out_ref, lse_ref, top_ref, acc_ref):
    near = q_ref.shape[0]
    size = near // 2
    query = q_ref[...] * jnp.asarray(SCALE, LOW)

    def step(keys, queries, masked, first):
        key = k_ref[keys, :]
        value = jnp.transpose(v_ref[keys, :])
        for head in range(2):
            ones = jnp.ones((16, key.shape[0]), LOW)
            wide = jnp.concatenate([value[head * HEAD : (head + 1) * HEAD], ones], 0)
            scores = dot_nt(key, head_lanes(query[queries], head))
            if masked:
                scores = jnp.where(causal(*scores.shape), scores, -1e9)
            row = slice(head, head + 1)
            top = jnp.max(scores, 0, keepdims=True)
            if first:
                acc_ref[head, :, queries] = dot(wide, jnp.exp(scores - top).astype(LOW))
            else:
                old = top_ref[row, queries]
                top = jnp.maximum(old, top)
                acc_ref[head, :, queries] = acc_ref[head, :, queries] * jnp.exp(old - top) + dot(
                    wide, jnp.exp(scores - top).astype(LOW)
                )
            top_ref[row, queries] = top

    step(slice(0, size), slice(0, near), True, True)
    step(slice(size, near), slice(size, near), True, False)

    @pl.when(far_ref[0] > 0)
    def _():
        step(slice(near, 2 * near), slice(0, near), False, False)

    outs = []
    for head in range(2):
        total = acc_ref[head, HEAD : HEAD + 1, :]
        outs.append(acc_ref[head, :HEAD, :] / total)
        lse_ref[0, head : head + 1, :] = top_ref[head : head + 1, :] + jnp.log(total)
    out_ref[...] = jnp.transpose(jnp.concatenate(outs, 0)).astype(LOW)


def attend(far, query, keyval):
    near, width = query.shape
    total = keyval.shape[0]
    pairs = width // LANES
    rows = pl.BlockSpec((near, LANES), lambda p, s: (0, p))
    return pl.pallas_call(
        attend_kernel,
        out_shape=(
            jax.ShapeDtypeStruct((near, width), LOW),
            jax.ShapeDtypeStruct((pairs, 8, near), FULL),
        ),
        grid_spec=pltpu.PrefetchScalarGridSpec(
            num_scalar_prefetch=1,
            grid=(pairs,),
            in_specs=[
                rows,
                pl.BlockSpec((total, LANES), lambda p, s: (0, p)),
                pl.BlockSpec((total, LANES), lambda p, s: (0, p + pairs)),
            ],
            out_specs=(rows, pl.BlockSpec((1, 8, near), lambda p, s: (p, 0, 0))),
            scratch_shapes=[
                pltpu.VMEM((8, near), FULL),
                pltpu.VMEM((2, HEAD + 16, near), FULL),
            ],
        ),
        compiler_params=pltpu.CompilerParams(vmem_limit_bytes=VMEM),
        cost_estimate=SHORT,
        name="attend",
    )(far, query, keyval, keyval)


def attend_back_kernel(
    far_ref, q_ref, k_ref, v_ref, grad_ref, out_ref, lse_ref, *refs
):
    dq_ref, dk_ref, dv_ref, acc_ref = refs[-4:]
    near = q_ref.shape[0]
    size = near // 2
    spans = (slice(0, size), slice(size, near))
    query = q_ref[...] * jnp.asarray(SCALE, LOW)
    grad = grad_ref[...]
    product = jnp.transpose(grad.astype(FULL) * out_ref[...].astype(FULL))
    delta = [
        jnp.sum(product[head * HEAD : (head + 1) * HEAD], 0, keepdims=True) for head in range(2)
    ]

    def block(at, work):
        key, value = k_ref[at, :], v_ref[at, :]
        turned = jnp.transpose(key)
        dk = dv = None
        for which, masked, first in work:
            span = spans[which]
            for head in range(2):
                part = slice(head * HEAD, (head + 1) * HEAD)
                q_head = head_lanes(query[span], head)
                g_head = head_lanes(grad[span], head)
                probs = jnp.exp(dot_nt(key, q_head) - lse_ref[0, head : head + 1, span])
                if masked:
                    probs = jnp.where(causal(size, size), probs, 0.0)
                moved = probs * (dot_nt(value, g_head) - delta[head][:, span])
                moved, probs = moved.astype(LOW), probs.astype(LOW)
                new_k, new_v = dot(moved, q_head), dot(probs, g_head)
                dk = new_k if dk is None else dk + new_k
                dv = new_v if dv is None else dv + new_v
                new_q = dot(turned[part], moved)
                if first:
                    acc_ref[which, part, :] = new_q
                else:
                    acc_ref[which, part, :] += new_q
        dk_ref[at, :] = dk.astype(LOW)
        dv_ref[at, :] = dv.astype(LOW)

    block(spans[0], [(0, True, True), (1, False, True)])
    block(spans[1], [(1, True, False)])

    @pl.loop(0, far_ref[0])
    def _(i):
        at = pl.ds(pl.multiple_of(near + i * size, size), size)
        block(at, [(0, False, False), (1, False, False)])

    @pl.loop(far_ref[0], 2)
    def _(i):
        at = pl.ds(pl.multiple_of(near + i * size, size), size)
        dk_ref[at, :] = jnp.zeros((size, LANES), LOW)
        dv_ref[at, :] = jnp.zeros((size, LANES), LOW)

    for which in range(2):
        dq_ref[spans[which], :] = (jnp.transpose(acc_ref[which]) * SCALE).astype(LOW)


def attend_back(far, query, keyval, grad, out, lse, which, earlier):
    near, width = query.shape
    total = keyval.shape[0]
    pairs = width // LANES
    rows = pl.BlockSpec((near, LANES), lambda p, s: (0, which))
    every = pl.BlockSpec((total, LANES), lambda p, s: (0, which))
    return pl.pallas_call(
        attend_back_kernel,
        out_shape=(
            jax.ShapeDtypeStruct((near, width), LOW),
            jax.ShapeDtypeStruct((total, width), LOW),
            jax.ShapeDtypeStruct((total, width), LOW),
        ),
        grid_spec=pltpu.PrefetchScalarGridSpec(
            num_scalar_prefetch=1,
            grid=(1,),
            in_specs=[
                rows,
                every,
                pl.BlockSpec((total, LANES), lambda p, s: (0, which + pairs)),
                rows,
                rows,
                pl.BlockSpec((1, 8, near), lambda p, s: (which, 0, 0)),
            ]
            + [pl.BlockSpec(memory_space=pl.ANY)] * len(earlier),
            out_specs=(rows, every, every),
            scratch_shapes=[pltpu.VMEM((2, LANES, near // 2), FULL)],
        ),
        input_output_aliases={7 + i: i for i in range(len(earlier))},
        compiler_params=pltpu.CompilerParams(vmem_limit_bytes=VMEM),
        cost_estimate=SHORT,
        name="attend_back",
    )(far, query, keyval, keyval, grad, out, lse, *earlier)


def grads_kernel(n_ref, dq_ref, dk_ref, dv_ref, mine_ref, other_ref, a_ref, b_ref):
    near, width = dq_ref.shape
    turned = jnp.transpose(n_ref[...])
    low = jnp.concatenate(
        [
            dot(turned[:, :near], dq_ref[...]).astype(LOW),
            dot(turned, dk_ref[...]).astype(LOW),
            dot(turned, dv_ref[...]).astype(LOW),
            (mine_ref[...].astype(FULL) + other_ref[...].astype(FULL)).astype(LOW),
        ],
        1,
    )
    cut = a_ref.shape[1]
    a_ref[...] = low[:, :cut]
    b_ref[...] = low[:, cut:]


def qkv_grads(normed, dq, dk, dv, mine, other):
    width = normed.shape[1]
    cut = 2 * dq.shape[1]
    return pl.pallas_call(
        grads_kernel,
        out_shape=(
            jax.ShapeDtypeStruct((width, cut), LOW),
            jax.ShapeDtypeStruct((width, cut), LOW),
        ),
        compiler_params=pltpu.CompilerParams(vmem_limit_bytes=VMEM),
        cost_estimate=SHORT,
        name="qkv_grads",
    )(normed, dq, dk, dv, mine, other)


CURVE = 0.7978845608028654
CUBIC = 0.044715


def feed_kernel(
    shard_rows, core_ref, n_ref, g_ref, fc_ref, fb_ref, *refs
):
    pieces, refs = refs[:-8], refs[-8:]
    out_ref, back_ref, fc_send_ref, fc_keep_ref, pr_send_ref, pr_keep_ref = refs[:6]
    fb_grad_ref, turned_ref = refs[6:]

    step = pl.program_id(0)
    half = g_ref.shape[1] // 2

    @pl.when(step == 0)
    def _():
        turned_ref[...] = jnp.transpose(n_ref[...])

    if len(pieces) == 1:
        proj = pieces[0][...]
    else:
        size = shard_rows
        wide = [piece[...].astype(FULL) for piece in pieces]
        proj = jnp.concatenate(
            [
                piece[at : at + size]
                for at in range(0, wide[0].shape[0], size)
                for piece in wide
            ],
            0,
        ).astype(LOW)
    grad = g_ref[...]
    hidden = dot(n_ref[...], fc_ref[...]) + fb_ref[...]
    square = hidden * hidden
    bend = jnp.tanh(hidden * (CURVE + (CURVE * CUBIC) * square))
    gate = 0.5 * (1.0 + bend)
    active = (hidden * gate).astype(LOW)
    slope = gate + hidden * (0.5 * (1.0 - bend * bend)) * (
        CURVE + (3 * CURVE * CUBIC) * square
    )
    grad_hidden = (dot_nt(grad, proj) * slope).astype(LOW)
    out, back = dot(active, proj), dot_nt(grad_hidden, fc_ref[...])

    @pl.when(step == 0)
    def _():
        out_ref[...] = out
        back_ref[...] = back

    @pl.when(step > 0)
    def _():
        out_ref[...] += out
        back_ref[...] += back

    fb_grad_ref[...] = jnp.sum(grad_hidden.astype(FULL), 0, keepdims=True)
    fc_grad = dot(turned_ref[...], grad_hidden).astype(LOW)
    others = pl.num_programs(0) // 2

    @pl.when(step < others)
    def _():
        fc_send_ref[...] = fc_grad

    @pl.when(step >= others)
    def _():
        fc_keep_ref[...] = fc_grad

    pr_grad = dot_tn(active, grad)
    low, high = pr_grad[:, :half].astype(LOW), pr_grad[:, half:].astype(LOW)
    first = core_ref[0] == 0
    pr_send_ref[...] = jnp.where(first, high, low)
    pr_keep_ref[...] = jnp.where(first, low, high)


def beside_kernel(fc_ref, proj_ref, last_ref, out_ref):
    rows, at = fc_ref.shape
    width = proj_ref.shape[1]
    out_ref[:, :at] = fc_ref[...]
    out_ref[:, 2 * at :] = last_ref[...]
    wide = proj_ref[...].astype(FULL)
    for i in range(wide.shape[0] // rows):
        out_ref[:, at + i * width : at + (i + 1) * width] = wide[i * rows : (i + 1) * rows].astype(
            LOW
        )


def beside_rows(fc, proj, last):
    rows = fc.shape[0]
    if rows % 8:
        return jnp.concatenate(
            [fc] + [proj[i : i + rows] for i in range(0, proj.shape[0], rows)] + [last], 1
        )
    vmem = pl.BlockSpec(memory_space=pltpu.VMEM)
    return pl.pallas_call(
        beside_kernel,
        in_specs=[vmem, vmem, vmem],
        out_shape=jax.ShapeDtypeStruct((rows, 2 * fc.shape[1] + last.shape[1]), LOW),
        cost_estimate=SHORT,
        name="beside",
    )(fc, proj, last)


def feed(core, normed, grad, late, fc_bias, proj, shard_rows):
    rows, width = normed.shape
    hidden = fc_bias.shape[1]
    chunk = width
    blocks = hidden // chunk
    steps = blocks // 2

    def block(i, s):
        return jnp.where(i < steps, (1 - s[0]) * steps + i, s[0] * steps + i - steps)

    whole = pl.BlockSpec((rows, width), lambda i, s: (0, 0))
    if proj is None:
        pieces = [late] * blocks
        piece_specs = [
            pl.BlockSpec((width // blocks, width), lambda i, s, at=at: (block(i, s), at))
            for at in range(blocks, 2 * blocks)
        ]
    else:
        pieces = [proj]
        piece_specs = [pl.BlockSpec((chunk, width), lambda i, s: (block(i, s), 0))]
    half = pl.BlockSpec((chunk, width // 2), lambda i, s: (block(i, s), 0))
    return pl.pallas_call(
        functools.partial(feed_kernel, shard_rows),
        out_shape=(
            jax.ShapeDtypeStruct((rows, width), FULL),
            jax.ShapeDtypeStruct((rows, width), FULL),
            jax.ShapeDtypeStruct((width, hidden // 2), LOW),
            jax.ShapeDtypeStruct((width, hidden // 2), LOW),
            jax.ShapeDtypeStruct((hidden, width // 2), LOW),
            jax.ShapeDtypeStruct((hidden, width // 2), LOW),
            jax.ShapeDtypeStruct((1, hidden), FULL),
        ),
        grid_spec=pltpu.PrefetchScalarGridSpec(
            num_scalar_prefetch=1,
            grid=(blocks,),
            in_specs=[
                whole,
                whole,
                pl.BlockSpec((width, chunk), lambda i, s: (0, block(i, s))),
                pl.BlockSpec((1, chunk), lambda i, s: (0, block(i, s))),
                *piece_specs,
            ],
            out_specs=(
                whole,
                whole,
                pl.BlockSpec((width, chunk), lambda i, s: (0, jnp.minimum(i, steps - 1))),
                pl.BlockSpec((width, chunk), lambda i, s: (0, jnp.maximum(i - steps, 0))),
                half,
                half,
                pl.BlockSpec((1, chunk), lambda i, s: (0, block(i, s))),
            ),
            scratch_shapes=[pltpu.VMEM((width, rows), LOW)],
        ),
        compiler_params=pltpu.CompilerParams(vmem_limit_bytes=VMEM),
        cost_estimate=SHORT,
        name="feed",
    )(core, normed, grad, late, fc_bias, *pieces)


def turn_kernel(
    core_ref, n_ref, hat_ref, root_ref, gain_ref, g_ref, att_ref, w_ref,
    middle_ref, keep_ref, send_ref, w_keep_ref, w_send_ref, gain_grad_ref, shift_ref, bias_ref, last_ref,
):
    half = keep_ref.shape[1]
    grad, hat = n_ref[...], hat_ref[...]
    gain_grad_ref[...] = jnp.sum(grad * hat, 0, keepdims=True)
    shift_ref[...] = jnp.sum(grad, 0, keepdims=True)
    middle = g_ref[...].astype(FULL) + normalize_back(grad, gain_ref[...], hat, root_ref[...])
    middle_ref[...] = middle
    last_ref[...] = jnp.sum(g_ref[...].astype(FULL), 0, keepdims=True)
    low = middle.astype(LOW)
    bias_ref[...] = jnp.sum(low.astype(FULL), 0, keepdims=True)
    first = core_ref[0] == 0
    for whole, kept, sent in (
        (dot_nt(low, w_ref[...]), keep_ref, send_ref),
        (dot(jnp.transpose(att_ref[...]), low), w_keep_ref, w_send_ref),
    ):
        whole = whole.astype(LOW)
        one, two = whole[:, :half], whole[:, half:]
        kept[...] = jnp.where(first, one, two)
        sent[...] = jnp.where(first, two, one)


def turn(core, grad, hat, root, gain, grad_valid, attended, late, at):
    rows, width = grad.shape
    shape = jax.ShapeDtypeStruct

    def spec(*dims):
        return pl.BlockSpec(dims, lambda i, s: (0, 0))

    whole = spec(rows, width)
    return pl.pallas_call(
        turn_kernel,
        grid_spec=pltpu.PrefetchScalarGridSpec(
            num_scalar_prefetch=1,
            grid=(1,),
            in_specs=[
                whole,
                whole,
                spec(rows, 1),
                spec(1, width),
                whole,
                whole,
                pl.BlockSpec((width, width), lambda i, s: (0, at)),
            ],
            out_specs=(
                whole,
                spec(rows, width // 2),
                spec(rows, width // 2),
                spec(width, width // 2),
                spec(width, width // 2),
                spec(1, width),
                spec(1, width),
                spec(1, width),
                spec(1, width),
            ),
        ),
        out_shape=(
            shape((rows, width), FULL),
            shape((rows, width // 2), LOW),
            shape((rows, width // 2), LOW),
            shape((width, width // 2), LOW),
            shape((width, width // 2), LOW),
            shape((1, width), FULL),
            shape((1, width), FULL),
            shape((1, width), FULL),
            shape((1, width), FULL),
        ),
        compiler_params=pltpu.CompilerParams(vmem_limit_bytes=VMEM),
        cost_estimate=SHORT,
        name="turn",
    )(core, grad, hat, root, gain, grad_valid, attended, late)


def norm_back_kernel(
    core_ref, dq_ref, dk_ref, dv_ref, wq_ref, wkv_ref, hat_ref,
    keep_ref, send_ref, gain_ref, shift_ref, q_sum_ref, v_sum_ref, part_ref,
):
    step = pl.program_id(0)
    half = dk_ref.shape[1]
    part_ref[...] = dot_nt(dk_ref[...], wkv_ref[:, :half]) + dot_nt(
        dv_ref[...], wkv_ref[:, half:]
    )

    @pl.when(step == 0)
    def _():
        for ref in (gain_ref, shift_ref, q_sum_ref, v_sum_ref):
            ref[...] = jnp.zeros_like(ref)

    @pl.when(lax.rem(step, 2) == 1)
    def _():
        part_ref[...] += dot_nt(dq_ref[...], wq_ref[...])
        q_sum_ref[...] += jnp.sum(dq_ref[...].astype(FULL), 0, keepdims=True)

    part = part_ref[...]
    v_sum_ref[...] += jnp.sum(dv_ref[...].astype(FULL), 0, keepdims=True)
    gain_ref[...] += jnp.sum(part * hat_ref[...], 0, keepdims=True)
    shift_ref[...] += jnp.sum(part, 0, keepdims=True)

    @pl.when(step < 2)
    def _():
        send_ref[0] = part.astype(LOW)

    @pl.when(step >= 2)
    def _():
        keep_ref[0] = part


def norm_back(core, dq, dk, dv, q_weight, keyval_weight, hat):
    quarter, half, width = dq.shape[0] // 2, dq.shape[1], hat.shape[1]

    def at(i, s):
        return jnp.where(i < 2, 1 - s[0], s[0])

    def block(i, s):
        return (jnp.where(lax.rem(i, 2) == 0, 2, 0) + at(i, s), 0)

    whole = lambda i, s: (0, 0)
    line, short = pl.BlockSpec((1, width), whole), pl.BlockSpec((1, half), whole)
    shape = jax.ShapeDtypeStruct
    return pl.pallas_call(
        norm_back_kernel,
        out_shape=(
            shape((2, quarter, width), FULL),
            shape((2, quarter, width), LOW),
            shape((1, width), FULL),
            shape((1, width), FULL),
            shape((1, half), FULL),
            shape((1, half), FULL),
        ),
        grid_spec=pltpu.PrefetchScalarGridSpec(
            num_scalar_prefetch=1,
            grid=(4,),
            in_specs=[
                pl.BlockSpec((quarter, half), lambda i, s: (at(i, s), 0)),
                pl.BlockSpec((quarter, half), block),
                pl.BlockSpec((quarter, half), block),
                pl.BlockSpec((width, half), whole),
                pl.BlockSpec((width, 2 * half), whole),
                pl.BlockSpec((quarter, width), block),
            ],
            out_specs=(
                pl.BlockSpec((1, quarter, width), lambda i, s: (jnp.maximum(i - 2, 0), 0, 0)),
                pl.BlockSpec((1, quarter, width), lambda i, s: (jnp.minimum(i, 1), 0, 0)),
                line,
                line,
                short,
                short,
            ),
            scratch_shapes=[pltpu.VMEM((quarter, width), FULL)],
        ),
        compiler_params=pltpu.CompilerParams(vmem_limit_bytes=VMEM),
        cost_estimate=SHORT,
        name="norm_back",
    )(core, dq, dk, dv, q_weight, keyval_weight, hat)


def pack_kernel(slots, core_ref, *refs):
    out_ref = refs[-1]
    count = out_ref.shape[0]
    spreads = {}
    for slot, parts in enumerate(slots):
        total = None
        for ref_at, size, shift, by_core in parts:
            line = refs[ref_at][...]
            length = line.shape[1]
            shape = (count, length)
            device = lax.broadcasted_iota(jnp.int32, shape, 0) - (shift + by_core * core_ref[0])
            lane = lax.broadcasted_iota(jnp.int32, shape, 1) - device * size
            piece = jnp.where((lane >= 0) & (lane < size), line, 0.0)
            if (length, size) not in spreads:
                shape = (length, LANES)
                at = lax.broadcasted_iota(jnp.int32, shape, 0).astype(FULL)
                at = at - size * jnp.floor((at + 0.5) * (1.0 / size))
                lane = lax.broadcasted_iota(jnp.int32, shape, 1).astype(FULL)
                spreads[length, size] = jnp.where(at == lane, 1.0, 0.0)
            piece = lax.dot_general(
                piece,
                spreads[length, size],
                (((1,), (0,)), ((), ())),
                precision=lax.Precision.HIGHEST,
                preferred_element_type=FULL,
            )
            total = piece if total is None else total + piece
        out_ref[:, slot * LANES : (slot + 1) * LANES] = total


def pack(core, count, q_sum, v_sum, lines):
    size = 4 * q_sum.shape[1] // count
    slots = [[(0, size, 0, count // 4), (1, size, count // 2, count // 4)]]
    slots += [[(2 + i, line.shape[1] // count, 0, 0)] for i, line in enumerate(lines)]
    lines = (q_sum, v_sum, *lines)
    whole = lambda i, s: (0, 0)
    packed = pl.pallas_call(
        functools.partial(pack_kernel, slots),
        out_shape=jax.ShapeDtypeStruct((count, len(slots) * LANES), FULL),
        grid_spec=pltpu.PrefetchScalarGridSpec(
            num_scalar_prefetch=1,
            grid=(1,),
            in_specs=[pl.BlockSpec(line.shape, whole) for line in lines],
            out_specs=pl.BlockSpec((count, len(slots) * LANES), whole),
        ),
        compiler_params=pltpu.CompilerParams(vmem_limit_bytes=VMEM),
        cost_estimate=SHORT,
        name="pack",
    )(core, *lines)
    return packed, [slot[0][1] for slot in slots]


def normalize(values):
    center = values - jnp.mean(values, -1, keepdims=True)
    spread = jnp.mean(center * center, -1, keepdims=True)
    root = lax.rsqrt(spread + 1e-05)
    return center * root, root


def normalize_back(grad, gain, hat, root):
    scaled = grad * gain
    return root * (
        scaled
        - jnp.mean(scaled, -1, keepdims=True)
        - hat * jnp.mean(scaled * hat, -1, keepdims=True)
    )


def shards(
    tokens,
    lengths,
    thought_pos,
    cotangent,
    qkv_weight,
    out_weight,
    fc_weight,
    proj_weight,
    qv_bias,
    out_bias,
    fc_bias,
    proj_bias,
    first_gain,
    first_shift,
    second_gain,
    second_shift,
):
    _, quarter, width = tokens.shape
    half = width // 2
    near = 2 * quarter
    slice_rows = qkv_weight.shape[0]
    count = 1 << flat_bits()
    plans = orders()
    core, second = bit_of(0), bit_of(1)
    far = (2 * second).astype(jnp.int32).reshape(1)

    high, hidden_width = proj_weight.shape[0], fc_weight.shape[1]
    blocks = hidden_width // width
    late = lax.all_gather(
        beside_rows(fc_weight, proj_weight, out_weight), ALL, axis=0, tiled=True
    )

    mine = tokens[0]
    flips = [(i, i ^ 2) for i in range(count) if not i & 2]
    before = lax.ppermute(mine, ALL, flips)
    near_tokens = pair(mine, swap(mine, 0), core, 0).reshape(near, width)

    third = slice_rows * 4
    small = jnp.zeros((slice_rows, LANES), LOW)
    rows_of = (
        jnp.concatenate([qv_bias, out_bias, first_gain]),
        fc_bias,
        jnp.concatenate([proj_bias, first_shift, second_gain, second_shift]),
    )
    small = small.at[:3, :third].set(jnp.stack(rows_of))
    split = qkv_weight.reshape(slice_rows, 3, 2, half)
    keep = lax.dynamic_index_in_dim(split, core, 2, keepdims=False).reshape(slice_rows, 3 * half)
    send = lax.dynamic_index_in_dim(split, 1 - core, 2, keepdims=False).reshape(
        slice_rows, 3 * half
    )
    keep, send = jnp.concatenate([keep, small], 1), jnp.concatenate([send, small], 1)
    chip = pair(keep, swap(send, 0), core, 0).reshape(2 * slice_rows, 3 * half + LANES)
    block = gather_common(chip, (before,))
    far_tokens = pair(before, swap(before, 0), core, 0).reshape(near, width)
    slots = jnp.arange(near, dtype=jnp.int32)
    thoughts = thought_pos[0]

    def is_thought(at_slots):
        return jnp.any(thoughts[None, :] == at_slots[:, None], 1, keepdims=True)

    thought_near = is_thought(second * near + slots)
    thought_far = is_thought(slots)
    shifted_near = jnp.concatenate([far_tokens[-1:], near_tokens[:-1]], 0)
    shifted_far = jnp.concatenate([far_tokens[:1], far_tokens[:-1]], 0)
    inputs_near = jnp.where(thought_near, shifted_near, near_tokens)
    inputs_far = jnp.where(thought_far, shifted_far, far_tokens)
    inputs_all = jnp.concatenate([inputs_near, inputs_far], 0)
    hat_all, root_all = normalize(inputs_all.astype(FULL))
    own = core * quarter
    inputs = lax.dynamic_slice_in_dim(inputs_near, own, quarter, 0).astype(FULL)

    parts = [
        jnp.concatenate([block[:, :, :half], block[:, :, 3 * half :]], 2),
        block[:, :, half : 3 * half],
    ]
    first_parts = gather_step(parts, plans, 0)

    parts = gather_step(first_parts, plans, 1, (hat_all, root_all))
    q_weight = parts[0][:, :, :half].reshape(width, half)
    keyval_weight = parts[1].reshape(width, 2 * half)
    small = parts[0].reshape(count, slice_rows, half + LANES)[:, :3, half : half + third]
    small = small.astype(FULL)
    at = slice_rows

    def vector(row, first, size):
        return small[:, row, first : first + size].reshape(1, count * size)

    qv_full = vector(0, 0, 2 * at)
    out_bias_full, gain_one = vector(0, 2 * at, at), vector(0, 3 * at, at)
    fc_bias_full = vector(1, 0, 4 * at)
    proj_bias_full, shift_one = vector(2, 0, at), vector(2, at, at)
    gain_two, shift_two = vector(2, 2 * at, at), vector(2, 3 * at, at)

    normed = (hat_all * gain_one + shift_one).astype(LOW)
    own_half = core * half
    q_bias = lax.dynamic_slice_in_dim(qv_full[:, :width], own_half, half, 1)
    v_bias = lax.dynamic_slice_in_dim(qv_full[:, width:], own_half, half, 1)
    query = (dot(normed[:near], q_weight) + q_bias).astype(LOW)
    keyval_bias = jnp.concatenate([jnp.zeros((1, half), FULL), v_bias], 1)
    keyval = (dot(normed, keyval_weight) + keyval_bias).astype(LOW)

    def rows_to_core(array):
        return (
            lax.dynamic_slice_in_dim(array, own, quarter, 0),
            lax.dynamic_slice_in_dim(array, quarter - own, quarter, 0),
        )

    pairs = half // LANES
    heads, logsums = attend(far, query, keyval)
    keep, send = rows_to_core(heads)
    attended = beside(keep, swap(send, 0), core)
    late = after(late, attended)
    out_full = late[:, 2 * hidden_width :]
    middle = inputs + dot(attended, out_full) + out_bias_full
    hat_two, root_two = normalize(middle)
    normed_two = (hat_two * gain_two + shift_two).astype(LOW)
    my_slots = (2 * second + core) * quarter + jnp.arange(quarter, dtype=jnp.int32)
    valid = (my_slots < lengths[0])[:, None]
    grad_valid = jnp.where(valid, cotangent[0], jnp.zeros_like(cotangent[0]))
    core_at = core.astype(jnp.int32).reshape(1)
    proj_full = None
    if slice_rows % 8:
        proj_full = late[:, hidden_width : 2 * hidden_width].reshape(count, slice_rows, blocks, width)
        proj_full = proj_full.transpose(0, 2, 1, 3).reshape(hidden_width, width)
    fed, grad_normed_two, fc_send, fc_keep, proj_send, proj_keep, fc_bias_grad = feed(
        core_at, normed_two, grad_valid, late, fc_bias_full, proj_full, slice_rows
    )
    output = middle + fed + proj_bias_full
    mixed = jnp.where(valid, output, 0.0).astype(LOW)[None]

    chips = count // 2
    fc_shape = (chips, 2 * slice_rows, hidden_width // 2)
    proj_shape = (chips, 2 * high, half)
    fc_got, proj_got = swap(fc_send, 0), swap(proj_send, 0)

    turned = turn(
        core_at, grad_normed_two, hat_two, root_two, gain_two, grad_valid, attended, late, 2 * blocks
    )
    grad_middle, keep, send, out_kept, out_send = turned[:5]
    second_gain_grad, second_shift_grad, out_bias_grad, proj_bias_grad = turned[5:]
    grad_heads = pair(keep, swap(send, 0), core, 0).reshape(near, half)
    fc_got, proj_got = after((fc_got, proj_got), grad_middle)
    fc_pair = [fc_keep.reshape(fc_shape), fc_got.reshape(fc_shape)]
    proj_pair = [proj_keep.reshape(proj_shape), proj_got.reshape(proj_shape)]
    early = [start_sum(fc_pair), start_sum(proj_pair)]
    ready = prepare(early, plans, 0)
    out_got = swap(after(out_send, *sends(ready)), 0)

    grads = ()
    now = after(grad_heads, *sends(ready))
    for which in range(pairs):
        if which == 2:
            ready = prepare(exchange(ready, grads), plans, 1)
            now = after(grad_heads, *sends(ready))
        grads = attend_back(
            far, query, keyval, now, heads, logsums, which, grads
        )
    out_got = after(out_got, *grads)
    ready = prepare(exchange(ready, grads), plans, 2)
    grad_query, grad_key, grad_value = after(grads, *sends(ready))

    last = [
        start_sum([value.reshape(chips, 2 * slice_rows, -1)])
        for value in qkv_grads(normed, grad_query, grad_key, grad_value, out_kept, out_got)
    ]
    last_ready = prepare(last, plans, 0)

    part, part_send, first_gain_grad, first_shift_grad, q_sum, v_sum = norm_back(
        core_at,
        after(grad_query, *sends(last_ready)),
        grad_key,
        grad_value,
        q_weight,
        keyval_weight,
        hat_all,
    )
    got = swap(part_send, 0)
    both = exchange(last_ready + ready, (part_send,))
    last_ready = prepare(both[:2], plans, 1)
    ready = prepare(both[2:], plans, 3)
    got = after(got, *sends(last_ready), *sends(ready))
    far_sum = (part[0] + got[0].astype(FULL)).astype(LOW)
    back = lax.ppermute(far_sum, ALL, [(b, a) for a, b in flips])
    packed, sizes = pack(
        core_at,
        count,
        q_sum,
        v_sum,
        (
            out_bias_grad,
            fc_bias_grad,
            proj_bias_grad,
            first_gain_grad,
            first_shift_grad,
            second_gain_grad,
            second_shift_grad,
        ),
    )
    packed = after(packed, far_sum)
    share = jnp.sum(lax.all_to_all(packed, ALL, 0, 0, tiled=True), 0, keepdims=True)
    for step in range(2, flat_bits() - 1):
        last = exchange(last_ready, (far_sum,))
        last_ready = prepare(last, plans, step)
    last = exchange(last_ready)
    for step in range(4, flat_bits() - 1):
        ready = prepare(exchange(ready), plans, step)
    early = exchange(ready, (far_sum,))
    fc_weight_grad, proj_weight_grad, qkv_weight_grad, out_weight_grad = finish(
        early + last,
        slice_rows,
        (
            (slice_rows, hidden_width),
            (high, width),
            (slice_rows, 3 * width),
            (slice_rows, width),
        ),
    )

    grad_normed = part[1] + got[1].astype(FULL) + back.astype(FULL)
    hat = lax.dynamic_slice_in_dim(hat_all, own, quarter, 0)
    root = lax.dynamic_slice_in_dim(root_all, own, quarter, 0)
    grad_inputs = grad_middle + normalize_back(grad_normed, gain_one, hat, root)
    thought = lax.dynamic_slice_in_dim(thought_near, own, quarter, 0)
    kept = jnp.where(thought, 0.0, grad_inputs)
    moved = jnp.where(thought, grad_inputs, 0.0)
    ctx = lax.axis_size("ctx")
    following = lax.ppermute(moved[:1], "ctx", [(i, i - 1) for i in range(1, ctx)])
    tokens_grad = (kept + jnp.concatenate([moved[1:], following], 0))[None]

    shares = [share[0, i * LANES : i * LANES + size] for i, size in enumerate(sizes)]
    return (
        mixed,
        tokens_grad,
        qkv_weight_grad,
        out_weight_grad,
        fc_weight_grad,
        proj_weight_grad,
        *shares,
    )


def solution(mesh):
    rows, matrix, vector = P("dp", "ctx", None), P(ALL, None), P(ALL)
    return jax.shard_map(
        shards,
        mesh=mesh,
        in_specs=(rows, P("dp"), P("dp", None), rows) + (matrix,) * 4 + (vector,) * 8,
        out_specs=(rows, rows) + (matrix,) * 4 + (vector,) * 8,
        check_vma=False,
    )
```

```python
import functools

import jax
import jax.numpy as jnp
from jax import lax
from jax.experimental import pallas as pl
from jax.experimental.pallas import tpu as pltpu
from jax.sharding import PartitionSpec as P

ALL = ("dp", "ctx")
LOW = jnp.bfloat16
FULL = jnp.float32
HEAD = 64
LANES = 128
SCALE = 0.125
VMEM = 48 << 20
MOST = 60 << 20
SHORT = pl.CostEstimate(flops=1 << 20, bytes_accessed=1 << 12, transcendentals=0)
LONG = pl.CostEstimate(flops=12 << 30, bytes_accessed=1 << 12, transcendentals=0)


def flat_bits():
    return (lax.axis_size("dp") * lax.axis_size("ctx")).bit_length() - 1


def flat_index():
    return lax.axis_index("dp") * lax.axis_size("ctx") + lax.axis_index("ctx")


def bit_of(bit):
    return (flat_index() >> bit) & 1


def swap(value, bit):
    count = 1 << flat_bits()
    return lax.ppermute(value, ALL, [(i, i ^ (1 << bit)) for i in range(count)])


def after(value, *others):
    return lax.optimization_barrier((value, others))[0]


def pair(mine, other, place, axis):
    shape = mine.shape[:axis] + (2,) + mine.shape[axis:]
    whole = jnp.broadcast_to(jnp.expand_dims(mine, axis), shape)
    return lax.dynamic_update_slice_in_dim(whole, jnp.expand_dims(other, axis), 1 - place, axis)


def beside(mine, other, place):
    low = place == 0
    return jnp.concatenate([jnp.where(low, mine, other), jnp.where(low, other, mine)], -1)


def orders():
    rest = list(range(3, flat_bits()))
    return [1, 2] + rest, [2, 1] + rest


def grow(block, done, bit, wait=()):
    other = after(swap(block, bit), *wait)
    rows, cols = block.shape[1:]
    high = 1 << len([b for b in done if b > bit])
    low = 1 << len([b for b in done if b < bit])
    whole = pair(
        block.reshape(high, low, rows, cols), other.reshape(high, low, rows, cols), bit_of(bit), 1
    )
    return whole.reshape(high * 2 * low, rows, cols)


def gather_common(block, wait=()):
    block, done = block[None], []
    for bit in reversed(range(3, flat_bits())):
        block = grow(block, done, bit, () if done else wait)
        done.append(bit)
    return block


def gather_step(parts, plans, step, wait=()):
    out = []
    for part, order in zip(parts, plans):
        plan = list(reversed(order))
        at = flat_bits() - 3 + step
        out.append(grow(part, plan[:at], plan[at], wait))
    return out


class Sum:
    def __init__(self, addends, left):
        self.addends = addends
        self.left = left


def group_of(bits, left, bit, part):
    order, rest = sorted(bits, reverse=True), sorted(left, reverse=True)

    def index(i, s):
        group = 0
        for b in order:
            here = (s[0] >> b) & 1
            if b == bit:
                here = 1 - here
            elif b in rest:
                here = (i >> (len(rest) - 1 - rest.index(b))) & 1
            group = 2 * group + here
        return (group, 0, part)

    return index


def total_of(refs):
    total = refs[0][0].astype(FULL)
    for ref in refs[1:]:
        value = ref[0].astype(FULL)
        rows, cols = value.shape
        if cols != total.shape[1]:
            size = total.shape[1]
            value = jnp.concatenate([value[:, i : i + size] for i in range(0, cols, size)], 0)
        total = total + value
    return total


def send_kernel(counts, joined, at_ref, *refs):
    outs = refs[len(refs) - (1 if joined else len(counts)) :]
    column = 0
    for which, count in enumerate(counts):
        total = total_of(refs[:count]).astype(LOW)
        refs = refs[count:]
        if not joined:
            outs[which][0] = total
            continue
        rows = outs[0].shape[1]
        for at in range(0, total.shape[0], rows):
            outs[0][0, :, column : column + total.shape[1]] = total[at : at + rows]
            column += total.shape[1]


def specs_of(sums, bits):
    arrays, specs = [], []
    for value, bit in zip(sums, bits):
        left = [b for b in value.left if b != bit]
        for array, own, part, parts in value.addends:
            rows, cols = array.shape[1:]
            arrays.append(array)
            specs.append(pl.BlockSpec((1, rows, cols // parts), group_of(own, left, bit, part)))
    return arrays, specs


def prepare(sums, plans, step):
    bits = [plan[step] for plan in plans]
    arrays, specs = specs_of(sums, bits)
    groups = 1 << (len(sums[0].left) - 1)
    shapes = [value.addends[0][0].shape[1:] for value in sums]
    sizes = {rows * cols for rows, cols in shapes}
    joined = len(set(bits)) == 1 and len(sizes) == 1 and len(sums) > 1
    if joined:
        low = min(rows for rows, _ in shapes)
        shapes = [(low, len(sums) * sizes.pop() // low)]
    sent = pl.pallas_call(
        functools.partial(send_kernel, [len(value.addends) for value in sums], joined),
        out_shape=tuple(jax.ShapeDtypeStruct((groups, *shape), LOW) for shape in shapes),
        grid_spec=pltpu.PrefetchScalarGridSpec(
            num_scalar_prefetch=1,
            grid=(groups,),
            in_specs=specs,
            out_specs=tuple(pl.BlockSpec((1, *shape), lambda i, s: (i, 0, 0)) for shape in shapes),
        ),
        compiler_params=pltpu.CompilerParams(vmem_limit_bytes=VMEM if groups > 2 else MOST),
        cost_estimate=LONG,
        name="send",
    )(flat_index().astype(jnp.int32).reshape(1), *arrays)
    kept = [Sum(value.addends, [b for b in value.left if b != bit]) for value, bit in zip(sums, bits)]
    if joined:
        return [(sent[0], kept, bits[0])]
    return [(send, [keep], bit) for send, keep, bit in zip(sent, kept, bits)]


def sends(prepared):
    return [send for send, _, _ in prepared]


def exchange(prepared, wait=()):
    gots = [swap(send, bit) for send, _, bit in prepared]
    gots = after(gots, *wait) if wait else gots
    return [
        Sum(keep.addends + [(got, keep.left, part, len(kept))], keep.left)
        for got, (_, kept, _) in zip(gots, prepared)
        for part, keep in enumerate(kept)
    ]


def start_sum(arrays):
    links = list(range(1, flat_bits()))
    return Sum([(value, links, 0, 1) for value in arrays], links)


def finish_kernel(counts, at_ref, *refs):
    mine_ref, send_ref = refs[-2:]
    rows = mine_ref.shape[0]
    first = (at_ref[0] & 1) == 0
    column = 0
    for count in counts:
        total = total_of(refs[:count])
        refs = refs[count:]
        half, cols = total.shape[0] // 2, total.shape[1]
        one, two = total[:half], total[half:]
        mine, other = jnp.where(first, one, two), jnp.where(first, two, one)
        for at in range(0, half, rows):
            mine_ref[:, column : column + cols] = mine[at : at + rows]
            send_ref[:, column : column + cols] = other[at : at + rows]
            column += cols


def settle_kernel(at_ref, mine_ref, other_ref, fc_ref, proj_ref, qkv_ref, out_ref):
    first = (at_ref[0] & 1) == 0
    rows = mine_ref.shape[0]
    half = out_ref.shape[1] // 2
    start = 0

    def both(size):
        mine, other = mine_ref[:, start : start + size], other_ref[:, start : start + size]
        return jnp.where(first, mine, other), jnp.where(first, other, mine)

    size = fc_ref.shape[1] // 2
    fc_ref[:, :size], fc_ref[:, size:] = both(size)
    start += size
    for at in range(0, proj_ref.shape[0], rows):
        proj_ref[at : at + rows, :half], proj_ref[at : at + rows, half:] = both(half)
        start += half
    for kind in range(3):
        at = 2 * kind * half
        qkv_ref[:, at : at + half], qkv_ref[:, at + half : at + 2 * half] = both(half)
        start += half
    out_ref[:, :half], out_ref[:, half:] = both(half)


def finish(sums, rows, widths):
    at = flat_index().astype(jnp.int32).reshape(1)
    arrays, specs = specs_of(sums, [None] * len(sums))
    total = sum(
        value.addends[0][0].shape[1] // (2 * rows) * value.addends[0][0].shape[2]
        for value in sums
    )
    shape = jax.ShapeDtypeStruct
    whole = pl.BlockSpec((rows, total), lambda i, s: (0, 0))
    mine, send = pl.pallas_call(
        functools.partial(finish_kernel, [len(value.addends) for value in sums]),
        out_shape=(shape((rows, total), FULL),) * 2,
        grid_spec=pltpu.PrefetchScalarGridSpec(
            num_scalar_prefetch=1, grid=(1,), in_specs=specs, out_specs=(whole, whole)
        ),
        compiler_params=pltpu.CompilerParams(vmem_limit_bytes=VMEM),
        cost_estimate=SHORT,
        name="finish",
    )(at, *arrays)
    return pl.pallas_call(
        settle_kernel,
        out_shape=tuple(shape(size, FULL) for size in widths),
        grid_spec=pltpu.PrefetchScalarGridSpec(
            num_scalar_prefetch=1,
            grid=(1,),
            in_specs=[whole, whole],
            out_specs=tuple(pl.BlockSpec(size, lambda i, s: (0, 0)) for size in widths),
        ),
        compiler_params=pltpu.CompilerParams(vmem_limit_bytes=VMEM),
        cost_estimate=SHORT,
        name="settle",
    )(at, mine, swap(send, 0))


def dot(a, b):
    return lax.dot_general(a, b, (((1,), (0,)), ((), ())), preferred_element_type=FULL)


def dot_nt(a, b):
    return lax.dot_general(a, b, (((1,), (1,)), ((), ())), preferred_element_type=FULL)


def dot_tn(a, b):
    return lax.dot_general(a, b, (((0,), (0,)), ((), ())), preferred_element_type=FULL)


def head_lanes(value, head):
    lane = lax.broadcasted_iota(jnp.int32, (1, LANES), 1)
    return jnp.where(lane // HEAD == head, value, jnp.zeros_like(value))


def causal(rows, cols):
    shape = (rows, cols)
    return lax.broadcasted_iota(jnp.int32, shape, 0) <= lax.broadcasted_iota(jnp.int32, shape, 1)


def attend_kernel(far_ref, q_ref, k_ref, v_ref, out_ref, lse_ref, top_ref, acc_ref):
    near = q_ref.shape[0]
    size = near // 2
    query = q_ref[...] * jnp.asarray(SCALE, LOW)

    def step(keys, queries, masked, first):
        key = k_ref[keys, :]
        value = jnp.transpose(v_ref[keys, :])
        for head in range(2):
            ones = jnp.ones((16, key.shape[0]), LOW)
            wide = jnp.concatenate([value[head * HEAD : (head + 1) * HEAD], ones], 0)
            scores = dot_nt(key, head_lanes(query[queries], head))
            if masked:
                scores = jnp.where(causal(*scores.shape), scores, -1e9)
            row = slice(head, head + 1)
            top = jnp.max(scores, 0, keepdims=True)
            if first:
                acc_ref[head, :, queries] = dot(wide, jnp.exp(scores - top).astype(LOW))
            else:
                old = top_ref[row, queries]
                top = jnp.maximum(old, top)
                acc_ref[head, :, queries] = acc_ref[head, :, queries] * jnp.exp(old - top) + dot(
                    wide, jnp.exp(scores - top).astype(LOW)
                )
            top_ref[row, queries] = top

    step(slice(0, size), slice(0, near), True, True)
    step(slice(size, near), slice(size, near), True, False)

    @pl.when(far_ref[0] > 0)
    def _():
        step(slice(near, 2 * near), slice(0, near), False, False)

    outs = []
    for head in range(2):
        total = acc_ref[head, HEAD : HEAD + 1, :]
        outs.append(acc_ref[head, :HEAD, :] / total)
        lse_ref[0, head : head + 1, :] = top_ref[head : head + 1, :] + jnp.log(total)
    out_ref[...] = jnp.transpose(jnp.concatenate(outs, 0)).astype(LOW)


def attend(far, query, keyval):
    near, width = query.shape
    total = keyval.shape[0]
    pairs = width // LANES
    rows = pl.BlockSpec((near, LANES), lambda p, s: (0, p))
    return pl.pallas_call(
        attend_kernel,
        out_shape=(
            jax.ShapeDtypeStruct((near, width), LOW),
            jax.ShapeDtypeStruct((pairs, 8, near), FULL),
        ),
        grid_spec=pltpu.PrefetchScalarGridSpec(
            num_scalar_prefetch=1,
            grid=(pairs,),
            in_specs=[
                rows,
                pl.BlockSpec((total, LANES), lambda p, s: (0, p)),
                pl.BlockSpec((total, LANES), lambda p, s: (0, p + pairs)),
            ],
            out_specs=(rows, pl.BlockSpec((1, 8, near), lambda p, s: (p, 0, 0))),
            scratch_shapes=[
                pltpu.VMEM((8, near), FULL),
                pltpu.VMEM((2, HEAD + 16, near), FULL),
            ],
        ),
        compiler_params=pltpu.CompilerParams(vmem_limit_bytes=VMEM),
        cost_estimate=SHORT,
        name="attend",
    )(far, query, keyval, keyval)


def attend_back_kernel(
    far_ref, q_ref, k_ref, v_ref, grad_ref, out_ref, lse_ref, *refs
):
    dq_ref, dk_ref, dv_ref, acc_ref = refs[-4:]
    near = q_ref.shape[0]
    size = near // 2
    spans = (slice(0, size), slice(size, near))
    query = q_ref[...] * jnp.asarray(SCALE, LOW)
    grad = grad_ref[...]
    product = jnp.transpose(grad.astype(FULL) * out_ref[...].astype(FULL))
    delta = [
        jnp.sum(product[head * HEAD : (head + 1) * HEAD], 0, keepdims=True) for head in range(2)
    ]

    def block(at, work):
        key, value = k_ref[at, :], v_ref[at, :]
        turned = jnp.transpose(key)
        dk = dv = None
        for which, masked, first in work:
            span = spans[which]
            for head in range(2):
                part = slice(head * HEAD, (head + 1) * HEAD)
                q_head = head_lanes(query[span], head)
                g_head = head_lanes(grad[span], head)
                probs = jnp.exp(dot_nt(key, q_head) - lse_ref[0, head : head + 1, span])
                if masked:
                    probs = jnp.where(causal(size, size), probs, 0.0)
                moved = probs * (dot_nt(value, g_head) - delta[head][:, span])
                moved, probs = moved.astype(LOW), probs.astype(LOW)
                new_k, new_v = dot(moved, q_head), dot(probs, g_head)
                dk = new_k if dk is None else dk + new_k
                dv = new_v if dv is None else dv + new_v
                new_q = dot(turned[part], moved)
                if first:
                    acc_ref[which, part, :] = new_q
                else:
                    acc_ref[which, part, :] += new_q
        dk_ref[at, :] = dk.astype(LOW)
        dv_ref[at, :] = dv.astype(LOW)

    block(spans[0], [(0, True, True), (1, False, True)])
    block(spans[1], [(1, True, False)])

    @pl.loop(0, far_ref[0])
    def _(i):
        at = pl.ds(pl.multiple_of(near + i * size, size), size)
        block(at, [(0, False, False), (1, False, False)])

    @pl.loop(far_ref[0], 2)
    def _(i):
        at = pl.ds(pl.multiple_of(near + i * size, size), size)
        dk_ref[at, :] = jnp.zeros((size, LANES), LOW)
        dv_ref[at, :] = jnp.zeros((size, LANES), LOW)

    for which in range(2):
        dq_ref[spans[which], :] = (jnp.transpose(acc_ref[which]) * SCALE).astype(LOW)


def attend_back(far, query, keyval, grad, out, lse, which, earlier):
    near, width = query.shape
    total = keyval.shape[0]
    pairs = width // LANES
    rows = pl.BlockSpec((near, LANES), lambda p, s: (0, which))
    every = pl.BlockSpec((total, LANES), lambda p, s: (0, which))
    return pl.pallas_call(
        attend_back_kernel,
        out_shape=(
            jax.ShapeDtypeStruct((near, width), LOW),
            jax.ShapeDtypeStruct((total, width), LOW),
            jax.ShapeDtypeStruct((total, width), LOW),
        ),
        grid_spec=pltpu.PrefetchScalarGridSpec(
            num_scalar_prefetch=1,
            grid=(1,),
            in_specs=[
                rows,
                every,
                pl.BlockSpec((total, LANES), lambda p, s: (0, which + pairs)),
                rows,
                rows,
                pl.BlockSpec((1, 8, near), lambda p, s: (which, 0, 0)),
            ]
            + [pl.BlockSpec(memory_space=pl.ANY)] * len(earlier),
            out_specs=(rows, every, every),
            scratch_shapes=[pltpu.VMEM((2, LANES, near // 2), FULL)],
        ),
        input_output_aliases={7 + i: i for i in range(len(earlier))},
        compiler_params=pltpu.CompilerParams(vmem_limit_bytes=VMEM),
        cost_estimate=SHORT,
        name="attend_back",
    )(far, query, keyval, keyval, grad, out, lse, *earlier)


def grads_kernel(n_ref, dq_ref, dk_ref, dv_ref, mine_ref, other_ref, a_ref, b_ref):
    near, width = dq_ref.shape
    turned = jnp.transpose(n_ref[...])
    low = jnp.concatenate(
        [
            dot(turned[:, :near], dq_ref[...]).astype(LOW),
            dot(turned, dk_ref[...]).astype(LOW),
            dot(turned, dv_ref[...]).astype(LOW),
            (mine_ref[...].astype(FULL) + other_ref[...].astype(FULL)).astype(LOW),
        ],
        1,
    )
    cut = a_ref.shape[1]
    a_ref[...] = low[:, :cut]
    b_ref[...] = low[:, cut:]


def qkv_grads(normed, dq, dk, dv, mine, other):
    width = normed.shape[1]
    cut = 2 * dq.shape[1]
    return pl.pallas_call(
        grads_kernel,
        out_shape=(
            jax.ShapeDtypeStruct((width, cut), LOW),
            jax.ShapeDtypeStruct((width, cut), LOW),
        ),
        compiler_params=pltpu.CompilerParams(vmem_limit_bytes=VMEM),
        cost_estimate=SHORT,
        name="qkv_grads",
    )(normed, dq, dk, dv, mine, other)


CURVE = 0.7978845608028654
CUBIC = 0.044715


def feed_kernel(
    shard_rows, core_ref, n_ref, g_ref, fc_ref, fb_ref, *refs
):
    pieces, refs = refs[:-8], refs[-8:]
    out_ref, back_ref, fc_send_ref, fc_keep_ref, pr_send_ref, pr_keep_ref = refs[:6]
    fb_grad_ref, turned_ref = refs[6:]

    step = pl.program_id(0)
    half = g_ref.shape[1] // 2

    @pl.when(step == 0)
    def _():
        turned_ref[...] = jnp.transpose(n_ref[...])

    if len(pieces) == 1:
        proj = pieces[0][...]
    else:
        size = shard_rows
        wide = [piece[...].astype(FULL) for piece in pieces]
        proj = jnp.concatenate(
            [
                piece[at : at + size]
                for at in range(0, wide[0].shape[0], size)
                for piece in wide
            ],
            0,
        ).astype(LOW)
    grad = g_ref[...]
    hidden = dot(n_ref[...], fc_ref[...]) + fb_ref[...]
    square = hidden * hidden
    bend = jnp.tanh(hidden * (CURVE + (CURVE * CUBIC) * square))
    gate = 0.5 * (1.0 + bend)
    active = (hidden * gate).astype(LOW)
    slope = gate + hidden * (0.5 * (1.0 - bend * bend)) * (
        CURVE + (3 * CURVE * CUBIC) * square
    )
    grad_hidden = (dot_nt(grad, proj) * slope).astype(LOW)
    out, back = dot(active, proj), dot_nt(grad_hidden, fc_ref[...])

    @pl.when(step == 0)
    def _():
        out_ref[...] = out
        back_ref[...] = back

    @pl.when(step > 0)
    def _():
        out_ref[...] += out
        back_ref[...] += back

    fb_grad_ref[...] = jnp.sum(grad_hidden.astype(FULL), 0, keepdims=True)
    fc_grad = dot(turned_ref[...], grad_hidden).astype(LOW)
    others = pl.num_programs(0) // 2

    @pl.when(step < others)
    def _():
        fc_send_ref[...] = fc_grad

    @pl.when(step >= others)
    def _():
        fc_keep_ref[...] = fc_grad

    pr_grad = dot_tn(active, grad)
    low, high = pr_grad[:, :half].astype(LOW), pr_grad[:, half:].astype(LOW)
    first = core_ref[0] == 0
    pr_send_ref[...] = jnp.where(first, high, low)
    pr_keep_ref[...] = jnp.where(first, low, high)


def beside_kernel(fc_ref, proj_ref, last_ref, out_ref):
    rows, at = fc_ref.shape
    width = proj_ref.shape[1]
    out_ref[:, :at] = fc_ref[...]
    out_ref[:, 2 * at :] = last_ref[...]
    wide = proj_ref[...].astype(FULL)
    for i in range(wide.shape[0] // rows):
        out_ref[:, at + i * width : at + (i + 1) * width] = wide[i * rows : (i + 1) * rows].astype(
            LOW
        )


def beside_rows(fc, proj, last):
    rows = fc.shape[0]
    if rows % 8:
        return jnp.concatenate(
            [fc] + [proj[i : i + rows] for i in range(0, proj.shape[0], rows)] + [last], 1
        )
    vmem = pl.BlockSpec(memory_space=pltpu.VMEM)
    return pl.pallas_call(
        beside_kernel,
        in_specs=[vmem, vmem, vmem],
        out_shape=jax.ShapeDtypeStruct((rows, 2 * fc.shape[1] + last.shape[1]), LOW),
        cost_estimate=SHORT,
        name="beside",
    )(fc, proj, last)


def feed(core, normed, grad, late, fc_bias, proj, shard_rows):
    rows, width = normed.shape
    hidden = fc_bias.shape[1]
    chunk = 2 * width
    blocks = hidden // width
    steps = hidden // (2 * chunk)

    def block(i, s):
        return jnp.where(i < steps, (1 - s[0]) * steps + i, s[0] * steps + i - steps)

    whole = pl.BlockSpec((rows, width), lambda i, s: (0, 0))
    if proj is None:
        pieces = [late] * blocks
        piece_specs = [
            pl.BlockSpec((chunk * width // hidden, width), lambda i, s, at=at: (block(i, s), at))
            for at in range(blocks, 2 * blocks)
        ]
    else:
        pieces = [proj]
        piece_specs = [pl.BlockSpec((chunk, width), lambda i, s: (block(i, s), 0))]
    half = pl.BlockSpec((chunk, width // 2), lambda i, s: (block(i, s), 0))
    return pl.pallas_call(
        functools.partial(feed_kernel, shard_rows),
        out_shape=(
            jax.ShapeDtypeStruct((rows, width), FULL),
            jax.ShapeDtypeStruct((rows, width), FULL),
            jax.ShapeDtypeStruct((width, hidden // 2), LOW),
            jax.ShapeDtypeStruct((width, hidden // 2), LOW),
            jax.ShapeDtypeStruct((hidden, width // 2), LOW),
            jax.ShapeDtypeStruct((hidden, width // 2), LOW),
            jax.ShapeDtypeStruct((1, hidden), FULL),
        ),
        grid_spec=pltpu.PrefetchScalarGridSpec(
            num_scalar_prefetch=1,
            grid=(2 * steps,),
            in_specs=[
                whole,
                whole,
                pl.BlockSpec((width, chunk), lambda i, s: (0, block(i, s))),
                pl.BlockSpec((1, chunk), lambda i, s: (0, block(i, s))),
                *piece_specs,
            ],
            out_specs=(
                whole,
                whole,
                pl.BlockSpec((width, chunk), lambda i, s: (0, jnp.minimum(i, steps - 1))),
                pl.BlockSpec((width, chunk), lambda i, s: (0, jnp.maximum(i - steps, 0))),
                half,
                half,
                pl.BlockSpec((1, chunk), lambda i, s: (0, block(i, s))),
            ),
            scratch_shapes=[pltpu.VMEM((width, rows), LOW)],
        ),
        compiler_params=pltpu.CompilerParams(vmem_limit_bytes=VMEM),
        cost_estimate=SHORT,
        name="feed",
    )(core, normed, grad, late, fc_bias, *pieces)


def turn_kernel(
    core_ref, n_ref, hat_ref, root_ref, gain_ref, g_ref, att_ref, w_ref,
    middle_ref, keep_ref, send_ref, w_keep_ref, w_send_ref, gain_grad_ref, shift_ref, bias_ref, last_ref,
):
    half = keep_ref.shape[1]
    grad, hat = n_ref[...], hat_ref[...]
    gain_grad_ref[...] = jnp.sum(grad * hat, 0, keepdims=True)
    shift_ref[...] = jnp.sum(grad, 0, keepdims=True)
    middle = g_ref[...].astype(FULL) + normalize_back(grad, gain_ref[...], hat, root_ref[...])
    middle_ref[...] = middle
    last_ref[...] = jnp.sum(g_ref[...].astype(FULL), 0, keepdims=True)
    low = middle.astype(LOW)
    bias_ref[...] = jnp.sum(low.astype(FULL), 0, keepdims=True)
    first = core_ref[0] == 0
    for whole, kept, sent in (
        (dot_nt(low, w_ref[...]), keep_ref, send_ref),
        (dot(jnp.transpose(att_ref[...]), low), w_keep_ref, w_send_ref),
    ):
        whole = whole.astype(LOW)
        one, two = whole[:, :half], whole[:, half:]
        kept[...] = jnp.where(first, one, two)
        sent[...] = jnp.where(first, two, one)


def turn(core, grad, hat, root, gain, grad_valid, attended, late, at):
    rows, width = grad.shape
    shape = jax.ShapeDtypeStruct

    def spec(*dims):
        return pl.BlockSpec(dims, lambda i, s: (0, 0))

    whole = spec(rows, width)
    return pl.pallas_call(
        turn_kernel,
        grid_spec=pltpu.PrefetchScalarGridSpec(
            num_scalar_prefetch=1,
            grid=(1,),
            in_specs=[
                whole,
                whole,
                spec(rows, 1),
                spec(1, width),
                whole,
                whole,
                pl.BlockSpec((width, width), lambda i, s: (0, at)),
            ],
            out_specs=(
                whole,
                spec(rows, width // 2),
                spec(rows, width // 2),
                spec(width, width // 2),
                spec(width, width // 2),
                spec(1, width),
                spec(1, width),
                spec(1, width),
                spec(1, width),
            ),
        ),
        out_shape=(
            shape((rows, width), FULL),
            shape((rows, width // 2), LOW),
            shape((rows, width // 2), LOW),
            shape((width, width // 2), LOW),
            shape((width, width // 2), LOW),
            shape((1, width), FULL),
            shape((1, width), FULL),
            shape((1, width), FULL),
            shape((1, width), FULL),
        ),
        compiler_params=pltpu.CompilerParams(vmem_limit_bytes=VMEM),
        cost_estimate=SHORT,
        name="turn",
    )(core, grad, hat, root, gain, grad_valid, attended, late)


def norm_back_kernel(
    core_ref, dq_ref, dk_ref, dv_ref, wq_ref, wkv_ref, hat_ref,
    keep_ref, send_ref, gain_ref, shift_ref, q_sum_ref, v_sum_ref, part_ref,
):
    step = pl.program_id(0)
    half = dk_ref.shape[1]
    part_ref[...] = dot_nt(dk_ref[...], wkv_ref[:, :half]) + dot_nt(
        dv_ref[...], wkv_ref[:, half:]
    )

    @pl.when(step == 0)
    def _():
        for ref in (gain_ref, shift_ref, q_sum_ref, v_sum_ref):
            ref[...] = jnp.zeros_like(ref)

    @pl.when(lax.rem(step, 2) == 1)
    def _():
        part_ref[...] += dot_nt(dq_ref[...], wq_ref[...])
        q_sum_ref[...] += jnp.sum(dq_ref[...].astype(FULL), 0, keepdims=True)

    part = part_ref[...]
    v_sum_ref[...] += jnp.sum(dv_ref[...].astype(FULL), 0, keepdims=True)
    gain_ref[...] += jnp.sum(part * hat_ref[...], 0, keepdims=True)
    shift_ref[...] += jnp.sum(part, 0, keepdims=True)

    @pl.when(step < 2)
    def _():
        send_ref[0] = part.astype(LOW)

    @pl.when(step >= 2)
    def _():
        keep_ref[0] = part


def norm_back(core, dq, dk, dv, q_weight, keyval_weight, hat):
    quarter, half, width = dq.shape[0] // 2, dq.shape[1], hat.shape[1]

    def at(i, s):
        return jnp.where(i < 2, 1 - s[0], s[0])

    def block(i, s):
        return (jnp.where(lax.rem(i, 2) == 0, 2, 0) + at(i, s), 0)

    whole = lambda i, s: (0, 0)
    line, short = pl.BlockSpec((1, width), whole), pl.BlockSpec((1, half), whole)
    shape = jax.ShapeDtypeStruct
    return pl.pallas_call(
        norm_back_kernel,
        out_shape=(
            shape((2, quarter, width), FULL),
            shape((2, quarter, width), LOW),
            shape((1, width), FULL),
            shape((1, width), FULL),
            shape((1, half), FULL),
            shape((1, half), FULL),
        ),
        grid_spec=pltpu.PrefetchScalarGridSpec(
            num_scalar_prefetch=1,
            grid=(4,),
            in_specs=[
                pl.BlockSpec((quarter, half), lambda i, s: (at(i, s), 0)),
                pl.BlockSpec((quarter, half), block),
                pl.BlockSpec((quarter, half), block),
                pl.BlockSpec((width, half), whole),
                pl.BlockSpec((width, 2 * half), whole),
                pl.BlockSpec((quarter, width), block),
            ],
            out_specs=(
                pl.BlockSpec((1, quarter, width), lambda i, s: (jnp.maximum(i - 2, 0), 0, 0)),
                pl.BlockSpec((1, quarter, width), lambda i, s: (jnp.minimum(i, 1), 0, 0)),
                line,
                line,
                short,
                short,
            ),
            scratch_shapes=[pltpu.VMEM((quarter, width), FULL)],
        ),
        compiler_params=pltpu.CompilerParams(vmem_limit_bytes=VMEM),
        cost_estimate=SHORT,
        name="norm_back",
    )(core, dq, dk, dv, q_weight, keyval_weight, hat)


def pack_kernel(slots, core_ref, *refs):
    out_ref = refs[-1]
    count = out_ref.shape[0]
    spreads = {}
    for slot, parts in enumerate(slots):
        total = None
        for ref_at, size, shift, by_core in parts:
            line = refs[ref_at][...]
            length = line.shape[1]
            shape = (count, length)
            device = lax.broadcasted_iota(jnp.int32, shape, 0) - (shift + by_core * core_ref[0])
            lane = lax.broadcasted_iota(jnp.int32, shape, 1) - device * size
            piece = jnp.where((lane >= 0) & (lane < size), line, 0.0)
            if (length, size) not in spreads:
                shape = (length, LANES)
                at = lax.broadcasted_iota(jnp.int32, shape, 0).astype(FULL)
                at = at - size * jnp.floor((at + 0.5) * (1.0 / size))
                lane = lax.broadcasted_iota(jnp.int32, shape, 1).astype(FULL)
                spreads[length, size] = jnp.where(at == lane, 1.0, 0.0)
            piece = lax.dot_general(
                piece,
                spreads[length, size],
                (((1,), (0,)), ((), ())),
                precision=lax.Precision.HIGHEST,
                preferred_element_type=FULL,
            )
            total = piece if total is None else total + piece
        out_ref[:, slot * LANES : (slot + 1) * LANES] = total


def pack(core, count, q_sum, v_sum, lines):
    size = 4 * q_sum.shape[1] // count
    slots = [[(0, size, 0, count // 4), (1, size, count // 2, count // 4)]]
    slots += [[(2 + i, line.shape[1] // count, 0, 0)] for i, line in enumerate(lines)]
    lines = (q_sum, v_sum, *lines)
    whole = lambda i, s: (0, 0)
    packed = pl.pallas_call(
        functools.partial(pack_kernel, slots),
        out_shape=jax.ShapeDtypeStruct((count, len(slots) * LANES), FULL),
        grid_spec=pltpu.PrefetchScalarGridSpec(
            num_scalar_prefetch=1,
            grid=(1,),
            in_specs=[pl.BlockSpec(line.shape, whole) for line in lines],
            out_specs=pl.BlockSpec((count, len(slots) * LANES), whole),
        ),
        compiler_params=pltpu.CompilerParams(vmem_limit_bytes=VMEM),
        cost_estimate=SHORT,
        name="pack",
    )(core, *lines)
    return packed, [slot[0][1] for slot in slots]


def normalize(values):
    center = values - jnp.mean(values, -1, keepdims=True)
    spread = jnp.mean(center * center, -1, keepdims=True)
    root = lax.rsqrt(spread + 1e-05)
    return center * root, root


def normalize_back(grad, gain, hat, root):
    scaled = grad * gain
    return root * (
        scaled
        - jnp.mean(scaled, -1, keepdims=True)
        - hat * jnp.mean(scaled * hat, -1, keepdims=True)
    )


def shards(
    tokens,
    lengths,
    thought_pos,
    cotangent,
    qkv_weight,
    out_weight,
    fc_weight,
    proj_weight,
    qv_bias,
    out_bias,
    fc_bias,
    proj_bias,
    first_gain,
    first_shift,
    second_gain,
    second_shift,
):
    _, quarter, width = tokens.shape
    half = width // 2
    near = 2 * quarter
    slice_rows = qkv_weight.shape[0]
    count = 1 << flat_bits()
    plans = orders()
    core, second = bit_of(0), bit_of(1)
    far = (2 * second).astype(jnp.int32).reshape(1)

    high, hidden_width = proj_weight.shape[0], fc_weight.shape[1]
    blocks = hidden_width // width
    late = lax.all_gather(
        beside_rows(fc_weight, proj_weight, out_weight), ALL, axis=0, tiled=True
    )

    mine = tokens[0]
    flips = [(i, i ^ 2) for i in range(count) if not i & 2]
    before = lax.ppermute(mine, ALL, flips)
    near_tokens = pair(mine, swap(mine, 0), core, 0).reshape(near, width)

    third = slice_rows * 4
    small = jnp.zeros((slice_rows, LANES), LOW)
    rows_of = (
        jnp.concatenate([qv_bias, out_bias, first_gain]),
        fc_bias,
        jnp.concatenate([proj_bias, first_shift, second_gain, second_shift]),
    )
    small = small.at[:3, :third].set(jnp.stack(rows_of))
    split = qkv_weight.reshape(slice_rows, 3, 2, half)
    keep = lax.dynamic_index_in_dim(split, core, 2, keepdims=False).reshape(slice_rows, 3 * half)
    send = lax.dynamic_index_in_dim(split, 1 - core, 2, keepdims=False).reshape(
        slice_rows, 3 * half
    )
    keep, send = jnp.concatenate([keep, small], 1), jnp.concatenate([send, small], 1)
    chip = pair(keep, swap(send, 0), core, 0).reshape(2 * slice_rows, 3 * half + LANES)
    block = gather_common(chip, (before,))
    far_tokens = pair(before, swap(before, 0), core, 0).reshape(near, width)
    slots = jnp.arange(near, dtype=jnp.int32)
    thoughts = thought_pos[0]

    def is_thought(at_slots):
        return jnp.any(thoughts[None, :] == at_slots[:, None], 1, keepdims=True)

    thought_near = is_thought(second * near + slots)
    thought_far = is_thought(slots)
    shifted_near = jnp.concatenate([far_tokens[-1:], near_tokens[:-1]], 0)
    shifted_far = jnp.concatenate([far_tokens[:1], far_tokens[:-1]], 0)
    inputs_near = jnp.where(thought_near, shifted_near, near_tokens)
    inputs_far = jnp.where(thought_far, shifted_far, far_tokens)
    inputs_all = jnp.concatenate([inputs_near, inputs_far], 0)
    hat_all, root_all = normalize(inputs_all.astype(FULL))
    own = core * quarter
    inputs = lax.dynamic_slice_in_dim(inputs_near, own, quarter, 0).astype(FULL)

    parts = [
        jnp.concatenate([block[:, :, :half], block[:, :, 3 * half :]], 2),
        block[:, :, half : 3 * half],
    ]
    first_parts = gather_step(parts, plans, 0)

    parts = gather_step(first_parts, plans, 1, (hat_all, root_all))
    q_weight = parts[0][:, :, :half].reshape(width, half)
    keyval_weight = parts[1].reshape(width, 2 * half)
    small = parts[0].reshape(count, slice_rows, half + LANES)[:, :3, half : half + third]
    small = small.astype(FULL)
    at = slice_rows

    def vector(row, first, size):
        return small[:, row, first : first + size].reshape(1, count * size)

    qv_full = vector(0, 0, 2 * at)
    out_bias_full, gain_one = vector(0, 2 * at, at), vector(0, 3 * at, at)
    fc_bias_full = vector(1, 0, 4 * at)
    proj_bias_full, shift_one = vector(2, 0, at), vector(2, at, at)
    gain_two, shift_two = vector(2, 2 * at, at), vector(2, 3 * at, at)

    normed = (hat_all * gain_one + shift_one).astype(LOW)
    own_half = core * half
    q_bias = lax.dynamic_slice_in_dim(qv_full[:, :width], own_half, half, 1)
    v_bias = lax.dynamic_slice_in_dim(qv_full[:, width:], own_half, half, 1)
    query = (dot(normed[:near], q_weight) + q_bias).astype(LOW)
    keyval_bias = jnp.concatenate([jnp.zeros((1, half), FULL), v_bias], 1)
    keyval = (dot(normed, keyval_weight) + keyval_bias).astype(LOW)

    def rows_to_core(array):
        return (
            lax.dynamic_slice_in_dim(array, own, quarter, 0),
            lax.dynamic_slice_in_dim(array, quarter - own, quarter, 0),
        )

    pairs = half // LANES
    heads, logsums = attend(far, query, keyval)
    keep, send = rows_to_core(heads)
    attended = beside(keep, swap(send, 0), core)
    late = after(late, attended)
    out_full = late[:, 2 * hidden_width :]
    middle = inputs + dot(attended, out_full) + out_bias_full
    hat_two, root_two = normalize(middle)
    normed_two = (hat_two * gain_two + shift_two).astype(LOW)
    my_slots = (2 * second + core) * quarter + jnp.arange(quarter, dtype=jnp.int32)
    valid = (my_slots < lengths[0])[:, None]
    grad_valid = jnp.where(valid, cotangent[0], jnp.zeros_like(cotangent[0]))
    core_at = core.astype(jnp.int32).reshape(1)
    proj_full = None
    if slice_rows % 8:
        proj_full = late[:, hidden_width : 2 * hidden_width].reshape(count, slice_rows, blocks, width)
        proj_full = proj_full.transpose(0, 2, 1, 3).reshape(hidden_width, width)
    fed, grad_normed_two, fc_send, fc_keep, proj_send, proj_keep, fc_bias_grad = feed(
        core_at, normed_two, grad_valid, late, fc_bias_full, proj_full, slice_rows
    )
    output = middle + fed + proj_bias_full
    mixed = jnp.where(valid, output, 0.0).astype(LOW)[None]

    chips = count // 2
    fc_shape = (chips, 2 * slice_rows, hidden_width // 2)
    proj_shape = (chips, 2 * high, half)
    fc_got, proj_got = swap(fc_send, 0), swap(proj_send, 0)

    turned = turn(
        core_at, grad_normed_two, hat_two, root_two, gain_two, grad_valid, attended, late, 2 * blocks
    )
    grad_middle, keep, send, out_kept, out_send = turned[:5]
    second_gain_grad, second_shift_grad, out_bias_grad, proj_bias_grad = turned[5:]
    grad_heads = pair(keep, swap(send, 0), core, 0).reshape(near, half)
    fc_got, proj_got = after((fc_got, proj_got), grad_middle)
    fc_pair = [fc_keep.reshape(fc_shape), fc_got.reshape(fc_shape)]
    proj_pair = [proj_keep.reshape(proj_shape), proj_got.reshape(proj_shape)]
    early = [start_sum(fc_pair), start_sum(proj_pair)]
    ready = prepare(early, plans, 0)
    out_got = swap(after(out_send, *sends(ready)), 0)

    grads = ()
    now = after(grad_heads, *sends(ready))
    for which in range(pairs):
        if which == 2:
            ready = prepare(exchange(ready, grads), plans, 1)
            now = after(grad_heads, *sends(ready))
        grads = attend_back(
            far, query, keyval, now, heads, logsums, which, grads
        )
    out_got = after(out_got, *grads)
    ready = prepare(exchange(ready, grads), plans, 2)
    grad_query, grad_key, grad_value = after(grads, *sends(ready))

    last = [
        start_sum([value.reshape(chips, 2 * slice_rows, -1)])
        for value in qkv_grads(normed, grad_query, grad_key, grad_value, out_kept, out_got)
    ]
    last_ready = prepare(last, plans, 0)

    part, part_send, first_gain_grad, first_shift_grad, q_sum, v_sum = norm_back(
        core_at,
        after(grad_query, *sends(last_ready)),
        grad_key,
        grad_value,
        q_weight,
        keyval_weight,
        hat_all,
    )
    got = swap(part_send, 0)
    both = exchange(last_ready + ready, (part_send,))
    last_ready = prepare(both[:2], plans, 1)
    ready = prepare(both[2:], plans, 3)
    got = after(got, *sends(last_ready), *sends(ready))
    far_sum = (part[0] + got[0].astype(FULL)).astype(LOW)
    back = lax.ppermute(far_sum, ALL, [(b, a) for a, b in flips])
    packed, sizes = pack(
        core_at,
        count,
        q_sum,
        v_sum,
        (
            out_bias_grad,
            fc_bias_grad,
            proj_bias_grad,
            first_gain_grad,
            first_shift_grad,
            second_gain_grad,
            second_shift_grad,
        ),
    )
    for step in range(2, flat_bits() - 1):
        last = exchange(last_ready, (far_sum,))
        last_ready = prepare(last, plans, step)
    packed = after(packed, *sends(last_ready))
    share = jnp.sum(lax.all_to_all(packed, ALL, 0, 0, tiled=True), 0, keepdims=True)
    last = exchange(last_ready)
    for step in range(4, flat_bits() - 1):
        ready = prepare(exchange(ready), plans, step)
    early = exchange(ready, (far_sum,))
    fc_weight_grad, proj_weight_grad, qkv_weight_grad, out_weight_grad = finish(
        early + last,
        slice_rows,
        (
            (slice_rows, hidden_width),
            (high, width),
            (slice_rows, 3 * width),
            (slice_rows, width),
        ),
    )

    grad_normed = part[1] + got[1].astype(FULL) + back.astype(FULL)
    hat = lax.dynamic_slice_in_dim(hat_all, own, quarter, 0)
    root = lax.dynamic_slice_in_dim(root_all, own, quarter, 0)
    grad_inputs = grad_middle + normalize_back(grad_normed, gain_one, hat, root)
    thought = lax.dynamic_slice_in_dim(thought_near, own, quarter, 0)
    kept = jnp.where(thought, 0.0, grad_inputs)
    moved = jnp.where(thought, grad_inputs, 0.0)
    ctx = lax.axis_size("ctx")
    following = lax.ppermute(moved[:1], "ctx", [(i, i - 1) for i in range(1, ctx)])
    tokens_grad = (kept + jnp.concatenate([moved[1:], following], 0))[None]

    shares = [share[0, i * LANES : i * LANES + size] for i, size in enumerate(sizes)]
    return (
        mixed,
        tokens_grad,
        qkv_weight_grad,
        out_weight_grad,
        fc_weight_grad,
        proj_weight_grad,
        *shares,
    )


def solution(mesh):
    rows, matrix, vector = P("dp", "ctx", None), P(ALL, None), P(ALL)
    return jax.shard_map(
        shards,
        mesh=mesh,
        in_specs=(rows, P("dp"), P("dp", None), rows) + (matrix,) * 4 + (vector,) * 8,
        out_specs=(rows, rows) + (matrix,) * 4 + (vector,) * 8,
        check_vma=False,
    )
```

```python
import functools

import jax
import jax.numpy as jnp
from jax import lax
from jax.experimental import pallas as pl
from jax.experimental.pallas import tpu as pltpu
from jax.sharding import PartitionSpec as P

ALL = ("dp", "ctx")
LOW = jnp.bfloat16
FULL = jnp.float32
HEAD = 64
LANES = 128
SCALE = 0.125
VMEM = 48 << 20
MOST = 60 << 20
SHORT = pl.CostEstimate(flops=1 << 20, bytes_accessed=1 << 12, transcendentals=0)
LONG = pl.CostEstimate(flops=12 << 30, bytes_accessed=1 << 12, transcendentals=0)


def flat_bits():
    return (lax.axis_size("dp") * lax.axis_size("ctx")).bit_length() - 1


def flat_index():
    return lax.axis_index("dp") * lax.axis_size("ctx") + lax.axis_index("ctx")


def bit_of(bit):
    return (flat_index() >> bit) & 1


def swap(value, bit):
    count = 1 << flat_bits()
    return lax.ppermute(value, ALL, [(i, i ^ (1 << bit)) for i in range(count)])


def after(value, *others):
    return lax.optimization_barrier((value, others))[0]


def pair(mine, other, place, axis):
    shape = mine.shape[:axis] + (2,) + mine.shape[axis:]
    whole = jnp.broadcast_to(jnp.expand_dims(mine, axis), shape)
    return lax.dynamic_update_slice_in_dim(whole, jnp.expand_dims(other, axis), 1 - place, axis)


def beside(mine, other, place):
    low = place == 0
    return jnp.concatenate([jnp.where(low, mine, other), jnp.where(low, other, mine)], -1)


def orders():
    rest = list(range(3, flat_bits()))
    return [1, 2] + rest, [2, 1] + rest


def grow(block, done, bit, wait=()):
    other = after(swap(block, bit), *wait)
    rows, cols = block.shape[1:]
    high = 1 << len([b for b in done if b > bit])
    low = 1 << len([b for b in done if b < bit])
    whole = pair(
        block.reshape(high, low, rows, cols), other.reshape(high, low, rows, cols), bit_of(bit), 1
    )
    return whole.reshape(high * 2 * low, rows, cols)


def gather_common(block, wait=()):
    block, done = block[None], []
    for bit in reversed(range(3, flat_bits())):
        block = grow(block, done, bit, () if done else wait)
        done.append(bit)
    return block


def gather_step(parts, plans, step, wait=()):
    out = []
    for part, order in zip(parts, plans):
        plan = list(reversed(order))
        at = flat_bits() - 3 + step
        out.append(grow(part, plan[:at], plan[at], wait))
    return out


class Sum:
    def __init__(self, addends, left):
        self.addends = addends
        self.left = left


def group_of(bits, left, bit, part):
    order, rest = sorted(bits, reverse=True), sorted(left, reverse=True)

    def index(i, s):
        group = 0
        for b in order:
            here = (s[0] >> b) & 1
            if b == bit:
                here = 1 - here
            elif b in rest:
                here = (i >> (len(rest) - 1 - rest.index(b))) & 1
            group = 2 * group + here
        return (group, 0, part)

    return index


def total_of(refs):
    total = refs[0][0].astype(FULL)
    for ref in refs[1:]:
        value = ref[0].astype(FULL)
        rows, cols = value.shape
        if cols != total.shape[1]:
            size = total.shape[1]
            value = jnp.concatenate([value[:, i : i + size] for i in range(0, cols, size)], 0)
        total = total + value
    return total


def send_kernel(counts, joined, at_ref, *refs):
    outs = refs[len(refs) - (1 if joined else len(counts)) :]
    column = 0
    for which, count in enumerate(counts):
        total = total_of(refs[:count]).astype(LOW)
        refs = refs[count:]
        if not joined:
            outs[which][0] = total
            continue
        rows = outs[0].shape[1]
        for at in range(0, total.shape[0], rows):
            outs[0][0, :, column : column + total.shape[1]] = total[at : at + rows]
            column += total.shape[1]


def specs_of(sums, bits):
    arrays, specs = [], []
    for value, bit in zip(sums, bits):
        left = [b for b in value.left if b != bit]
        for array, own, part, parts in value.addends:
            rows, cols = array.shape[1:]
            arrays.append(array)
            specs.append(pl.BlockSpec((1, rows, cols // parts), group_of(own, left, bit, part)))
    return arrays, specs


def prepare(sums, plans, step):
    bits = [plan[step] for plan in plans]
    arrays, specs = specs_of(sums, bits)
    groups = 1 << (len(sums[0].left) - 1)
    shapes = [value.addends[0][0].shape[1:] for value in sums]
    sizes = {rows * cols for rows, cols in shapes}
    joined = len(set(bits)) == 1 and len(sizes) == 1 and len(sums) > 1
    if joined:
        low = min(rows for rows, _ in shapes)
        shapes = [(low, len(sums) * sizes.pop() // low)]
    sent = pl.pallas_call(
        functools.partial(send_kernel, [len(value.addends) for value in sums], joined),
        out_shape=tuple(jax.ShapeDtypeStruct((groups, *shape), LOW) for shape in shapes),
        grid_spec=pltpu.PrefetchScalarGridSpec(
            num_scalar_prefetch=1,
            grid=(groups,),
            in_specs=specs,
            out_specs=tuple(pl.BlockSpec((1, *shape), lambda i, s: (i, 0, 0)) for shape in shapes),
        ),
        compiler_params=pltpu.CompilerParams(vmem_limit_bytes=VMEM if groups > 2 else MOST),
        cost_estimate=LONG,
        name="send",
    )(flat_index().astype(jnp.int32).reshape(1), *arrays)
    kept = [Sum(value.addends, [b for b in value.left if b != bit]) for value, bit in zip(sums, bits)]
    if joined:
        return [(sent[0], kept, bits[0])]
    return [(send, [keep], bit) for send, keep, bit in zip(sent, kept, bits)]


def sends(prepared):
    return [send for send, _, _ in prepared]


def exchange(prepared, wait=()):
    gots = [swap(send, bit) for send, _, bit in prepared]
    gots = after(gots, *wait) if wait else gots
    return [
        Sum(keep.addends + [(got, keep.left, part, len(kept))], keep.left)
        for got, (_, kept, _) in zip(gots, prepared)
        for part, keep in enumerate(kept)
    ]


def start_sum(arrays):
    links = list(range(1, flat_bits()))
    return Sum([(value, links, 0, 1) for value in arrays], links)


def finish_kernel(counts, at_ref, *refs):
    mine_ref, send_ref = refs[-2:]
    rows = mine_ref.shape[0]
    first = (at_ref[0] & 1) == 0
    column = 0
    for count in counts:
        total = total_of(refs[:count])
        refs = refs[count:]
        half, cols = total.shape[0] // 2, total.shape[1]
        one, two = total[:half], total[half:]
        mine, other = jnp.where(first, one, two), jnp.where(first, two, one)
        for at in range(0, half, rows):
            mine_ref[:, column : column + cols] = mine[at : at + rows]
            send_ref[:, column : column + cols] = other[at : at + rows]
            column += cols


def settle_kernel(at_ref, mine_ref, other_ref, fc_ref, proj_ref, qkv_ref, out_ref):
    first = (at_ref[0] & 1) == 0
    rows = mine_ref.shape[0]
    half = out_ref.shape[1] // 2
    start = 0

    def both(size):
        mine, other = mine_ref[:, start : start + size], other_ref[:, start : start + size]
        return jnp.where(first, mine, other), jnp.where(first, other, mine)

    size = fc_ref.shape[1] // 2
    fc_ref[:, :size], fc_ref[:, size:] = both(size)
    start += size
    for at in range(0, proj_ref.shape[0], rows):
        proj_ref[at : at + rows, :half], proj_ref[at : at + rows, half:] = both(half)
        start += half
    for kind in range(3):
        at = 2 * kind * half
        qkv_ref[:, at : at + half], qkv_ref[:, at + half : at + 2 * half] = both(half)
        start += half
    out_ref[:, :half], out_ref[:, half:] = both(half)


def finish(sums, rows, widths):
    at = flat_index().astype(jnp.int32).reshape(1)
    arrays, specs = specs_of(sums, [None] * len(sums))
    total = sum(
        value.addends[0][0].shape[1] // (2 * rows) * value.addends[0][0].shape[2]
        for value in sums
    )
    shape = jax.ShapeDtypeStruct
    whole = pl.BlockSpec((rows, total), lambda i, s: (0, 0))
    mine, send = pl.pallas_call(
        functools.partial(finish_kernel, [len(value.addends) for value in sums]),
        out_shape=(shape((rows, total), FULL),) * 2,
        grid_spec=pltpu.PrefetchScalarGridSpec(
            num_scalar_prefetch=1, grid=(1,), in_specs=specs, out_specs=(whole, whole)
        ),
        compiler_params=pltpu.CompilerParams(vmem_limit_bytes=VMEM),
        cost_estimate=SHORT,
        name="finish",
    )(at, *arrays)
    return pl.pallas_call(
        settle_kernel,
        out_shape=tuple(shape(size, FULL) for size in widths),
        grid_spec=pltpu.PrefetchScalarGridSpec(
            num_scalar_prefetch=1,
            grid=(1,),
            in_specs=[whole, whole],
            out_specs=tuple(pl.BlockSpec(size, lambda i, s: (0, 0)) for size in widths),
        ),
        compiler_params=pltpu.CompilerParams(vmem_limit_bytes=VMEM),
        cost_estimate=SHORT,
        name="settle",
    )(at, mine, swap(send, 0))


def dot(a, b):
    return lax.dot_general(a, b, (((1,), (0,)), ((), ())), preferred_element_type=FULL)


def dot_nt(a, b):
    return lax.dot_general(a, b, (((1,), (1,)), ((), ())), preferred_element_type=FULL)


def dot_tn(a, b):
    return lax.dot_general(a, b, (((0,), (0,)), ((), ())), preferred_element_type=FULL)


def head_lanes(value, head):
    lane = lax.broadcasted_iota(jnp.int32, (1, LANES), 1)
    return jnp.where(lane // HEAD == head, value, jnp.zeros_like(value))


def causal(rows, cols):
    shape = (rows, cols)
    return lax.broadcasted_iota(jnp.int32, shape, 0) <= lax.broadcasted_iota(jnp.int32, shape, 1)


def attend_kernel(far_ref, q_ref, k_ref, v_ref, out_ref, lse_ref, top_ref, acc_ref):
    near = q_ref.shape[0]
    size = near // 2
    query = q_ref[...] * jnp.asarray(SCALE, LOW)

    def step(keys, queries, masked, first):
        key = k_ref[keys, :]
        value = jnp.transpose(v_ref[keys, :])
        for head in range(2):
            ones = jnp.ones((16, key.shape[0]), LOW)
            wide = jnp.concatenate([value[head * HEAD : (head + 1) * HEAD], ones], 0)
            scores = dot_nt(key, head_lanes(query[queries], head))
            if masked:
                scores = jnp.where(causal(*scores.shape), scores, -1e9)
            row = slice(head, head + 1)
            top = jnp.max(scores, 0, keepdims=True)
            if first:
                acc_ref[head, :, queries] = dot(wide, jnp.exp(scores - top).astype(LOW))
            else:
                old = top_ref[row, queries]
                top = jnp.maximum(old, top)
                acc_ref[head, :, queries] = acc_ref[head, :, queries] * jnp.exp(old - top) + dot(
                    wide, jnp.exp(scores - top).astype(LOW)
                )
            top_ref[row, queries] = top

    step(slice(0, size), slice(0, near), True, True)
    step(slice(size, near), slice(size, near), True, False)

    @pl.when(far_ref[0] > 0)
    def _():
        step(slice(near, 2 * near), slice(0, near), False, False)

    outs = []
    for head in range(2):
        total = acc_ref[head, HEAD : HEAD + 1, :]
        outs.append(acc_ref[head, :HEAD, :] / total)
        lse_ref[0, head : head + 1, :] = top_ref[head : head + 1, :] + jnp.log(total)
    out_ref[...] = jnp.transpose(jnp.concatenate(outs, 0)).astype(LOW)


def attend(far, query, keyval):
    near, width = query.shape
    total = keyval.shape[0]
    pairs = width // LANES
    rows = pl.BlockSpec((near, LANES), lambda p, s: (0, p))
    return pl.pallas_call(
        attend_kernel,
        out_shape=(
            jax.ShapeDtypeStruct((near, width), LOW),
            jax.ShapeDtypeStruct((pairs, 8, near), FULL),
        ),
        grid_spec=pltpu.PrefetchScalarGridSpec(
            num_scalar_prefetch=1,
            grid=(pairs,),
            in_specs=[
                rows,
                pl.BlockSpec((total, LANES), lambda p, s: (0, p)),
                pl.BlockSpec((total, LANES), lambda p, s: (0, p + pairs)),
            ],
            out_specs=(rows, pl.BlockSpec((1, 8, near), lambda p, s: (p, 0, 0))),
            scratch_shapes=[
                pltpu.VMEM((8, near), FULL),
                pltpu.VMEM((2, HEAD + 16, near), FULL),
            ],
        ),
        compiler_params=pltpu.CompilerParams(vmem_limit_bytes=VMEM),
        cost_estimate=SHORT,
        name="attend",
    )(far, query, keyval, keyval)


def attend_back_kernel(
    far_ref, q_ref, k_ref, v_ref, grad_ref, out_ref, lse_ref, *refs
):
    dq_ref, dk_ref, dv_ref, acc_ref = refs[-4:]
    near = q_ref.shape[0]
    size = near // 2
    spans = (slice(0, size), slice(size, near))
    query = q_ref[...] * jnp.asarray(SCALE, LOW)
    grad = grad_ref[...]
    product = jnp.transpose(grad.astype(FULL) * out_ref[...].astype(FULL))
    delta = [
        jnp.sum(product[head * HEAD : (head + 1) * HEAD], 0, keepdims=True) for head in range(2)
    ]

    def block(at, work):
        key, value = k_ref[at, :], v_ref[at, :]
        turned = jnp.transpose(key)
        dk = dv = None
        for which, masked, first in work:
            span = spans[which]
            for head in range(2):
                part = slice(head * HEAD, (head + 1) * HEAD)
                q_head = head_lanes(query[span], head)
                g_head = head_lanes(grad[span], head)
                probs = jnp.exp(dot_nt(key, q_head) - lse_ref[0, head : head + 1, span])
                if masked:
                    probs = jnp.where(causal(size, size), probs, 0.0)
                moved = probs * (dot_nt(value, g_head) - delta[head][:, span])
                moved, probs = moved.astype(LOW), probs.astype(LOW)
                new_k, new_v = dot(moved, q_head), dot(probs, g_head)
                dk = new_k if dk is None else dk + new_k
                dv = new_v if dv is None else dv + new_v
                new_q = dot(turned[part], moved)
                if first:
                    acc_ref[which, part, :] = new_q
                else:
                    acc_ref[which, part, :] += new_q
        dk_ref[at, :] = dk.astype(LOW)
        dv_ref[at, :] = dv.astype(LOW)

    block(spans[0], [(0, True, True), (1, False, True)])
    block(spans[1], [(1, True, False)])

    @pl.loop(0, far_ref[0])
    def _(i):
        at = pl.ds(pl.multiple_of(near + i * size, size), size)
        block(at, [(0, False, False), (1, False, False)])

    @pl.loop(far_ref[0], 2)
    def _(i):
        at = pl.ds(pl.multiple_of(near + i * size, size), size)
        dk_ref[at, :] = jnp.zeros((size, LANES), LOW)
        dv_ref[at, :] = jnp.zeros((size, LANES), LOW)

    for which in range(2):
        dq_ref[spans[which], :] = (jnp.transpose(acc_ref[which]) * SCALE).astype(LOW)


def attend_back(far, query, keyval, grad, out, lse, which, earlier):
    near, width = query.shape
    total = keyval.shape[0]
    pairs = width // LANES
    rows = pl.BlockSpec((near, LANES), lambda p, s: (0, which))
    every = pl.BlockSpec((total, LANES), lambda p, s: (0, which))
    return pl.pallas_call(
        attend_back_kernel,
        out_shape=(
            jax.ShapeDtypeStruct((near, width), LOW),
            jax.ShapeDtypeStruct((total, width), LOW),
            jax.ShapeDtypeStruct((total, width), LOW),
        ),
        grid_spec=pltpu.PrefetchScalarGridSpec(
            num_scalar_prefetch=1,
            grid=(1,),
            in_specs=[
                rows,
                every,
                pl.BlockSpec((total, LANES), lambda p, s: (0, which + pairs)),
                rows,
                rows,
                pl.BlockSpec((1, 8, near), lambda p, s: (which, 0, 0)),
            ]
            + [pl.BlockSpec(memory_space=pl.ANY)] * len(earlier),
            out_specs=(rows, every, every),
            scratch_shapes=[pltpu.VMEM((2, LANES, near // 2), FULL)],
        ),
        input_output_aliases={7 + i: i for i in range(len(earlier))},
        compiler_params=pltpu.CompilerParams(vmem_limit_bytes=VMEM),
        cost_estimate=SHORT,
        name="attend_back",
    )(far, query, keyval, keyval, grad, out, lse, *earlier)


def grads_kernel(n_ref, dq_ref, dk_ref, dv_ref, mine_ref, other_ref, a_ref, b_ref):
    near, width = dq_ref.shape
    turned = jnp.transpose(n_ref[...])
    low = jnp.concatenate(
        [
            dot(turned[:, :near], dq_ref[...]).astype(LOW),
            dot(turned, dk_ref[...]).astype(LOW),
            dot(turned, dv_ref[...]).astype(LOW),
            (mine_ref[...].astype(FULL) + other_ref[...].astype(FULL)).astype(LOW),
        ],
        1,
    )
    cut = a_ref.shape[1]
    a_ref[...] = low[:, :cut]
    b_ref[...] = low[:, cut:]


def qkv_grads(normed, dq, dk, dv, mine, other):
    width = normed.shape[1]
    cut = 2 * dq.shape[1]
    return pl.pallas_call(
        grads_kernel,
        out_shape=(
            jax.ShapeDtypeStruct((width, cut), LOW),
            jax.ShapeDtypeStruct((width, cut), LOW),
        ),
        compiler_params=pltpu.CompilerParams(vmem_limit_bytes=VMEM),
        cost_estimate=SHORT,
        name="qkv_grads",
    )(normed, dq, dk, dv, mine, other)


CURVE = 0.7978845608028654
CUBIC = 0.044715


def feed_kernel(
    shard_rows, core_ref, n_ref, g_ref, fc_ref, fb_ref, *refs
):
    pieces, refs = refs[:-8], refs[-8:]
    out_ref, back_ref, fc_send_ref, fc_keep_ref, pr_send_ref, pr_keep_ref = refs[:6]
    fb_grad_ref, turned_ref = refs[6:]

    step = pl.program_id(0)
    half = g_ref.shape[1] // 2

    @pl.when(step == 0)
    def _():
        turned_ref[...] = jnp.transpose(n_ref[...])

    if len(pieces) == 1:
        proj = pieces[0][...]
    else:
        size = shard_rows
        wide = [piece[...].astype(FULL) for piece in pieces]
        proj = jnp.concatenate(
            [
                piece[at : at + size]
                for at in range(0, wide[0].shape[0], size)
                for piece in wide
            ],
            0,
        ).astype(LOW)
    grad = g_ref[...]
    hidden = dot(n_ref[...], fc_ref[...]) + fb_ref[...]
    square = hidden * hidden
    bend = jnp.tanh(hidden * (CURVE + (CURVE * CUBIC) * square))
    gate = 0.5 * (1.0 + bend)
    active = (hidden * gate).astype(LOW)
    slope = gate + hidden * (0.5 * (1.0 - bend * bend)) * (
        CURVE + (3 * CURVE * CUBIC) * square
    )
    grad_hidden = (dot_nt(grad, proj) * slope).astype(LOW)
    out, back = dot(active, proj), dot_nt(grad_hidden, fc_ref[...])

    @pl.when(step == 0)
    def _():
        out_ref[...] = out
        back_ref[...] = back

    @pl.when(step > 0)
    def _():
        out_ref[...] += out
        back_ref[...] += back

    fb_grad_ref[...] = jnp.sum(grad_hidden.astype(FULL), 0, keepdims=True)
    fc_grad = dot(turned_ref[...], grad_hidden).astype(LOW)
    others = pl.num_programs(0) // 2

    @pl.when(step < others)
    def _():
        fc_send_ref[...] = fc_grad

    @pl.when(step >= others)
    def _():
        fc_keep_ref[...] = fc_grad

    pr_grad = dot_tn(active, grad)
    low, high = pr_grad[:, :half].astype(LOW), pr_grad[:, half:].astype(LOW)
    first = core_ref[0] == 0
    pr_send_ref[...] = jnp.where(first, high, low)
    pr_keep_ref[...] = jnp.where(first, low, high)


def beside_kernel(fc_ref, proj_ref, last_ref, out_ref):
    rows, at = fc_ref.shape
    width = proj_ref.shape[1]
    out_ref[:, :at] = fc_ref[...]
    out_ref[:, 2 * at :] = last_ref[...]
    wide = proj_ref[...].astype(FULL)
    for i in range(wide.shape[0] // rows):
        out_ref[:, at + i * width : at + (i + 1) * width] = wide[i * rows : (i + 1) * rows].astype(
            LOW
        )


def beside_rows(fc, proj, last):
    rows = fc.shape[0]
    if rows % 8:
        return jnp.concatenate(
            [fc] + [proj[i : i + rows] for i in range(0, proj.shape[0], rows)] + [last], 1
        )
    vmem = pl.BlockSpec(memory_space=pltpu.VMEM)
    return pl.pallas_call(
        beside_kernel,
        in_specs=[vmem, vmem, vmem],
        out_shape=jax.ShapeDtypeStruct((rows, 2 * fc.shape[1] + last.shape[1]), LOW),
        cost_estimate=SHORT,
        name="beside",
    )(fc, proj, last)


def feed(core, normed, grad, late, fc_bias, proj, shard_rows):
    rows, width = normed.shape
    hidden = fc_bias.shape[1]
    chunk = 2 * width
    blocks = hidden // width
    steps = hidden // (2 * chunk)

    def block(i, s):
        return jnp.where(i < steps, (1 - s[0]) * steps + i, s[0] * steps + i - steps)

    whole = pl.BlockSpec((rows, width), lambda i, s: (0, 0))
    if proj is None:
        pieces = [late] * blocks
        piece_specs = [
            pl.BlockSpec((chunk * width // hidden, width), lambda i, s, at=at: (block(i, s), at))
            for at in range(blocks, 2 * blocks)
        ]
    else:
        pieces = [proj]
        piece_specs = [pl.BlockSpec((chunk, width), lambda i, s: (block(i, s), 0))]
    half = pl.BlockSpec((chunk, width // 2), lambda i, s: (block(i, s), 0))
    return pl.pallas_call(
        functools.partial(feed_kernel, shard_rows),
        out_shape=(
            jax.ShapeDtypeStruct((rows, width), FULL),
            jax.ShapeDtypeStruct((rows, width), FULL),
            jax.ShapeDtypeStruct((width, hidden // 2), LOW),
            jax.ShapeDtypeStruct((width, hidden // 2), LOW),
            jax.ShapeDtypeStruct((hidden, width // 2), LOW),
            jax.ShapeDtypeStruct((hidden, width // 2), LOW),
            jax.ShapeDtypeStruct((1, hidden), FULL),
        ),
        grid_spec=pltpu.PrefetchScalarGridSpec(
            num_scalar_prefetch=1,
            grid=(2 * steps,),
            in_specs=[
                whole,
                whole,
                pl.BlockSpec((width, chunk), lambda i, s: (0, block(i, s))),
                pl.BlockSpec((1, chunk), lambda i, s: (0, block(i, s))),
                *piece_specs,
            ],
            out_specs=(
                whole,
                whole,
                pl.BlockSpec((width, chunk), lambda i, s: (0, jnp.minimum(i, steps - 1))),
                pl.BlockSpec((width, chunk), lambda i, s: (0, jnp.maximum(i - steps, 0))),
                half,
                half,
                pl.BlockSpec((1, chunk), lambda i, s: (0, block(i, s))),
            ),
            scratch_shapes=[pltpu.VMEM((width, rows), LOW)],
        ),
        compiler_params=pltpu.CompilerParams(vmem_limit_bytes=VMEM),
        cost_estimate=SHORT,
        name="feed",
    )(core, normed, grad, late, fc_bias, *pieces)


def turn_kernel(
    core_ref, n_ref, hat_ref, root_ref, gain_ref, g_ref, att_ref, w_ref,
    middle_ref, keep_ref, send_ref, w_keep_ref, w_send_ref, gain_grad_ref, shift_ref, bias_ref, last_ref,
):
    half = keep_ref.shape[1]
    grad, hat = n_ref[...], hat_ref[...]
    gain_grad_ref[...] = jnp.sum(grad * hat, 0, keepdims=True)
    shift_ref[...] = jnp.sum(grad, 0, keepdims=True)
    middle = g_ref[...].astype(FULL) + normalize_back(grad, gain_ref[...], hat, root_ref[...])
    middle_ref[...] = middle
    last_ref[...] = jnp.sum(g_ref[...].astype(FULL), 0, keepdims=True)
    low = middle.astype(LOW)
    bias_ref[...] = jnp.sum(low.astype(FULL), 0, keepdims=True)
    first = core_ref[0] == 0
    for whole, kept, sent in (
        (dot_nt(low, w_ref[...]), keep_ref, send_ref),
        (dot(jnp.transpose(att_ref[...]), low), w_keep_ref, w_send_ref),
    ):
        whole = whole.astype(LOW)
        one, two = whole[:, :half], whole[:, half:]
        kept[...] = jnp.where(first, one, two)
        sent[...] = jnp.where(first, two, one)


def turn(core, grad, hat, root, gain, grad_valid, attended, late, at):
    rows, width = grad.shape
    shape = jax.ShapeDtypeStruct

    def spec(*dims):
        return pl.BlockSpec(dims, lambda i, s: (0, 0))

    whole = spec(rows, width)
    return pl.pallas_call(
        turn_kernel,
        grid_spec=pltpu.PrefetchScalarGridSpec(
            num_scalar_prefetch=1,
            grid=(1,),
            in_specs=[
                whole,
                whole,
                spec(rows, 1),
                spec(1, width),
                whole,
                whole,
                pl.BlockSpec((width, width), lambda i, s: (0, at)),
            ],
            out_specs=(
                whole,
                spec(rows, width // 2),
                spec(rows, width // 2),
                spec(width, width // 2),
                spec(width, width // 2),
                spec(1, width),
                spec(1, width),
                spec(1, width),
                spec(1, width),
            ),
        ),
        out_shape=(
            shape((rows, width), FULL),
            shape((rows, width // 2), LOW),
            shape((rows, width // 2), LOW),
            shape((width, width // 2), LOW),
            shape((width, width // 2), LOW),
            shape((1, width), FULL),
            shape((1, width), FULL),
            shape((1, width), FULL),
            shape((1, width), FULL),
        ),
        compiler_params=pltpu.CompilerParams(vmem_limit_bytes=56 << 20),
        cost_estimate=SHORT,
        name="turn",
    )(core, grad, hat, root, gain, grad_valid, attended, late)


def norm_back_kernel(
    core_ref, dq_ref, dk_ref, dv_ref, wq_ref, wkv_ref, hat_ref,
    keep_ref, send_ref, gain_ref, shift_ref, q_sum_ref, v_sum_ref, part_ref,
):
    step = pl.program_id(0)
    half = dk_ref.shape[1]
    part_ref[...] = dot_nt(dk_ref[...], wkv_ref[:, :half]) + dot_nt(
        dv_ref[...], wkv_ref[:, half:]
    )

    @pl.when(step == 0)
    def _():
        for ref in (gain_ref, shift_ref, q_sum_ref, v_sum_ref):
            ref[...] = jnp.zeros_like(ref)

    @pl.when(lax.rem(step, 2) == 1)
    def _():
        part_ref[...] += dot_nt(dq_ref[...], wq_ref[...])
        q_sum_ref[...] += jnp.sum(dq_ref[...].astype(FULL), 0, keepdims=True)

    part = part_ref[...]
    v_sum_ref[...] += jnp.sum(dv_ref[...].astype(FULL), 0, keepdims=True)
    gain_ref[...] += jnp.sum(part * hat_ref[...], 0, keepdims=True)
    shift_ref[...] += jnp.sum(part, 0, keepdims=True)

    @pl.when(step < 2)
    def _():
        send_ref[0] = part.astype(LOW)

    @pl.when(step >= 2)
    def _():
        keep_ref[0] = part


def norm_back(core, dq, dk, dv, q_weight, keyval_weight, hat):
    quarter, half, width = dq.shape[0] // 2, dq.shape[1], hat.shape[1]

    def at(i, s):
        return jnp.where(i < 2, 1 - s[0], s[0])

    def block(i, s):
        return (jnp.where(lax.rem(i, 2) == 0, 2, 0) + at(i, s), 0)

    whole = lambda i, s: (0, 0)
    line, short = pl.BlockSpec((1, width), whole), pl.BlockSpec((1, half), whole)
    shape = jax.ShapeDtypeStruct
    return pl.pallas_call(
        norm_back_kernel,
        out_shape=(
            shape((2, quarter, width), FULL),
            shape((2, quarter, width), LOW),
            shape((1, width), FULL),
            shape((1, width), FULL),
            shape((1, half), FULL),
            shape((1, half), FULL),
        ),
        grid_spec=pltpu.PrefetchScalarGridSpec(
            num_scalar_prefetch=1,
            grid=(4,),
            in_specs=[
                pl.BlockSpec((quarter, half), lambda i, s: (at(i, s), 0)),
                pl.BlockSpec((quarter, half), block),
                pl.BlockSpec((quarter, half), block),
                pl.BlockSpec((width, half), whole),
                pl.BlockSpec((width, 2 * half), whole),
                pl.BlockSpec((quarter, width), block),
            ],
            out_specs=(
                pl.BlockSpec((1, quarter, width), lambda i, s: (jnp.maximum(i - 2, 0), 0, 0)),
                pl.BlockSpec((1, quarter, width), lambda i, s: (jnp.minimum(i, 1), 0, 0)),
                line,
                line,
                short,
                short,
            ),
            scratch_shapes=[pltpu.VMEM((quarter, width), FULL)],
        ),
        compiler_params=pltpu.CompilerParams(vmem_limit_bytes=VMEM),
        cost_estimate=SHORT,
        name="norm_back",
    )(core, dq, dk, dv, q_weight, keyval_weight, hat)


def pack_kernel(slots, core_ref, *refs):
    out_ref = refs[-1]
    count = out_ref.shape[0]
    spreads = {}
    for slot, parts in enumerate(slots):
        total = None
        for ref_at, size, shift, by_core in parts:
            line = refs[ref_at][...]
            length = line.shape[1]
            shape = (count, length)
            device = lax.broadcasted_iota(jnp.int32, shape, 0) - (shift + by_core * core_ref[0])
            lane = lax.broadcasted_iota(jnp.int32, shape, 1) - device * size
            piece = jnp.where((lane >= 0) & (lane < size), line, 0.0)
            if (length, size) not in spreads:
                shape = (length, LANES)
                at = lax.broadcasted_iota(jnp.int32, shape, 0).astype(FULL)
                at = at - size * jnp.floor((at + 0.5) * (1.0 / size))
                lane = lax.broadcasted_iota(jnp.int32, shape, 1).astype(FULL)
                spreads[length, size] = jnp.where(at == lane, 1.0, 0.0)
            piece = lax.dot_general(
                piece,
                spreads[length, size],
                (((1,), (0,)), ((), ())),
                precision=lax.Precision.HIGHEST,
                preferred_element_type=FULL,
            )
            total = piece if total is None else total + piece
        out_ref[:, slot * LANES : (slot + 1) * LANES] = total


def pack(core, count, q_sum, v_sum, lines):
    size = 4 * q_sum.shape[1] // count
    slots = [[(0, size, 0, count // 4), (1, size, count // 2, count // 4)]]
    slots += [[(2 + i, line.shape[1] // count, 0, 0)] for i, line in enumerate(lines)]
    lines = (q_sum, v_sum, *lines)
    whole = lambda i, s: (0, 0)
    packed = pl.pallas_call(
        functools.partial(pack_kernel, slots),
        out_shape=jax.ShapeDtypeStruct((count, len(slots) * LANES), FULL),
        grid_spec=pltpu.PrefetchScalarGridSpec(
            num_scalar_prefetch=1,
            grid=(1,),
            in_specs=[pl.BlockSpec(line.shape, whole) for line in lines],
            out_specs=pl.BlockSpec((count, len(slots) * LANES), whole),
        ),
        compiler_params=pltpu.CompilerParams(vmem_limit_bytes=VMEM),
        cost_estimate=SHORT,
        name="pack",
    )(core, *lines)
    return packed, [slot[0][1] for slot in slots]


def normalize(values):
    center = values - jnp.mean(values, -1, keepdims=True)
    spread = jnp.mean(center * center, -1, keepdims=True)
    root = lax.rsqrt(spread + 1e-05)
    return center * root, root


def normalize_back(grad, gain, hat, root):
    scaled = grad * gain
    return root * (
        scaled
        - jnp.mean(scaled, -1, keepdims=True)
        - hat * jnp.mean(scaled * hat, -1, keepdims=True)
    )


def shards(
    tokens,
    lengths,
    thought_pos,
    cotangent,
    qkv_weight,
    out_weight,
    fc_weight,
    proj_weight,
    qv_bias,
    out_bias,
    fc_bias,
    proj_bias,
    first_gain,
    first_shift,
    second_gain,
    second_shift,
):
    _, quarter, width = tokens.shape
    half = width // 2
    near = 2 * quarter
    slice_rows = qkv_weight.shape[0]
    count = 1 << flat_bits()
    plans = orders()
    core, second = bit_of(0), bit_of(1)
    far = (2 * second).astype(jnp.int32).reshape(1)

    high, hidden_width = proj_weight.shape[0], fc_weight.shape[1]
    blocks = hidden_width // width
    late = lax.all_gather(
        beside_rows(fc_weight, proj_weight, out_weight), ALL, axis=0, tiled=True
    )

    mine = tokens[0]
    flips = [(i, i ^ 2) for i in range(count) if not i & 2]
    before = lax.ppermute(mine, ALL, flips)
    near_tokens = pair(mine, swap(mine, 0), core, 0).reshape(near, width)

    third = slice_rows * 4
    small = jnp.zeros((slice_rows, LANES), LOW)
    rows_of = (
        jnp.concatenate([qv_bias, out_bias, first_gain]),
        fc_bias,
        jnp.concatenate([proj_bias, first_shift, second_gain, second_shift]),
    )
    small = small.at[:3, :third].set(jnp.stack(rows_of))
    split = qkv_weight.reshape(slice_rows, 3, 2, half)
    keep = lax.dynamic_index_in_dim(split, core, 2, keepdims=False).reshape(slice_rows, 3 * half)
    send = lax.dynamic_index_in_dim(split, 1 - core, 2, keepdims=False).reshape(
        slice_rows, 3 * half
    )
    keep, send = jnp.concatenate([keep, small], 1), jnp.concatenate([send, small], 1)
    chip = pair(keep, swap(send, 0), core, 0).reshape(2 * slice_rows, 3 * half + LANES)
    block = gather_common(chip, (before,))
    far_tokens = pair(before, swap(before, 0), core, 0).reshape(near, width)
    slots = jnp.arange(near, dtype=jnp.int32)
    thoughts = thought_pos[0]

    def is_thought(at_slots):
        return jnp.any(thoughts[None, :] == at_slots[:, None], 1, keepdims=True)

    thought_near = is_thought(second * near + slots)
    thought_far = is_thought(slots)
    shifted_near = jnp.concatenate([far_tokens[-1:], near_tokens[:-1]], 0)
    shifted_far = jnp.concatenate([far_tokens[:1], far_tokens[:-1]], 0)
    inputs_near = jnp.where(thought_near, shifted_near, near_tokens)
    inputs_far = jnp.where(thought_far, shifted_far, far_tokens)
    inputs_all = jnp.concatenate([inputs_near, inputs_far], 0)
    hat_all, root_all = normalize(inputs_all.astype(FULL))
    own = core * quarter
    inputs = lax.dynamic_slice_in_dim(inputs_near, own, quarter, 0).astype(FULL)

    parts = [
        jnp.concatenate([block[:, :, :half], block[:, :, 3 * half :]], 2),
        block[:, :, half : 3 * half],
    ]
    first_parts = gather_step(parts, plans, 0)

    parts = gather_step(first_parts, plans, 1, (hat_all, root_all))
    q_weight = parts[0][:, :, :half].reshape(width, half)
    keyval_weight = parts[1].reshape(width, 2 * half)
    small = parts[0].reshape(count, slice_rows, half + LANES)[:, :3, half : half + third]
    small = small.astype(FULL)
    at = slice_rows

    def vector(row, first, size):
        return small[:, row, first : first + size].reshape(1, count * size)

    qv_full = vector(0, 0, 2 * at)
    out_bias_full, gain_one = vector(0, 2 * at, at), vector(0, 3 * at, at)
    fc_bias_full = vector(1, 0, 4 * at)
    proj_bias_full, shift_one = vector(2, 0, at), vector(2, at, at)
    gain_two, shift_two = vector(2, 2 * at, at), vector(2, 3 * at, at)

    normed = (hat_all * gain_one + shift_one).astype(LOW)
    own_half = core * half
    q_bias = lax.dynamic_slice_in_dim(qv_full[:, :width], own_half, half, 1)
    v_bias = lax.dynamic_slice_in_dim(qv_full[:, width:], own_half, half, 1)
    query = (dot(normed[:near], q_weight) + q_bias).astype(LOW)
    keyval_bias = jnp.concatenate([jnp.zeros((1, half), FULL), v_bias], 1)
    keyval = (dot(normed, keyval_weight) + keyval_bias).astype(LOW)

    def rows_to_core(array):
        return (
            lax.dynamic_slice_in_dim(array, own, quarter, 0),
            lax.dynamic_slice_in_dim(array, quarter - own, quarter, 0),
        )

    pairs = half // LANES
    heads, logsums = attend(far, query, keyval)
    keep, send = rows_to_core(heads)
    attended = beside(keep, swap(send, 0), core)
    late = after(late, attended)
    out_full = late[:, 2 * hidden_width :]
    middle = inputs + dot(attended, out_full) + out_bias_full
    hat_two, root_two = normalize(middle)
    normed_two = (hat_two * gain_two + shift_two).astype(LOW)
    my_slots = (2 * second + core) * quarter + jnp.arange(quarter, dtype=jnp.int32)
    valid = (my_slots < lengths[0])[:, None]
    grad_valid = jnp.where(valid, cotangent[0], jnp.zeros_like(cotangent[0]))
    core_at = core.astype(jnp.int32).reshape(1)
    proj_full = None
    if slice_rows % 8:
        proj_full = late[:, hidden_width : 2 * hidden_width].reshape(count, slice_rows, blocks, width)
        proj_full = proj_full.transpose(0, 2, 1, 3).reshape(hidden_width, width)
    fed, grad_normed_two, fc_send, fc_keep, proj_send, proj_keep, fc_bias_grad = feed(
        core_at, normed_two, grad_valid, late, fc_bias_full, proj_full, slice_rows
    )
    output = middle + fed + proj_bias_full
    mixed = jnp.where(valid, output, 0.0).astype(LOW)[None]

    chips = count // 2
    fc_shape = (chips, 2 * slice_rows, hidden_width // 2)
    proj_shape = (chips, 2 * high, half)
    fc_got, proj_got = swap(fc_send, 0), swap(proj_send, 0)

    turned = turn(
        core_at, grad_normed_two, hat_two, root_two, gain_two, grad_valid, attended, late, 2 * blocks
    )
    grad_middle, keep, send, out_kept, out_send = turned[:5]
    second_gain_grad, second_shift_grad, out_bias_grad, proj_bias_grad = turned[5:]
    grad_heads = pair(keep, swap(send, 0), core, 0).reshape(near, half)
    fc_got, proj_got = after((fc_got, proj_got), grad_middle)
    fc_pair = [fc_keep.reshape(fc_shape), fc_got.reshape(fc_shape)]
    proj_pair = [proj_keep.reshape(proj_shape), proj_got.reshape(proj_shape)]
    early = [start_sum(fc_pair), start_sum(proj_pair)]
    ready = prepare(early, plans, 0)
    out_got = swap(after(out_send, *sends(ready)), 0)

    grads = ()
    now = after(grad_heads, *sends(ready))
    for which in range(pairs):
        if which == 2:
            ready = prepare(exchange(ready, grads), plans, 1)
            now = after(grad_heads, *sends(ready))
        grads = attend_back(
            far, query, keyval, now, heads, logsums, which, grads
        )
    out_got = after(out_got, *grads)
    ready = prepare(exchange(ready, grads), plans, 2)
    grad_query, grad_key, grad_value = after(grads, *sends(ready))

    last = [
        start_sum([value.reshape(chips, 2 * slice_rows, -1)])
        for value in qkv_grads(normed, grad_query, grad_key, grad_value, out_kept, out_got)
    ]
    last_ready = prepare(last, plans, 0)

    part, part_send, first_gain_grad, first_shift_grad, q_sum, v_sum = norm_back(
        core_at,
        after(grad_query, *sends(last_ready)),
        grad_key,
        grad_value,
        q_weight,
        keyval_weight,
        hat_all,
    )
    got = swap(part_send, 0)
    both = exchange(last_ready + ready, (part_send,))
    last_ready = prepare(both[:2], plans, 1)
    ready = prepare(both[2:], plans, 3)
    got = after(got, *sends(last_ready), *sends(ready))
    far_sum = (part[0] + got[0].astype(FULL)).astype(LOW)
    back = lax.ppermute(far_sum, ALL, [(b, a) for a, b in flips])
    packed, sizes = pack(
        core_at,
        count,
        q_sum,
        v_sum,
        (
            out_bias_grad,
            fc_bias_grad,
            proj_bias_grad,
            first_gain_grad,
            first_shift_grad,
            second_gain_grad,
            second_shift_grad,
        ),
    )
    for step in range(2, flat_bits() - 1):
        last = exchange(last_ready, (far_sum,))
        last_ready = prepare(last, plans, step)
    packed = after(packed, *sends(last_ready))
    share = jnp.sum(lax.all_to_all(packed, ALL, 0, 0, tiled=True), 0, keepdims=True)
    last = exchange(last_ready, (back,))
    for step in range(4, flat_bits() - 1):
        ready = prepare(exchange(ready), plans, step)
    early = exchange(ready, (far_sum,))
    fc_weight_grad, proj_weight_grad, qkv_weight_grad, out_weight_grad = finish(
        early + last,
        slice_rows,
        (
            (slice_rows, hidden_width),
            (high, width),
            (slice_rows, 3 * width),
            (slice_rows, width),
        ),
    )

    grad_normed = part[1] + got[1].astype(FULL) + back.astype(FULL)
    hat = lax.dynamic_slice_in_dim(hat_all, own, quarter, 0)
    root = lax.dynamic_slice_in_dim(root_all, own, quarter, 0)
    grad_inputs = grad_middle + normalize_back(grad_normed, gain_one, hat, root)
    thought = lax.dynamic_slice_in_dim(thought_near, own, quarter, 0)
    kept = jnp.where(thought, 0.0, grad_inputs)
    moved = jnp.where(thought, grad_inputs, 0.0)
    ctx = lax.axis_size("ctx")
    following = lax.ppermute(moved[:1], "ctx", [(i, i - 1) for i in range(1, ctx)])
    tokens_grad = (kept + jnp.concatenate([moved[1:], following], 0))[None]

    shares = [share[0, i * LANES : i * LANES + size] for i, size in enumerate(sizes)]
    return (
        mixed,
        tokens_grad,
        qkv_weight_grad,
        out_weight_grad,
        fc_weight_grad,
        proj_weight_grad,
        *shares,
    )


def solution(mesh):
    rows, matrix, vector = P("dp", "ctx", None), P(ALL, None), P(ALL)
    return jax.shard_map(
        shards,
        mesh=mesh,
        in_specs=(rows, P("dp"), P("dp", None), rows) + (matrix,) * 4 + (vector,) * 8,
        out_specs=(rows, rows) + (matrix,) * 4 + (vector,) * 8,
        check_vma=False,
    )
```
